512 devices in a mesh: gx: 8 (over z), gy: 8 (over y), gz: 8 (over x, core).
Axes of the slice: x: 4, y: 8, z: 8, core: 2. Of those that a mesh axis runs over, the one named last changes fastest.
Arguments:
- levels: int32 [64, 64, 1024], P('gx', 'gy', 'gz'), may hold values from 1 to 255
- residual: float32 [3, 64, 64, 1024], P(None, 'gx', 'gy', 'gz'), may hold values from -4 to 4
Outputs:
- correction: float32 [3, 64, 64, 1024], P(None, 'gx', 'gy', 'gz')
- coarse: float32 [3, 32, 32, 512], P(None, 'gx', 'gy', 'gz')
The draws below stay inside these ranges and needn't reach their ends.
All inputs are finite; a program needn't handle non-finite values.
Results may differ from the reference program's by a relative error of at most 0.00002.
Values sent between devices are 32-bit elements; how exact they have to be, the bound alone decides.
No kernel may reach another device: no remote copies, remote signals or barrier semaphores. Data moves between devices by JAX's collectives and lax.ppermute only.
A program may use at most 128 MiB of HBM per device.

```python
import jax
import jax.numpy as jnp

SWEEPS = 4
NX = 64
NY = 64
NZ = 1024


def draw_residual(key, part):
    key = jax.random.fold_in(key, 7)
    shape = (3, NX, NY, NZ)
    return jnp.clip(jax.random.normal(key, shape, jnp.float32), -4.0, 4.0)


def place_ends(entries, rng, least, top_value):
    spot = [jax.random.randint(jax.random.fold_in(rng, axis), (), 0, length) for axis, length in enumerate(entries.shape)]
    widest = entries.shape.index(max(entries.shape))
    neighbour = spot[:widest] + [(spot[widest] + 1) % entries.shape[widest]] + spot[widest + 1:]
    return entries.at[tuple(spot)].set(least).at[tuple(neighbour)].set(top_value)


def setup_inputs(seed: int = 0) -> dict:
    key_of = jax.random.split(jax.random.key(seed), 3)
    levels = place_ends(jax.random.randint(key_of[0], (NX, NY, NZ), 1, 256), jax.random.fold_in(key_of[0], 1), 1, 255).astype(jnp.int32)
    residual = draw_residual(jax.random.fold_in(key_of[2], 71), 0)
    return dict(levels=levels, residual=residual)


THETA = 1.15
DELTA = 0.85


def offset_table():
    table = []
    coefs = {1: (0.10, 0.06), 2: (0.03, 0.03), 3: (0.01, 0.02)}
    for dx in (-1, 0, 1):
        for dy in (-1, 0, 1):
            for dz in (-1, 0, 1):
                sqr = dx * dx + dy * dy + dz * dz
                if sqr == 0:
                    continue
                first, second = coefs[sqr]
                unit = (dx, dy, dz)
                block = [[(first if c == e else 0.0) + second * unit[c] * unit[e] / sqr for e in range(3)] for c in range(3)]
                table.append((dx, dy, dz, first + second, block))
    return table


def stiffness(levels):
    ratio = levels.astype(jnp.float32) / 255.0
    return 0.05 + 0.95 * ratio * ratio * ratio


def couple(mod_pad):
    nx, ny, nz = mod_pad.shape[0] - 2, mod_pad.shape[1] - 2, mod_pad.shape[2] - 2
    centre = mod_pad[1:1 + nx, 1:1 + ny, 1:1 + nz]
    weights = []
    total = jnp.zeros_like(centre)
    for dx, dy, dz, summed, block in offset_table():
        nbr = mod_pad[1 + dx:1 + dx + nx, 1 + dy:1 + dy + ny, 1 + dz:1 + dz + nz]
        weight = 0.5 * (centre + nbr)
        weights.append(weight)
        total = total + summed * weight
    return weights, 1.05 * total


def apply(field_pad, weights, diag):
    nx, ny, nz = diag.shape
    centre = field_pad[:, 1:1 + nx, 1:1 + ny, 1:1 + nz]
    parts = [diag * centre[c] for c in range(3)]
    for index, entry in enumerate(offset_table()):
        dx, dy, dz, summed, block = entry
        nbr = field_pad[:, 1 + dx:1 + dx + nx, 1 + dy:1 + dy + ny, 1 + dz:1 + dz + nz]
        for c in range(3):
            mixed = None
            for e in range(3):
                if block[c][e] != 0.0:
                    term = block[c][e] * nbr[e]
                    mixed = term if mixed is None else mixed + term
            parts[c] = parts[c] - weights[index] * mixed
    return jnp.stack(parts)


def chebyshev(rest, diag, operate, final):
    sigma = THETA / DELTA
    rho = 1.0 / sigma
    step = rest / (THETA * diag)
    total = step
    for sweep in range(SWEEPS):
        if sweep > 0:
            total = total + step
        if sweep + 1 < SWEEPS or final:
            rest = rest - operate(step)
        if sweep + 1 < SWEEPS:
            rho_next = 1.0 / (2.0 * sigma - rho)
            step = (rho_next * rho) * step + (2.0 * rho_next / DELTA) * rest / diag
            rho = rho_next
    return total, rest


def children(field):
    comps, nx, ny, nz = field.shape
    return field.reshape(comps, nx // 2, 2, ny // 2, 2, nz // 2, 2).sum(axis=(2, 4, 6))


def prolong(field):
    return jnp.repeat(jnp.repeat(jnp.repeat(field, 2, axis=1), 2, axis=2), 2, axis=3)


def pad_field(field):
    return jnp.pad(field, ((0, 0), (1, 1), (1, 1), (1, 1)))


def reference(levels, residual):
    modulus = stiffness(levels)
    weights, diag = couple(jnp.pad(modulus, 1))

    def operate(field):
        return apply(pad_field(field), weights, diag)

    smooth, rest = chebyshev(residual, diag, operate, True)
    coarse_rest = children(rest)
    coarse_mod = children(modulus[None])[0] / 4.0
    coarse_w, coarse_d = couple(jnp.pad(coarse_mod, 1))

    def coarse_op(field):
        return apply(pad_field(field), coarse_w, coarse_d)

    coarse, unused = chebyshev(coarse_rest, coarse_d, coarse_op, False)
    lifted = prolong(coarse)
    after = rest - operate(lifted)
    post, unused = chebyshev(after, diag, operate, False)
    return (smooth + lifted) + post, coarse
```

```python
import functools

import jax
import jax.numpy as jnp
from jax import lax
from jax.experimental import pallas as pl
from jax.experimental.pallas import tpu as pltpu
from jax.sharding import PartitionSpec as P

SWEEPS = 4
THETA = 1.15
DELTA = 0.85

FACE, SIDE, EDGE, FLAT, TURN, TWIST = 9.6, 6.0, 2.7, 1.8, 0.9, 0.4
UNIT = 120.0
WHOLE = 1.92
HALO = 16


def sweep_scales():
    sigma = THETA / DELTA
    rho = 1.0 / sigma
    scales = []
    for _ in range(SWEEPS - 1):
        rho_next = 1.0 / (2.0 * sigma - rho)
        scales.append((rho_next * rho, 2.0 * rho_next / DELTA))
        rho = rho_next
    return scales


def lane_index():
    return lax.broadcasted_iota(jnp.int32, (8, 128), 1)


def join_lanes(centre, above, below):
    up = [pltpu.roll(a, 127, 1) for a in above]
    down = [pltpu.roll(b, 1, 1) for b in below]
    if len(centre) == 2:
        lane = lane_index()
        last, first = lane == 127, lane == 0
        up = [jnp.where(last, up[1], up[0]), jnp.where(last, up[0], up[1])]
        down = [jnp.where(first, down[1], down[0]), jnp.where(first, down[0], down[1])]
    return [c + (u + d) for c, u, d in zip(centre, up, down)]


def stencil(field, plane, row, tiles):
    centre, above, below = [[], [], []], [[], [], []], [[], [], []]
    for tile in range(tiles):
        flat, even, odd = [None] * 3, [None] * 3, [None] * 3
        turn = [None] * 2
        sums = []
        for c in range(3):
            def at(dx, dy):
                return field[c, plane + dx, tile, pl.ds(row + dy, 8), :]

            u = at(0, 0)
            xp, xm, yp, ym = at(1, 0), at(-1, 0), at(0, 1), at(0, -1)
            pp, pm, mp, mm = at(1, 1), at(1, -1), at(-1, 1), at(-1, -1)
            sx, sy = xp + xm, yp + ym
            a, b = pp + mm, pm + mp
            sxy = a + b
            if c < 2:
                dxy = a - b
                turn[c] = dxy
            e, f = pp - mm, pm - mp
            if c != 1:
                dx_sy = e + f
                dx = xp - xm
            if c != 0:
                dy_sx = e - f
                dy = yp - ym
            if c == 0:
                even[0] = SIDE * u + EDGE * sx + FLAT * sy + sxy
                flat[0] = FACE * sx + SIDE * sy + EDGE * sxy
                sums.append((dx, dx_sy))
            elif c == 1:
                even[1] = SIDE * u + EDGE * sy + FLAT * sx + sxy
                flat[1] = FACE * sy + SIDE * sx + EDGE * sxy
                sums.append((dy, dy_sx))
            else:
                both = sx + sy
                even[2] = FACE * u + EDGE * both + sxy
                flat[2] = SIDE * both + FLAT * sxy
                odd[0] = TURN * dx + TWIST * dx_sy
                odd[1] = TURN * dy + TWIST * dy_sx
        odd[2] = TURN * (sums[0][0] + sums[1][0]) + TWIST * (sums[0][1] + sums[1][1])
        even[0] = even[0] + TWIST * turn[1]
        flat[0] = flat[0] + TURN * turn[1]
        even[1] = even[1] + TWIST * turn[0]
        flat[1] = flat[1] + TURN * turn[0]
        for c in range(3):
            centre[c].append(flat[c])
            above[c].append(even[c] + odd[c])
            below[c].append(even[c] - odd[c])
    return [join_lanes(centre[c], above[c], below[c]) for c in range(3)]


def coupling(field, scaled, modulus, plane, row, tiles):
    plain = stencil(field, plane, row, tiles)
    heavy = stencil(scaled, plane, row, tiles)
    return [[modulus[t] * plain[c][t] + heavy[c][t] for t in range(tiles)] for c in range(3)]


def diagonal(modulus, plane, row, tiles):
    centre, even = [], []
    mids = []
    for tile in range(tiles):
        def at(dx, dy):
            return modulus[plane + dx, tile, pl.ds(row + dy, 8), :]

        u = at(0, 0)
        cross = (at(1, 0) + at(-1, 0)) + (at(0, 1) + at(0, -1))
        corner = (at(1, 1) + at(-1, -1)) + (at(1, -1) + at(-1, 1))
        even.append(0.16 * u + 0.06 * cross + 0.03 * corner)
        centre.append(WHOLE * u + 0.16 * cross + 0.06 * corner)
        mids.append(u)
    total = join_lanes(centre, even, even)
    out = []
    for tile in range(tiles):
        diag = (1.05 * 0.5 * UNIT) * total[tile]
        inside = mids[tile] > 0.0
        inverse = jnp.where(inside, 1.0 / jnp.where(inside, diag, 1.0), 0.0)
        out.append((mids[tile], diag, inverse))
    return out


def pair_matrix(shape, fine_axis):
    fine = lax.broadcasted_iota(jnp.int32, shape, fine_axis)
    coarse = lax.broadcasted_iota(jnp.int32, shape, 1 - fine_axis)
    return (lax.shift_right_logical(fine, 1) == coarse).astype(jnp.float32)


def prepare(levels, residual, main, first, last):
    lane = lane_index()
    for c in range(4):
        head = jnp.zeros((8, 128), jnp.float32)
        tail = jnp.zeros((8, 128), jnp.float32)
        for p in range(8):
            if c < 3:
                value = residual[c, p]
            else:
                ratio = levels[p].astype(jnp.float32) / 255.0
                value = (0.05 + 0.95 * ratio * ratio * ratio) / UNIT
            main[c, p] = value
            mine = (lane >= HALO * p) & (lane < HALO * (p + 1))
            head = jnp.where(mine, pltpu.roll(value, HALO * p, 1) if p else value, head)
            tail = jnp.where(mine, pltpu.roll(value, (HALO * p + HALO) % 128, 1) if p < 7 else value, tail)
        first[c, 0] = head
        last[c, 0] = tail


def smooth_kernel(down, own, up, smooth, message, state, u, v, rest, modulus, diag, inverse, pairs):
    lane = lane_index()
    low, high = lane < HALO, lane >= 128 - HALO

    for t, block in enumerate((down, own, up)):
        def place(b, carry, t=t, block=block):
            for c in range(4):
                left, right = block[b, c, 8], block[b, c, 9]
                for p in range(8):
                    side_r = pltpu.roll(right, 128 - HALO * p, 1) if p else right
                    side_l = pltpu.roll(left, 112 - HALO * p, 1) if p < 7 else left
                    side = jnp.where(low, side_r, jnp.where(high, side_l, 0.0))
                    if c < 3:
                        rest[c, 8 * b + p, 0, pl.ds(8 * t, 8), :] = block[b, c, p]
                        rest[c, 8 * b + p, 1, pl.ds(8 * t, 8), :] = side
                    else:
                        modulus[8 * b + p, 0, pl.ds(8 + 8 * t, 8), :] = block[b, c, p]
                        modulus[8 * b + p, 1, pl.ds(8 + 8 * t, 8), :] = side
            return carry

        lax.fori_loop(0, 3, place, 0)

    def begin(plane, carry):
        for t in range(3):
            parts = diagonal(modulus, plane, 8 + 8 * t, 2)
            for tile, (mid, d, inv) in enumerate(parts):
                diag[plane, tile, pl.ds(8 * t, 8), :] = d
                inverse[plane, tile, pl.ds(8 * t, 8), :] = inv
                for c in range(3):
                    step = rest[c, plane, tile, pl.ds(8 * t, 8), :] * (inv * (1.0 / THETA))
                    u[0, c, plane, tile, pl.ds(8 + 8 * t, 8), :] = step
                    v[0, c, plane, tile, pl.ds(8 + 8 * t, 8), :] = mid * step
        return carry

    lax.fori_loop(1, 23, begin, 0)

    def gather(slot, start):
        def body(p, carry):
            for c in range(3):
                step = u[slot, c, 8 + p, 0, pl.ds(16, 8), :]
                smooth[c, p] = step if start else smooth[c, p] + step
            return carry

        lax.fori_loop(0, 8, body, 0)

    gather(0, True)
    scales = sweep_scales()
    for k in range(1, SWEEPS + 1):
        now, later = (k - 1) % 2, k % 2
        rows = (0, 8, 16) if k < 3 else (4, 12)

        def sweep(plane, carry, k=k, now=now, later=later, rows=rows):
            for row in rows:
                mod = [modulus[plane, tile, pl.ds(8 + row, 8), :] for tile in range(2)]
                out = coupling(u.at[now], v.at[now], mod, plane, 8 + row, 2)
                for tile in range(2):
                    d = diag[plane, tile, pl.ds(row, 8), :]
                    if k < SWEEPS:
                        keep, push = scales[k - 1]
                        inv = inverse[plane, tile, pl.ds(row, 8), :] * push
                    for c in range(3):
                        old = u[now, c, plane, tile, pl.ds(8 + row, 8), :]
                        r = rest[c, plane, tile, pl.ds(row, 8), :] - d * old + out[c][tile]
                        rest[c, plane, tile, pl.ds(row, 8), :] = r
                        if k < SWEEPS:
                            step = keep * old + inv * r
                            u[later, c, plane, tile, pl.ds(8 + row, 8), :] = step
                            v[later, c, plane, tile, pl.ds(8 + row, 8), :] = mod[tile] * step
            return carry

        lax.fori_loop(1 + k if k < SWEEPS else 5, 23 - k if k < SWEEPS else 19, sweep, 0)
        if k < SWEEPS:
            gather(later, False)

    def restrict(p, carry):
        for tile in range(2):
            for c in range(4):
                total = None
                for dx in range(2):
                    for dy in range(2):
                        if c < 3:
                            part = rest[c, 4 + 2 * p + dx, tile, pl.ds(4 + dy, 8, stride=2), :]
                        else:
                            part = 0.25 * modulus[4 + 2 * p + dx, tile, pl.ds(12 + dy, 8, stride=2), :]
                        total = part if total is None else total + part
                pairs[tile, c, p] = total
        return carry

    lax.fori_loop(0, 8, restrict, 0)
    matrix = pair_matrix((256, 128), 0)
    coarse = jnp.dot(
        pairs[0].reshape(256, 128),
        matrix[:128],
        precision=lax.Precision.HIGHEST,
        preferred_element_type=jnp.float32,
    ) + jnp.dot(
        pairs[1].reshape(256, 128),
        matrix[128:],
        precision=lax.Precision.HIGHEST,
        preferred_element_type=jnp.float32,
    )
    message[...] = coarse.reshape(4, 8, 8, 128)

    def keep_state(p, carry):
        for tile in range(2):
            for c in range(3):
                state[c, p, tile] = rest[c, 4 + p, tile, pl.ds(4, 16), :]
            state[3, p, tile] = modulus[4 + p, tile, pl.ds(12, 16), :]
            state[4, p, tile] = diag[4 + p, tile, pl.ds(4, 16), :]
            state[5, p, tile] = inverse[4 + p, tile, pl.ds(4, 16), :]
        return carry

    lax.fori_loop(0, 16, keep_state, 0)


def post_kernel(down, own, up, state, smooth, correction, coarse, cu, cv, crest, cmod, cinv, cdiag, total, u, v, wide):
    scales = sweep_scales()

    def place(p, carry):
        for c in range(4):
            below, mid, above = down[c, p], own[c, p, pl.ds(2, 4), :], up[c, p]
            if c < 3:
                crest[c, p, 0, pl.ds(0, 8), :] = below
                crest[c, p, 0, pl.ds(8, 8), :] = above
                crest[c, p, 0, pl.ds(6, 4), :] = mid
            else:
                cmod[p, 0, pl.ds(8, 8), :] = below
                cmod[p, 0, pl.ds(16, 8), :] = above
                cmod[p, 0, pl.ds(14, 4), :] = mid
        return carry

    lax.fori_loop(0, 16, place, 0)

    def begin(plane, carry):
        for t in range(2):
            mid, d, inv = diagonal(cmod, plane, 8 + 8 * t, 1)[0]
            cdiag[plane, 0, pl.ds(8 * t, 8), :] = d
            cinv[plane, 0, pl.ds(8 * t, 8), :] = inv
            for c in range(3):
                step = crest[c, plane, 0, pl.ds(8 * t, 8), :] * (inv * (1.0 / THETA))
                cu[0, c, plane, 0, pl.ds(8 + 8 * t, 8), :] = step
                cv[0, c, plane, 0, pl.ds(8 + 8 * t, 8), :] = mid * step
        return carry

    lax.fori_loop(1, 15, begin, 0)

    def gather(slot, start):
        def body(p, carry):
            for c in range(3):
                step = cu[slot, c, 4 + p, 0, pl.ds(12, 8), :]
                total[c, p] = step if start else total[c, p] + step
            return carry

        lax.fori_loop(0, 8, body, 0)

    gather(0, True)
    for k in range(1, SWEEPS):
        now, later = (k - 1) % 2, k % 2

        def sweep(plane, carry, k=k, now=now, later=later):
            for row in (0, 8):
                mod = [cmod[plane, 0, pl.ds(8 + row, 8), :]]
                out = coupling(cu.at[now], cv.at[now], mod, plane, 8 + row, 1)
                d = cdiag[plane, 0, pl.ds(row, 8), :]
                keep, push = scales[k - 1]
                inv = cinv[plane, 0, pl.ds(row, 8), :] * push
                for c in range(3):
                    old = cu[now, c, plane, 0, pl.ds(8 + row, 8), :]
                    r = crest[c, plane, 0, pl.ds(row, 8), :] - d * old + out[c][0]
                    crest[c, plane, 0, pl.ds(row, 8), :] = r
                    step = keep * old + inv * r
                    cu[later, c, plane, 0, pl.ds(8 + row, 8), :] = step
                    cv[later, c, plane, 0, pl.ds(8 + row, 8), :] = mod[0] * step
            return carry

        lax.fori_loop(1 + k, 15 - k, sweep, 0)
        gather(later, False)

    for c in range(3):
        for p in range(4):
            coarse[c, p] = total[c, 2 + p, pl.ds(2, 4), pl.ds(0, 64)]

    matrix = pair_matrix((128, 256), 1)
    for tile in range(2):
        spread = jnp.dot(
            total[...].reshape(192, 128),
            matrix[:, 128 * tile : 128 * (tile + 1)],
            precision=lax.Precision.HIGHEST,
            preferred_element_type=jnp.float32,
        )
        wide[tile] = spread.reshape(3, 8, 8, 128)

    def lift(p, carry):
        for tile in range(2):
            for c in range(3):
                value = wide[tile, c, p]
                for dx in range(2):
                    for dy in range(2):
                        u[0, c, 2 * p + dx, tile, pl.ds(8 + dy, 8, stride=2), :] = value
        return carry

    lax.fori_loop(0, 8, lift, 0)

    def weigh(p, carry):
        for tile in range(2):
            mod = state[3, p, tile]
            for c in range(3):
                v[0, c, p, tile, pl.ds(8, 16), :] = mod * u[0, c, p, tile, pl.ds(8, 16), :]
        return carry

    lax.fori_loop(0, 16, weigh, 0)

    def add_own(slot, start):
        def body(p, carry):
            for c in range(3):
                step = u[slot, c, 4 + p, 0, pl.ds(12, 8), :]
                correction[c, p] = (smooth[c, p] if start else correction[c, p]) + step
            return carry

        lax.fori_loop(0, 8, body, 0)

    add_own(0, True)
    for k in range(SWEEPS):
        now, later = k % 2, (k + 1) % 2
        rows = (0, 8) if k < SWEEPS - 1 else (4,)

        def sweep(plane, carry, k=k, now=now, later=later, rows=rows):
            for row in rows:
                mod = [state[3, plane, tile, pl.ds(row, 8), :] for tile in range(2)]
                out = coupling(u.at[now], v.at[now], mod, plane, 8 + row, 2)
                for tile in range(2 if k < SWEEPS - 1 else 1):
                    d = state[4, plane, tile, pl.ds(row, 8), :]
                    keep, push = scales[k - 1] if k else (None, 1.0 / THETA)
                    inv = state[5, plane, tile, pl.ds(row, 8), :] * push
                    for c in range(3):
                        old = u[now, c, plane, tile, pl.ds(8 + row, 8), :]
                        r = state[c, plane, tile, pl.ds(row, 8), :] - d * old + out[c][tile]
                        step = inv * r
                        if k:
                            step = keep * old + step
                        if k < SWEEPS - 1:
                            state[c, plane, tile, pl.ds(row, 8), :] = r
                            u[later, c, plane, tile, pl.ds(8 + row, 8), :] = step
                            v[later, c, plane, tile, pl.ds(8 + row, 8), :] = mod[tile] * step
                        else:
                            correction[c, plane - 4] = correction[c, plane - 4] + step
            return carry

        lax.fori_loop(1 + k, 15 - k, sweep, 0)
        if k < SWEEPS - 1:
            add_own(later, False)


def call(kernel, outs, scratch=(), aliases=None):
    return pl.pallas_call(
        kernel,
        out_shape=[jax.ShapeDtypeStruct(s, jnp.float32) for s in outs],
        scratch_shapes=[pltpu.VMEM(s, jnp.float32) for s in scratch],
        input_output_aliases=aliases or {},
        compiler_params=pltpu.CompilerParams(vmem_limit_bytes=48 * 1024 * 1024),
    )


def neighbours(to_next, to_previous, axis):
    count = lax.axis_size(axis)
    before = lax.ppermute(to_next, axis, [(i, i + 1) for i in range(count - 1)])
    after = lax.ppermute(to_previous, axis, [(i + 1, i) for i in range(count - 1)])
    return before, after


def on_device(levels, residual):
    main, first, last = call(prepare, [(4, 8, 8, 128), (4, 1, 8, 128), (4, 1, 8, 128)])(levels, residual)
    left, right = neighbours(last, first, "gz")
    block = jnp.concatenate([main, left, right], axis=1)
    before, after = neighbours(block, block, "gx")
    slab = jnp.stack([before, block, after])
    down, up = neighbours(slab, slab, "gy")
    planes, rows = 24, 24
    smooth, message, state = call(
        smooth_kernel,
        [(3, 8, 8, 128), (4, 8, 8, 128), (6, 16, 2, 16, 128)],
        [
            (2, 3, planes, 2, rows + 16, 128),
            (2, 3, planes, 2, rows + 16, 128),
            (3, planes, 2, rows, 128),
            (planes, 2, rows + 16, 128),
            (planes, 2, rows, 128),
            (planes, 2, rows, 128),
            (2, 4, 8, 8, 128),
        ],
    )(down, slab, up)
    before, after = neighbours(message, message, "gx")
    slab = jnp.concatenate([before[:, :6], message[:, 2:6], after[:, 2:]], axis=1)
    down, up = neighbours(slab, slab, "gy")
    correction, coarse = call(
        functools.partial(post_outer),
        [(3, 8, 8, 128), (3, 4, 4, 64)],
        [
            (2, 3, 16, 1, 32, 128),
            (2, 3, 16, 1, 32, 128),
            (3, 16, 1, 16, 128),
            (16, 1, 32, 128),
            (16, 1, 16, 128),
            (16, 1, 16, 128),
            (3, 8, 8, 128),
            (2, 3, 16, 2, 32, 128),
            (2, 3, 16, 2, 32, 128),
            (2, 3, 8, 8, 128),
            (6, 16, 2, 16, 128),
        ],
    )(down, slab, up, state, smooth)
    return correction, coarse


def post_outer(down, own, up, state_in, smooth, correction, coarse, *scratch):
    state = scratch[-1]

    def copy(p, carry):
        for f in range(6):
            state[f, p] = state_in[f, p]
        return carry

    lax.fori_loop(0, 16, copy, 0)
    post_kernel(down, own, up, state, smooth, correction, coarse, *scratch[:-1])


def solution(mesh):
    return jax.shard_map(
        on_device,
        mesh=mesh,
        in_specs=(P("gx", "gy", "gz"), P(None, "gx", "gy", "gz")),
        out_specs=(P(None, "gx", "gy", "gz"), P(None, "gx", "gy", "gz")),
        check_vma=False,
    )
```

```python
import functools

import jax
import jax.numpy as jnp
from jax import lax
from jax.experimental import pallas as pl
from jax.experimental.pallas import tpu as pltpu
from jax.sharding import PartitionSpec as P

SWEEPS = 4
THETA = 1.15
DELTA = 0.85

FACE, SIDE, EDGE, FLAT, TURN, TWIST = 9.6, 6.0, 2.7, 1.8, 0.9, 0.4
UNIT = 120.0
WHOLE = 1.92
HALO = 16


def sweep_scales():
    sigma = THETA / DELTA
    rho = 1.0 / sigma
    scales = []
    for _ in range(SWEEPS - 1):
        rho_next = 1.0 / (2.0 * sigma - rho)
        scales.append((rho_next * rho, 2.0 * rho_next / DELTA))
        rho = rho_next
    return scales


def lane_index():
    return lax.broadcasted_iota(jnp.int32, (8, 128), 1)


def join_lanes(centre, above, below):
    up = [pltpu.roll(a, 127, 1) for a in above]
    down = [pltpu.roll(b, 1, 1) for b in below]
    if len(centre) == 2:
        lane = lane_index()
        last, first = lane == 127, lane == 0
        up = [jnp.where(last, up[1], up[0]), jnp.where(last, up[0], up[1])]
        down = [jnp.where(first, down[1], down[0]), jnp.where(first, down[0], down[1])]
    return [c + (u + d) for c, u, d in zip(centre, up, down)]


def stencil(field, plane, count, row, tiles):
    centre = [[[] for _ in range(3)] for _ in range(count)]
    above = [[[] for _ in range(3)] for _ in range(count)]
    below = [[[] for _ in range(3)] for _ in range(count)]
    for tile in range(tiles):
        mid, summed, spread = [], [], []
        for c in range(3):
            mids, sums, diffs = [], [], []
            for p in range(count + 2):
                u = field[c, plane + (p - 1), tile, pl.ds(row, 8), :]
                yp = field[c, plane + (p - 1), tile, pl.ds(row + 1, 8), :]
                ym = field[c, plane + (p - 1), tile, pl.ds(row - 1, 8), :]
                mids.append(u)
                sums.append(yp + ym)
                diffs.append(yp - ym)
            mid.append(mids)
            summed.append(sums)
            spread.append(diffs)
        for p in range(count):
            u, sy, dy = ([f[c][p + 1] for c in range(3)] for f in (mid, summed, spread))
            sx = [mid[c][p + 2] + mid[c][p] for c in range(3)]
            sxy = [summed[c][p + 2] + summed[c][p] for c in range(3)]
            dxy = [spread[c][p + 2] - spread[c][p] for c in range(2)]
            dx = {c: mid[c][p + 2] - mid[c][p] for c in (0, 2)}
            dx_sy = {c: summed[c][p + 2] - summed[c][p] for c in (0, 2)}
            dy_sx = {c: spread[c][p + 2] + spread[c][p] for c in (1, 2)}
            both = sx[2] + sy[2]
            flat = [
                FACE * sx[0] + SIDE * sy[0] + EDGE * sxy[0] + TURN * dxy[1],
                FACE * sy[1] + SIDE * sx[1] + EDGE * sxy[1] + TURN * dxy[0],
                SIDE * both + FLAT * sxy[2],
            ]
            even = [
                SIDE * u[0] + EDGE * sx[0] + FLAT * sy[0] + sxy[0] + TWIST * dxy[1],
                SIDE * u[1] + EDGE * sy[1] + FLAT * sx[1] + sxy[1] + TWIST * dxy[0],
                FACE * u[2] + EDGE * both + sxy[2],
            ]
            odd = [
                TURN * dx[2] + TWIST * dx_sy[2],
                TURN * dy[2] + TWIST * dy_sx[2],
                TURN * (dx[0] + dy[1]) + TWIST * (dx_sy[0] + dy_sx[1]),
            ]
            for c in range(3):
                centre[p][c].append(flat[c])
                above[p][c].append(even[c] + odd[c])
                below[p][c].append(even[c] - odd[c])
    return [[join_lanes(centre[p][c], above[p][c], below[p][c]) for c in range(3)] for p in range(count)]


def coupling(field, scaled, modulus, plane, count, row, tiles):
    plain = stencil(field, plane, count, row, tiles)
    part = [[[modulus[p][t] * plain[p][c][t] for t in range(tiles)] for c in range(3)] for p in range(count)]
    heavy = stencil(scaled, plane, count, row, tiles)
    return [[[part[p][c][t] + heavy[p][c][t] for t in range(tiles)] for c in range(3)] for p in range(count)]


def sweep(planes, rows, tiles, now, later, fields, scale, kept_tiles=None, emit=None):
    rest, modulus, diag, inverse = fields
    kept_tiles = kept_tiles or tiles
    lo, hi = planes
    chunk = next(n for n in (4, 7, 6, 5, 2, 1) if (hi - lo) % n == 0)

    def body(i, carry):
        first = lo + i * chunk
        for row in rows:
            mod = [[modulus(first + j, t, row) for t in range(tiles)] for j in range(chunk)]
            out = coupling(now[0], now[1], mod, first, chunk, 8 + row, tiles)
            for j in range(chunk):
                plane = first + j
                for t in range(kept_tiles):
                    d = diag(plane, t, row)
                    if scale:
                        inv = inverse(plane, t, row) * scale[1]
                    for c in range(3):
                        old = now[0][c, plane, t, pl.ds(8 + row, 8), :]
                        r = rest[c, plane, t, pl.ds(row, 8), :] - d * old + out[j][c][t]
                        if not emit:
                            rest[c, plane, t, pl.ds(row, 8), :] = r
                        if scale:
                            step = inv * r
                            if scale[0]:
                                step = scale[0] * old + step
                            if emit:
                                emit(c, plane, step)
                            else:
                                later[0][c, plane, t, pl.ds(8 + row, 8), :] = step
                                later[1][c, plane, t, pl.ds(8 + row, 8), :] = mod[j][t] * step
        return carry

    lax.fori_loop(0, (hi - lo) // chunk, body, 0)


def diagonal(modulus, plane, row, tiles):
    centre, even = [], []
    mids = []
    for tile in range(tiles):
        def at(dx, dy):
            return modulus[plane + dx, tile, pl.ds(row + dy, 8), :]

        u = at(0, 0)
        cross = (at(1, 0) + at(-1, 0)) + (at(0, 1) + at(0, -1))
        corner = (at(1, 1) + at(-1, -1)) + (at(1, -1) + at(-1, 1))
        even.append(0.16 * u + 0.06 * cross + 0.03 * corner)
        centre.append(WHOLE * u + 0.16 * cross + 0.06 * corner)
        mids.append(u)
    total = join_lanes(centre, even, even)
    out = []
    for tile in range(tiles):
        diag = (1.05 * 0.5 * UNIT) * total[tile]
        inside = mids[tile] > 0.0
        inverse = jnp.where(inside, 1.0 / jnp.where(inside, diag, 1.0), 0.0)
        out.append((mids[tile], diag, inverse))
    return out


def pair_matrix(shape, fine_axis):
    fine = lax.broadcasted_iota(jnp.int32, shape, fine_axis)
    coarse = lax.broadcasted_iota(jnp.int32, shape, 1 - fine_axis)
    return (lax.shift_right_logical(fine, 1) == coarse).astype(jnp.float32)


def prepare(levels, residual, main, first, last):
    lane = lane_index()
    for c in range(4):
        head = jnp.zeros((8, 128), jnp.float32)
        tail = jnp.zeros((8, 128), jnp.float32)
        for p in range(8):
            if c < 3:
                value = residual[c, p]
            else:
                ratio = levels[p].astype(jnp.float32) / 255.0
                value = (0.05 + 0.95 * ratio * ratio * ratio) / UNIT
            main[c, p] = value
            mine = (lane >= HALO * p) & (lane < HALO * (p + 1))
            head = jnp.where(mine, pltpu.roll(value, HALO * p, 1) if p else value, head)
            tail = jnp.where(mine, pltpu.roll(value, (HALO * p + HALO) % 128, 1) if p < 7 else value, tail)
        first[c, 0] = head
        last[c, 0] = tail


def smooth_kernel(down, own, up, smooth, message, state, ua, ub, va, vb, rest, modulus, diag, inverse, pairs):
    lane = lane_index()
    low, high = lane < HALO, lane >= 128 - HALO

    for t, block in enumerate((down, own, up)):
        def place(b, carry, t=t, block=block):
            for c in range(4):
                left, right = block[b, c, 8], block[b, c, 9]
                for p in range(8):
                    side_r = pltpu.roll(right, 128 - HALO * p, 1) if p else right
                    side_l = pltpu.roll(left, 112 - HALO * p, 1) if p < 7 else left
                    side = jnp.where(low, side_r, jnp.where(high, side_l, 0.0))
                    if c < 3:
                        rest[c, 8 * b + p, 0, pl.ds(8 * t, 8), :] = block[b, c, p]
                        rest[c, 8 * b + p, 1, pl.ds(8 * t, 8), :] = side
                    else:
                        modulus[8 * b + p, 0, pl.ds(8 + 8 * t, 8), :] = block[b, c, p]
                        modulus[8 * b + p, 1, pl.ds(8 + 8 * t, 8), :] = side
            return carry

        lax.fori_loop(0, 3, place, 0)

    def begin(plane, carry):
        for t in range(3):
            parts = diagonal(modulus, plane, 8 + 8 * t, 2)
            for tile, (mid, d, inv) in enumerate(parts):
                diag[plane, tile, pl.ds(8 * t, 8), :] = d
                inverse[plane, tile, pl.ds(8 * t, 8), :] = inv
                for c in range(3):
                    step = rest[c, plane, tile, pl.ds(8 * t, 8), :] * (inv * (1.0 / THETA))
                    ua[c, plane, tile, pl.ds(8 + 8 * t, 8), :] = step
                    va[c, plane, tile, pl.ds(8 + 8 * t, 8), :] = mid * step
        return carry

    lax.fori_loop(1, 23, begin, 0)

    def gather(slot, start):
        def body(p, carry):
            for c in range(3):
                step = slot[c, 8 + p, 0, pl.ds(16, 8), :]
                smooth[c, p] = step if start else smooth[c, p] + step
            return carry

        lax.fori_loop(0, 8, body, 0)

    gather(ua, True)
    scales = sweep_scales()

    def plain(ref, margin):
        return lambda plane, tile, row: ref[plane, tile, pl.ds(margin + row, 8), :]

    fields = (rest, plain(modulus, 8), plain(diag, 0), plain(inverse, 0))
    for k in range(1, SWEEPS + 1):
        now, later = ((ua, va), (ub, vb)) if k % 2 else ((ub, vb), (ua, va))
        planes = (1 + k, 23 - k) if k < SWEEPS else (5, 19)
        sweep(planes, (0, 8, 16) if k < 3 else (4, 12), 2, now, later, fields, scales[k - 1] if k < SWEEPS else None)
        if k < SWEEPS:
            gather(later[0], False)

    def restrict(p, carry):
        for tile in range(2):
            for c in range(4):
                total = None
                for dx in range(2):
                    for dy in range(2):
                        if c < 3:
                            part = rest[c, 4 + 2 * p + dx, tile, pl.ds(4 + dy, 8, stride=2), :]
                        else:
                            part = 0.25 * modulus[4 + 2 * p + dx, tile, pl.ds(12 + dy, 8, stride=2), :]
                        total = part if total is None else total + part
                pairs[tile, c, p] = total
        return carry

    lax.fori_loop(0, 8, restrict, 0)
    matrix = pair_matrix((256, 128), 0)
    coarse = jnp.dot(
        pairs[0].reshape(256, 128),
        matrix[:128],
        precision=lax.Precision.HIGHEST,
        preferred_element_type=jnp.float32,
    ) + jnp.dot(
        pairs[1].reshape(256, 128),
        matrix[128:],
        precision=lax.Precision.HIGHEST,
        preferred_element_type=jnp.float32,
    )
    message[...] = coarse.reshape(4, 8, 8, 128)

    def keep_state(p, carry):
        for tile in range(2):
            for c in range(3):
                state[c, p, tile] = rest[c, 4 + p, tile, pl.ds(4, 16), :]
            state[3, p, tile] = modulus[4 + p, tile, pl.ds(12, 16), :]
            state[4, p, tile] = diag[4 + p, tile, pl.ds(4, 16), :]
            state[5, p, tile] = inverse[4 + p, tile, pl.ds(4, 16), :]
        return carry

    lax.fori_loop(0, 16, keep_state, 0)


def post_kernel(down, own, up, state, smooth, correction, coarse, ca, cb, cva, cvb, crest, cmod, cinv, cdiag, total, ua, ub, va, vb, wide):
    scales = sweep_scales()

    def place(p, carry):
        for c in range(4):
            below, mid, above = down[c, p], own[c, p, pl.ds(2, 4), :], up[c, p]
            if c < 3:
                crest[c, p, 0, pl.ds(0, 8), :] = below
                crest[c, p, 0, pl.ds(8, 8), :] = above
                crest[c, p, 0, pl.ds(6, 4), :] = mid
            else:
                cmod[p, 0, pl.ds(8, 8), :] = below
                cmod[p, 0, pl.ds(16, 8), :] = above
                cmod[p, 0, pl.ds(14, 4), :] = mid
        return carry

    lax.fori_loop(0, 16, place, 0)

    def begin(plane, carry):
        for t in range(2):
            mid, d, inv = diagonal(cmod, plane, 8 + 8 * t, 1)[0]
            cdiag[plane, 0, pl.ds(8 * t, 8), :] = d
            cinv[plane, 0, pl.ds(8 * t, 8), :] = inv
            for c in range(3):
                step = crest[c, plane, 0, pl.ds(8 * t, 8), :] * (inv * (1.0 / THETA))
                ca[c, plane, 0, pl.ds(8 + 8 * t, 8), :] = step
                cva[c, plane, 0, pl.ds(8 + 8 * t, 8), :] = mid * step
        return carry

    lax.fori_loop(1, 15, begin, 0)

    def gather(slot, start):
        def body(p, carry):
            for c in range(3):
                step = slot[c, 4 + p, 0, pl.ds(12, 8), :]
                total[c, p] = step if start else total[c, p] + step
            return carry

        lax.fori_loop(0, 8, body, 0)

    gather(ca, True)

    def plain(ref, margin):
        return lambda plane, tile, row: ref[plane, tile, pl.ds(margin + row, 8), :]

    fields = (crest, plain(cmod, 8), plain(cdiag, 0), plain(cinv, 0))
    for k in range(1, SWEEPS):
        now, later = ((ca, cva), (cb, cvb)) if k % 2 else ((cb, cvb), (ca, cva))
        sweep((1 + k, 15 - k), (0, 8), 1, now, later, fields, scales[k - 1])
        gather(later[0], False)

    for c in range(3):
        for p in range(4):
            coarse[c, p] = total[c, 2 + p, pl.ds(2, 4), pl.ds(0, 64)]

    matrix = pair_matrix((128, 256), 1)
    for tile in range(2):
        spread = jnp.dot(
            total[...].reshape(192, 128),
            matrix[:, 128 * tile : 128 * (tile + 1)],
            precision=lax.Precision.HIGHEST,
            preferred_element_type=jnp.float32,
        )
        wide[tile] = spread.reshape(3, 8, 8, 128)

    def lift(p, carry):
        for tile in range(2):
            for c in range(3):
                value = wide[tile, c, p]
                for dx in range(2):
                    for dy in range(2):
                        ua[c, 2 * p + dx, tile, pl.ds(8 + dy, 8, stride=2), :] = value
        return carry

    lax.fori_loop(0, 8, lift, 0)

    def weigh(p, carry):
        for tile in range(2):
            mod = state[3, p, tile]
            for c in range(3):
                va[c, p, tile, pl.ds(8, 16), :] = mod * ua[c, p, tile, pl.ds(8, 16), :]
        return carry

    lax.fori_loop(0, 16, weigh, 0)

    def add_own(slot, start):
        def body(p, carry):
            for c in range(3):
                step = slot[c, 4 + p, 0, pl.ds(12, 8), :]
                correction[c, p] = (smooth[c, p] if start else correction[c, p]) + step
            return carry

        lax.fori_loop(0, 8, body, 0)

    add_own(ua, True)

    def held(index):
        return lambda plane, tile, row: state[index, plane, tile, pl.ds(row, 8), :]

    def emit(c, plane, step):
        correction[c, plane - 4] = correction[c, plane - 4] + step

    fields = (state, held(3), held(4), held(5))
    for k in range(SWEEPS):
        now, later = ((ub, vb), (ua, va)) if k % 2 else ((ua, va), (ub, vb))
        scale = scales[k - 1] if k else (None, 1.0 / THETA)
        if k < SWEEPS - 1:
            sweep((1 + k, 15 - k), (0, 8), 2, now, later, fields, scale)
            add_own(later[0], False)
        else:
            sweep((1 + k, 15 - k), (4,), 2, now, None, fields, scale, 1, emit)


def call(kernel, outs, scratch=(), aliases=None):
    return pl.pallas_call(
        kernel,
        out_shape=[jax.ShapeDtypeStruct(s, jnp.float32) for s in outs],
        scratch_shapes=[pltpu.VMEM(s, jnp.float32) for s in scratch],
        input_output_aliases=aliases or {},
        compiler_params=pltpu.CompilerParams(vmem_limit_bytes=48 * 1024 * 1024),
    )


def neighbours(to_next, to_previous, axis):
    count = lax.axis_size(axis)
    before = lax.ppermute(to_next, axis, [(i, i + 1) for i in range(count - 1)])
    after = lax.ppermute(to_previous, axis, [(i + 1, i) for i in range(count - 1)])
    return before, after


def on_device(levels, residual):
    main, first, last = call(prepare, [(4, 8, 8, 128), (4, 1, 8, 128), (4, 1, 8, 128)])(levels, residual)
    left, right = neighbours(last, first, "gz")
    block = jnp.concatenate([main, left, right], axis=1)
    before, after = neighbours(block, block, "gx")
    slab = jnp.stack([before, block, after])
    down, up = neighbours(slab, slab, "gy")
    planes, rows = 24, 24
    smooth, message, state = call(
        smooth_kernel,
        [(3, 8, 8, 128), (4, 8, 8, 128), (6, 16, 2, 16, 128)],
        [
            *[(3, planes, 2, rows + 16, 128)] * 4,
            (3, planes, 2, rows, 128),
            (planes, 2, rows + 16, 128),
            (planes, 2, rows, 128),
            (planes, 2, rows, 128),
            (2, 4, 8, 8, 128),
        ],
    )(down, slab, up)
    before, after = neighbours(message, message, "gx")
    slab = jnp.concatenate([before[:, :6], message[:, 2:6], after[:, 2:]], axis=1)
    down, up = neighbours(slab, slab, "gy")
    correction, coarse = call(
        functools.partial(post_outer),
        [(3, 8, 8, 128), (3, 4, 4, 64)],
        [
            *[(3, 16, 1, 32, 128)] * 4,
            (3, 16, 1, 16, 128),
            (16, 1, 32, 128),
            (16, 1, 16, 128),
            (16, 1, 16, 128),
            (3, 8, 8, 128),
            *[(3, 16, 2, 32, 128)] * 4,
            (2, 3, 8, 8, 128),
            (6, 16, 2, 16, 128),
        ],
    )(down, slab, up, state, smooth)
    return correction, coarse


def post_outer(down, own, up, state_in, smooth, correction, coarse, *scratch):
    state = scratch[-1]

    def copy(p, carry):
        for f in range(6):
            state[f, p] = state_in[f, p]
        return carry

    lax.fori_loop(0, 16, copy, 0)
    post_kernel(down, own, up, state, smooth, correction, coarse, *scratch[:-1])


def solution(mesh):
    return jax.shard_map(
        on_device,
        mesh=mesh,
        in_specs=(P("gx", "gy", "gz"), P(None, "gx", "gy", "gz")),
        out_specs=(P(None, "gx", "gy", "gz"), P(None, "gx", "gy", "gz")),
        check_vma=False,
    )
```

```python
import jax
import jax.numpy as jnp
from jax import lax
from jax.experimental import pallas as pl
from jax.experimental.pallas import tpu as pltpu
from jax.sharding import PartitionSpec as P

SWEEPS = 4
THETA = 1.15
DELTA = 0.85

FACE, SIDE, EDGE, FLAT, TURN, TWIST = 9.6, 6.0, 2.7, 1.8, 0.9, 0.4
UNIT = 120.0
WHOLE = 1.92
HALO = 16
CHUNKS = (4, 3, 2, 1)
FAR = pltpu.HBM


def sweep_scales():
    sigma = THETA / DELTA
    rho = 1.0 / sigma
    scales = []
    for _ in range(SWEEPS - 1):
        rho_next = 1.0 / (2.0 * sigma - rho)
        scales.append((rho_next * rho, 2.0 * rho_next / DELTA))
        rho = rho_next
    return scales


def lane_index():
    return lax.broadcasted_iota(jnp.int32, (8, 128), 1)


def by_group(values):
    group = lane_index() // 32
    out = jnp.full((8, 128), values[-1], jnp.float32)
    for g in range(len(values) - 1):
        out = jnp.where(group == g, values[g], out)
    return out


def neighbourhood(load, count):
    mid, summed, spread = [], [], []
    for p in range(-1, count + 1):
        u, yp, ym = load(p, 0), load(p, 1), load(p, -1)
        mid.append(u)
        summed.append(yp + ym)
        spread.append(yp - ym)
    return mid, summed, spread


def stencil(field, plane, count, row):
    def loader(c):
        return lambda p, dy: field[c, plane + p, pl.ds(row + dy, 8), :]

    flat, even, odd = ([[None] * 3 for _ in range(count)] for _ in range(3))
    cross, along, across = [None] * count, [None] * count, [None] * count
    mid, summed, spread = neighbourhood(loader(0), count)
    for p in range(count):
        u, sy = mid[p + 1], summed[p + 1]
        sx, sxy = mid[p + 2] + mid[p], summed[p + 2] + summed[p]
        flat[p][0] = FACE * sx + SIDE * sy + EDGE * sxy
        even[p][0] = SIDE * u + EDGE * sx + FLAT * sy + sxy
        cross[p] = spread[p + 2] - spread[p]
        along[p], across[p] = mid[p + 2] - mid[p], summed[p + 2] - summed[p]
    mid, summed, spread = neighbourhood(loader(1), count)
    for p in range(count):
        u, sy = mid[p + 1], summed[p + 1]
        sx, sxy = mid[p + 2] + mid[p], summed[p + 2] + summed[p]
        flat[p][1] = FACE * sy + SIDE * sx + EDGE * sxy + TURN * cross[p]
        even[p][1] = SIDE * u + EDGE * sy + FLAT * sx + sxy + TWIST * cross[p]
        back = spread[p + 2] - spread[p]
        flat[p][0] = flat[p][0] + TURN * back
        even[p][0] = even[p][0] + TWIST * back
        odd[p][2] = TURN * (along[p] + spread[p + 1]) + TWIST * (across[p] + (spread[p + 2] + spread[p]))
    mid, summed, spread = neighbourhood(loader(2), count)
    for p in range(count):
        both, sxy = mid[p + 2] + mid[p] + summed[p + 1], summed[p + 2] + summed[p]
        flat[p][2] = SIDE * both + FLAT * sxy
        even[p][2] = FACE * mid[p + 1] + EDGE * both + sxy
        odd[p][0] = TURN * (mid[p + 2] - mid[p]) + TWIST * (summed[p + 2] - summed[p])
        odd[p][1] = TURN * spread[p + 1] + TWIST * (spread[p + 2] + spread[p])
    return [[(flat[p][c], even[p][c] + odd[p][c], even[p][c] - odd[p][c]) for c in range(3)] for p in range(count)]


def side_stencil(field, plane, count, row):
    mid, summed, spread = neighbourhood(lambda p, dy: field[plane + p, pl.ds(row + dy, 8), :], count)
    group = lane_index() // 32
    flat_x, flat_y = by_group((FACE, SIDE, SIDE)), by_group((SIDE, FACE, SIDE))
    flat_xy, even_u = by_group((EDGE, EDGE, FLAT)), by_group((SIDE, SIDE, FACE))
    even_x, even_y = by_group((EDGE, FLAT, EDGE)), by_group((FLAT, EDGE, EDGE))
    found = []
    for p in range(count):
        u, sy, dy = mid[p + 1], summed[p + 1], spread[p + 1]
        sx, dx = mid[p + 2] + mid[p], mid[p + 2] - mid[p]
        sxy, dx_sy = summed[p + 2] + summed[p], summed[p + 2] - summed[p]
        dy_sx, dxy = spread[p + 2] + spread[p], spread[p + 2] - spread[p]
        along_x, along_y = TURN * dx + TWIST * dx_sy, TURN * dy + TWIST * dy_sx
        down = pltpu.roll(jnp.where(group == 1, dxy, along_y), 96, 1)
        up = pltpu.roll(jnp.where(group == 0, dxy, along_y), 32, 1)
        far = pltpu.roll(along_x, 64, 1)
        cross = jnp.where(group == 0, down, jnp.where(group == 1, up, 0.0))
        flat = flat_x * sx + flat_y * sy + flat_xy * sxy + TURN * cross
        even = even_u * u + even_x * sx + even_y * sy + sxy + TWIST * cross
        odd = jnp.where(group == 0, far, jnp.where(group == 1, down, far + up))
        found.append((flat, even + odd, even - odd))
    return found


def join_ring(part):
    centre, above, below = part
    return centre + (pltpu.roll(above, 127, 1) + pltpu.roll(below, 1, 1))


def side_lanes():
    lane = lane_index()
    return lane, lane % 32 == HALO


def join_sides(parts, side):
    lane, begins = side_lanes()
    ends = jnp.where(begins, side[1], side[2])
    side_above, side_below = side[1], side[2]
    joined = []
    for c, (centre, above, below) in enumerate(parts):
        inward = pltpu.roll(ends, 112 - 32 * c, 1)
        outward = pltpu.roll(jnp.where(lane == 0, above, below), 32 * c + HALO, 1)
        up = pltpu.roll(jnp.where(lane == 0, inward, above), 127, 1)
        down = pltpu.roll(jnp.where(lane == 127, inward, below), 1, 1)
        joined.append(centre + (up + down))
        side_above = jnp.where(lane == 32 * c + HALO, outward, side_above)
        side_below = jnp.where(lane == 32 * c + HALO - 1, outward, side_below)
    return joined, side[0] + (pltpu.roll(side_above, 127, 1) + pltpu.roll(side_below, 1, 1))


def shifted(main, side):
    lane, begins = side_lanes()
    inward = pltpu.roll(side, 112, 1)
    side_below, side_above = side, side
    for g in range(4):
        outward = pltpu.roll(main, 32 * g + HALO, 1)
        side_above = jnp.where(lane == 32 * g + HALO, outward, side_above)
        side_below = jnp.where(lane == 32 * g + HALO - 1, outward, side_below)
    return (
        (pltpu.roll(jnp.where(lane == 127, inward, main), 1, 1), pltpu.roll(jnp.where(lane == 0, inward, main), 127, 1)),
        (pltpu.roll(side_below, 1, 1), pltpu.roll(side_above, 127, 1)),
    )


def weighted(modulus, plain, heavy):
    here, before, after = modulus
    return (here * plain[0] + heavy[0], before * plain[1] + heavy[1], after * plain[2] + heavy[2])


def coupling(now, modulus, plane, count, row):
    plain, heavy = (stencil(now[k], plane, count, row) for k in range(2))
    parts = [[weighted(modulus[p][0], *both) for both in zip(plain[p], heavy[p])] for p in range(count)]
    if len(now) == 2:
        return [([join_ring(part) for part in parts[p]], None) for p in range(count)]
    plain, heavy = (side_stencil(now[2 + k], plane, count, row) for k in range(2))
    return [join_sides(parts[p], weighted(modulus[p][1], plain[p], heavy[p])) for p in range(count)]


def sweep(planes, rows, now, later, rest, modulus, diag, inverse, scale, emit=None):
    lo, hi = planes
    chunk = next(n for n in CHUNKS if (hi - lo) % n == 0)
    sides = len(rest) if not emit else 1

    def body(i, carry):
        first = lo + i * chunk
        for row in rows:
            mods = [[[read(first + j, row) for read in reads] for reads in modulus] for j in range(chunk)]
            out = coupling(now, mods, first, chunk, 8 + row)
            for j in range(chunk):
                plane = first + j
                for t in range(sides):
                    d = diag[t](plane, row)
                    if scale:
                        inv = inverse[t](plane, row) * scale[1]
                    for c in range(1 if t else 3):
                        at = (plane,) if t else (c, plane)
                        here, margin = (*at, pl.ds(row, 8), slice(None)), (*at, pl.ds(8 + row, 8), slice(None))
                        old = now[2 * t][margin]
                        r = rest[t][here] - d * old + (out[j][1] if t else out[j][0][c])
                        if not emit:
                            rest[t][here] = r
                        if scale:
                            step = inv * r
                            if scale[0]:
                                step = scale[0] * old + step
                            if emit:
                                emit(c, plane, step)
                            else:
                                later[2 * t][margin] = step
                                later[2 * t + 1][margin] = mods[j][t][0] * step
        return carry

    lax.fori_loop(0, (hi - lo) // chunk, body, 0)


def diagonal_parts(modulus, plane, row):
    def at(dx, dy):
        return modulus[plane + dx, pl.ds(row + dy, 8), :]

    u = at(0, 0)
    cross = (at(1, 0) + at(-1, 0)) + (at(0, 1) + at(0, -1))
    corner = (at(1, 1) + at(-1, -1)) + (at(1, -1) + at(-1, 1))
    even = 0.16 * u + 0.06 * cross + 0.03 * corner
    return u, (WHOLE * u + 0.16 * cross + 0.06 * corner, even, even)


def finish_diagonal(mid, total):
    diag = (1.05 * 0.5 * UNIT) * total
    inside = mid > 0.0
    return mid, diag, jnp.where(inside, 1.0 / jnp.where(inside, diag, 1.0), 0.0)


def ring_diagonal(modulus, plane, row):
    mid, part = diagonal_parts(modulus, plane, row)
    return finish_diagonal(mid, join_ring(part))


def side_diagonal(modulus, side_modulus, plane, row):
    mid, (centre, even, _) = diagonal_parts(modulus, plane, row)
    side_mid, (side_centre, side_even, _) = diagonal_parts(side_modulus, plane, row)
    (below, above), (side_below, side_above) = shifted(even, side_even)
    main = finish_diagonal(mid, centre + (below + above))
    side_mid, side_diag, side_inverse = finish_diagonal(side_mid, side_centre + (side_below + side_above))
    side_inverse = jnp.where(lane_index() < 96, side_inverse, 0.0)
    return main, (side_mid, side_diag, side_inverse), shifted(mid, side_mid)


def pair_matrix(group, fine_axis):
    fine = lax.broadcasted_iota(jnp.int32, (128, 128), fine_axis)
    coarse = lax.broadcasted_iota(jnp.int32, (128, 128), 1 - fine_axis)
    if group is None:
        return (lax.shift_right_logical(fine, 1) == coarse).astype(jnp.float32)
    inner = fine - 32 * group
    target = lax.shift_right_logical(fine, 1) - 16 * group + jnp.where(inner < HALO, 120, 56)
    return ((target == coarse) & (inner >= 0) & (inner < 32)).astype(jnp.float32)


def exact_dot(a, b):
    return jnp.dot(a, b, precision=lax.Precision.HIGHEST, preferred_element_type=jnp.float32)


def prepare(levels, residual, own, ahead, behind, held_levels, held_residual, sems):
    copies = [
        pltpu.make_async_copy(levels, held_levels, sems.at[0]),
        pltpu.make_async_copy(residual, held_residual, sems.at[1]),
    ]
    for copy in copies:
        copy.start()
    copies[0].wait()
    for p in range(8):
        ratio = held_levels[p].astype(jnp.float32) / 255.0
        value = (0.05 + 0.95 * ratio * ratio * ratio) / UNIT
        own[3, p] = value
        if p > 0:
            ahead[p - 1] = value
        if p < 7:
            behind[p] = value
    copies[1].wait()
    for c in range(3):
        for p in range(8):
            value = held_residual[c, p]
            own[c, p] = value
            if p > 1:
                ahead[7 + 6 * c + p - 2] = value
            if p < 6:
                behind[7 + 6 * c + p] = value


def fine_planes(own, left, right):
    found = []
    for plane in range(1, 23):
        if plane < 8:
            found.append((3, plane, left, (plane - 1,)))
        elif plane < 16:
            found.append((3, plane, own, (3, plane - 8)))
        else:
            found.append((3, plane, right, (plane - 16,)))
    for c in range(3):
        for plane in range(2, 22):
            if plane < 8:
                found.append((c, plane, left, (7 + 6 * c + plane - 2,)))
            elif plane < 16:
                found.append((c, plane, own, (c, plane - 8)))
            else:
                found.append((c, plane, right, (7 + 6 * c + plane - 16,)))
    return found


FINE_ROWS = 520


def fine_rows(c, plane):
    return (7 * (plane - 1), 7) if c == 3 else (154 + 6 * (20 * c + plane - 2), 6)


def pack_rows(own, left, right, ahead, behind):
    empty = jnp.zeros((8, 128), jnp.float32)
    ahead[pl.ds(FINE_ROWS - 8, 8), :] = empty
    behind[pl.ds(FINE_ROWS - 8, 8), :] = empty
    for c, plane, source, index in fine_planes(own, left, right):
        base, count = fine_rows(c, plane)
        ahead[pl.ds(base, count), :] = source[(*index, pl.ds(8 - count, count), slice(None))]
        behind[pl.ds(base, count), :] = source[(*index, pl.ds(0, count), slice(None))]


def pack_lanes(own, left, right, down, up, main, first, last):
    empty = jnp.zeros((24, 128), jnp.float32)
    for plane in (0, 1, 22, 23):
        for c in range(3):
            main[c, plane] = empty
    main[3, 0] = empty
    main[3, 23] = empty
    gap = jnp.zeros((2, 128), jnp.float32)
    for c, plane, source, index in fine_planes(own, left, right):
        base, count = fine_rows(c, plane)
        main[c, plane, pl.ds(0, 2), :] = gap
        main[c, plane, pl.ds(22, 2), :] = gap
        main[c, plane, pl.ds(8, 8), :] = source[index]
        main[c, plane, pl.ds(8 - count, count), :] = down[pl.ds(base, count), :]
        main[c, plane, pl.ds(16, count), :] = up[pl.ds(base, count), :]
    lane = lane_index()

    def pack(pair, carry):
        for t in range(3):
            head = jnp.zeros((8, 128), jnp.float32)
            tail = head
            for s in range(2):
                for c in range(4):
                    value, place = main[c, 2 * pair + s, pl.ds(8 * t, 8), :], 32 * c + HALO * s
                    mine = (lane >= place) & (lane < place + HALO)
                    head = jnp.where(mine, pltpu.roll(value, place, 1) if place else value, head)
                    turn = (place + HALO) % 128
                    tail = jnp.where(mine, pltpu.roll(value, turn, 1) if turn else value, tail)
            first[pair, pl.ds(8 * t, 8), :] = head
            last[pair, pl.ds(8 * t, 8), :] = tail
        return carry

    lax.fori_loop(0, 12, pack, 0, unroll=2)


LAYER_X = 6 * 8 + 3 * 5 * 6
LAYER_Y = 16 * 6 + 3 * 14 * 5
COARSE_ROWS_X = 192
COARSE_ROWS_Y = 368


def coarse_planes(own, left, right):
    found = []
    for i in range(16):
        if i < 6:
            found.append((3, i, left, (), 8 * i))
        elif i < 10:
            found.append((3, i, own, (3, i - 4), 0))
        else:
            found.append((3, i, right, (), 8 * (i - 10)))
    for c in range(3):
        for i in range(14):
            if i < 5:
                found.append((c, i + 1, left, (), 48 + 6 * (5 * c + i)))
            elif i < 9:
                found.append((c, i + 1, own, (c, i - 3), 1))
            else:
                found.append((c, i + 1, right, (), 48 + 6 * (5 * c + i - 9)))
    return found


def coarse_rows(c, plane):
    return (6 * plane, 6, 2) if c == 3 else (96 + 5 * (14 * c + plane - 1), 5, 1)


def pack_coarse(own, left, right, layer_ahead, layer_behind, ahead, behind):
    empty = jnp.zeros((8, 128), jnp.float32)
    for message, layer, offset in ((ahead, layer_ahead, 7), (behind, layer_behind, 4)):
        message[pl.ds(COARSE_ROWS_Y - 8, 8), :] = empty
        for f in range(4):
            base = LAYER_Y + 14 * f
            message[pl.ds(base, 1), :] = left[pl.ds(LAYER_X + 12 * f + offset, 1), :]
            message[pl.ds(base + 1, 12), :] = layer[f]
            message[pl.ds(base + 13, 1), :] = right[pl.ds(LAYER_X + 12 * f + offset, 1), :]
    for c, plane, source, index, row in coarse_planes(own, left, right):
        base, count, margin = coarse_rows(c, plane)
        ahead[pl.ds(base, count), :] = source[(*index, pl.ds(row, count), slice(None))]
        behind[pl.ds(base, count), :] = source[(*index, pl.ds(row + margin, count), slice(None))]


def smooth_kernel(
    main, before, after, smooth, message, ahead, behind, layer_ahead, layer_behind, state, side_state,
    ua, ub, va, vb, usa, usb, vsa, vsb, rest, modulus, diag, inverse, prev, next, rest_s, modulus_s, diag_s, inverse_s, prev_s, next_s, pairs, pairs_s,
):
    group = lane_index() // 32

    low = lane_index() % 32 < HALO

    def place(pair, carry):
        for s in range(2):
            plane = 2 * pair + s
            for t in range(3):
                here = pl.ds(8 * t, 8)
                for c in range(3):
                    rest[c, plane, here, :] = main[c, plane, here, :]
                modulus[plane, pl.ds(8 + 8 * t, 8), :] = main[3, plane, here, :]
                lower, upper = before[pair, here, :], after[pair, here, :]
                if s:
                    lower = pltpu.roll(lower, 128 - HALO, 1)
                else:
                    upper = pltpu.roll(upper, HALO, 1)
                value = jnp.where(low, lower, upper)
                rest_s[plane, here, :] = value
                spread = jnp.where(group == 1, pltpu.roll(value, 64, 1), pltpu.roll(value, 96, 1))
                spread = jnp.where(group == 0, pltpu.roll(value, 32, 1), spread)
                modulus_s[plane, pl.ds(8 + 8 * t, 8), :] = jnp.where(group == 3, value, spread)
        return carry

    lax.fori_loop(0, 12, place, 0, unroll=2)

    def begin(i, carry):
        for plane in (2 + 2 * i, 3 + 2 * i):
            for t in range(3):
                here, margin = pl.ds(8 * t, 8), pl.ds(8 + 8 * t, 8)
                (mid, d, inv), (mid_s, d_s, inv_s), beside = side_diagonal(modulus, modulus_s, plane, 8 + 8 * t)
                for refs, values in zip(((prev, next), (prev_s, next_s)), beside):
                    for ref, value in zip(refs, values):
                        ref[plane, here, :] = value
                diag[plane, here, :] = d
                inverse[plane, here, :] = inv
                diag_s[plane, here, :] = d_s
                inverse_s[plane, here, :] = inv_s
                inv = inv * (1.0 / THETA)
                for c in range(3):
                    step = rest[c, plane, here, :] * inv
                    ua[c, plane, margin, :] = step
                    va[c, plane, margin, :] = mid * step
                step = rest_s[plane, here, :] * (inv_s * (1.0 / THETA))
                usa[plane, margin, :] = step
                vsa[plane, margin, :] = mid_s * step
        return carry

    lax.fori_loop(0, 10, begin, 0)

    def gather(steps, start):
        def body(p, carry):
            for c in range(3):
                step = steps[c, 8 + p, pl.ds(16, 8), :]
                smooth[c, p] = step if start else smooth[c, p] + step
            return carry

        lax.fori_loop(0, 8, body, 0, unroll=4)

    gather(ua, True)
    scales = sweep_scales()

    def reader(ref, margin):
        return lambda plane, row: ref[plane, pl.ds(margin + row, 8), :]

    moduli = [
        [reader(modulus, 8), reader(prev, 0), reader(next, 0)],
        [reader(modulus_s, 8), reader(prev_s, 0), reader(next_s, 0)],
    ]
    readers = [moduli] + [[reader(ref, 0) for ref in refs] for refs in ((diag, diag_s), (inverse, inverse_s))]
    for k in range(1, SWEEPS + 1):
        now, later = (ua, va, usa, vsa), (ub, vb, usb, vsb)
        if k % 2 == 0:
            now, later = later, now
        rows = (0, 8, 16) if k == 1 else (4, 12)
        sweep((2 + k, 22 - k), rows, now, later, (rest, rest_s), *readers, scales[k - 1] if k < SWEEPS else None)
        if k < SWEEPS:
            gather(later[0], False)

    def restrict(p, carry):
        def four(ref, at, margin):
            a, b = (ref[(*at, 4 + 2 * p + dx, pl.ds(margin + 4, 8, stride=2), slice(None))] for dx in range(2))
            c, d = (ref[(*at, 4 + 2 * p + dx, pl.ds(margin + 5, 8, stride=2), slice(None))] for dx in range(2))
            return (a + b) + (c + d)

        for c in range(3):
            pairs[c, p] = four(rest, (c,), 0)
        pairs[3, p] = 0.25 * four(modulus, (), 8)
        pairs_s[0, p] = four(rest_s, (), 0)
        pairs_s[1, p] = 0.25 * four(modulus_s, (), 8)
        return carry

    lax.fori_loop(0, 8, restrict, 0, unroll=2)
    coarse = exact_dot(pairs[...].reshape(256, 128), pair_matrix(None, 0)).reshape(4, 8, 8, 128)
    for c in range(4):
        source = pairs_s[1 if c == 3 else 0].reshape(64, 128)
        message[c] = coarse[c] + exact_dot(source, pair_matrix(c % 3, 0)).reshape(8, 8, 128)
    for i in range(6):
        ahead[pl.ds(8 * i, 8), :] = message[3, i]
        behind[pl.ds(8 * i, 8), :] = message[3, 2 + i]
    for f, source in enumerate([rest.at[c] for c in range(3)] + [rest_s]):
        ahead[pl.ds(LAYER_X + 12 * f, 12), :] = source[13, pl.ds(6, 12), :]
        behind[pl.ds(LAYER_X + 12 * f, 12), :] = source[10, pl.ds(6, 12), :]
        for p in range(12):
            layer_ahead[f, pl.ds(p, 1), :] = source[6 + p, pl.ds(13, 1), :]
            layer_behind[f, pl.ds(p, 1), :] = source[6 + p, pl.ds(10, 1), :]
    empty = jnp.zeros((6, 128), jnp.float32)
    ahead[pl.ds(LAYER_X + 48, 6), :] = empty
    behind[pl.ds(LAYER_X + 48, 6), :] = empty
    for c in range(3):
        for i in range(5):
            ahead[pl.ds(48 + 6 * (5 * c + i), 6), :] = message[c, 1 + i, pl.ds(1, 6), :]
            behind[pl.ds(48 + 6 * (5 * c + i), 6), :] = message[c, 2 + i, pl.ds(1, 6), :]

    kept = (
        (modulus, modulus_s, 12), (diag, diag_s, 4), (inverse, inverse_s, 4), (prev, prev_s, 4), (next, next_s, 4)
    )

    def keep_state(p, carry):
        for c in range(3):
            state[c, p] = rest[c, 4 + p, pl.ds(4, 16), :]
        side_state[0, p] = rest_s[4 + p, pl.ds(4, 16), :]
        for f, (ref, ref_s, row) in enumerate(kept):
            state[3 + f, p] = ref[4 + p, pl.ds(row, 16), :]
            side_state[1 + f, p] = ref_s[4 + p, pl.ds(row, 16), :]
        return carry

    lax.fori_loop(0, 16, keep_state, 0, unroll=2)


def post_kernel(
    own, left, right, down, up, state_in, side_in, smooth, correction, coarse,
    ca, cb, cva, cvb, crest, cmod, cinv, cdiag, cprev, cnext, total, ua, ub, va, vb, usa, usb, vsa, vsb, wide, wide_s, rest, rest_s,
):
    scales = sweep_scales()

    empty = jnp.zeros((16, 128), jnp.float32)
    for c in range(3):
        crest[c, 0] = empty
        crest[c, 15] = empty
    edge = jnp.zeros((1, 128), jnp.float32)
    for c, plane, source, index, row in coarse_planes(own, left, right):
        base, count, margin = coarse_rows(c, plane)
        mid = source[(*index, pl.ds(row + margin, 4), slice(None))]
        below, above = down[pl.ds(base, count), :], up[pl.ds(base, count), :]
        if c < 3:
            crest[c, plane, pl.ds(0, 1), :] = edge
            crest[c, plane, pl.ds(1, 5), :] = below
            crest[c, plane, pl.ds(6, 4), :] = mid
            crest[c, plane, pl.ds(10, 5), :] = above
            crest[c, plane, pl.ds(15, 1), :] = edge
        else:
            cmod[plane, pl.ds(8, 6), :] = below
            cmod[plane, pl.ds(14, 4), :] = mid
            cmod[plane, pl.ds(18, 6), :] = above

    def begin(i, carry):
        for plane in (1 + 2 * i, 2 + 2 * i):
            for t in range(2):
                here, margin = pl.ds(8 * t, 8), pl.ds(8 + 8 * t, 8)
                mid, d, inv = ring_diagonal(cmod, plane, 8 + 8 * t)
                cdiag[plane, here, :] = d
                cprev[plane, here, :] = pltpu.roll(mid, 1, 1)
                cnext[plane, here, :] = pltpu.roll(mid, 127, 1)
                cinv[plane, here, :] = inv
                inv = inv * (1.0 / THETA)
                for c in range(3):
                    step = crest[c, plane, here, :] * inv
                    ca[c, plane, margin, :] = step
                    cva[c, plane, margin, :] = mid * step
        return carry

    lax.fori_loop(0, 7, begin, 0)

    def gather(steps, start):
        def body(p, carry):
            for c in range(3):
                step = steps[c, 4 + p, pl.ds(12, 8), :]
                total[c, p] = step if start else total[c, p] + step
            return carry

        lax.fori_loop(0, 8, body, 0, unroll=4)

    gather(ca, True)

    def reader(ref, margin):
        return lambda plane, row: ref[plane, pl.ds(margin + row, 8), :]

    coarse_moduli = [[reader(cmod, 8), reader(cprev, 0), reader(cnext, 0)]]
    for k in range(1, SWEEPS):
        now, later = ((ca, cva), (cb, cvb)) if k % 2 else ((cb, cvb), (ca, cva))
        sweep((1 + k, 15 - k), (0, 8), now, later, (crest,), coarse_moduli, [reader(cdiag, 0)], [reader(cinv, 0)], scales[k - 1])
        gather(later[0], False)

    for c in range(3):
        for p in range(4):
            coarse[c, p] = total[c, 2 + p, pl.ds(2, 4), pl.ds(0, 64)]

    wide[...] = exact_dot(total[...].reshape(192, 128), pair_matrix(None, 1)).reshape(3, 8, 8, 128)
    spread = None
    for c in range(3):
        part = exact_dot(total[c].reshape(64, 128), pair_matrix(c, 1))
        spread = part if spread is None else spread + part
    wide_s[...] = spread.reshape(8, 8, 128)

    def lift(p, carry):
        for dx in range(2):
            for dy in range(2):
                for c in range(3):
                    ua[c, 2 * p + dx, pl.ds(8 + dy, 8, stride=2), :] = wide[c, p]
                usa[2 * p + dx, pl.ds(8 + dy, 8, stride=2), :] = wide_s[p]
        return carry

    lax.fori_loop(0, 8, lift, 0, unroll=2)

    def weigh(p, carry):
        for c in range(3):
            va[c, p, pl.ds(8, 16), :] = state_in[3, p] * ua[c, p, pl.ds(8, 16), :]
            rest[c, p] = state_in[c, p]
        vsa[p, pl.ds(8, 16), :] = side_in[1, p] * usa[p, pl.ds(8, 16), :]
        rest_s[p] = side_in[0, p]
        return carry

    lax.fori_loop(0, 16, weigh, 0, unroll=2)
    for f, target in enumerate([rest.at[c] for c in range(3)] + [rest_s]):
        target[1, pl.ds(2, 12), :] = left[pl.ds(LAYER_X + 12 * f, 12), :]
        target[14, pl.ds(2, 12), :] = right[pl.ds(LAYER_X + 12 * f, 12), :]
        for p in range(14):
            target[1 + p, pl.ds(1, 1), :] = down[pl.ds(LAYER_Y + 14 * f + p, 1), :]
            target[1 + p, pl.ds(14, 1), :] = up[pl.ds(LAYER_Y + 14 * f + p, 1), :]

    def add_own(steps, start):
        def body(p, carry):
            for c in range(3):
                step = steps[c, 4 + p, pl.ds(12, 8), :]
                correction[c, p] = (smooth[c, p] if start else correction[c, p]) + step
            return carry

        lax.fori_loop(0, 8, body, 0, unroll=4)

    add_own(ua, True)

    def held(f):
        return [
            lambda plane, row: state_in[3 + f, plane, pl.ds(row, 8), :],
            lambda plane, row: side_in[1 + f, plane, pl.ds(row, 8), :],
        ]

    moduli = list(zip(held(0), held(3), held(4)))

    def emit(c, plane, step):
        correction[c, plane - 4] = correction[c, plane - 4] + step

    for k in range(SWEEPS):
        now, later = (ua, va, usa, vsa), (ub, vb, usb, vsb)
        if k % 2:
            now, later = later, now
        scale = scales[k - 1] if k else (None, 1.0 / THETA)
        last = k == SWEEPS - 1
        sweep(
            (1 + k, 15 - k), (4,) if last else (0, 8), now, later, (rest, rest_s), moduli, held(1), held(2), scale,
            emit if last else None,
        )
        if not last:
            add_own(later[0], False)


def call(kernel, outs, scratch=(), far=False, extra=()):
    return pl.pallas_call(
        kernel,
        out_shape=[jax.ShapeDtypeStruct(s, jnp.float32) for s in outs],
        **(dict(in_specs=[pl.BlockSpec(memory_space=FAR)] * 2) if far else {}),
        scratch_shapes=[pltpu.VMEM(s, jnp.float32) for s in scratch] + list(extra),
        compiler_params=pltpu.CompilerParams(vmem_limit_bytes=48 * 1024 * 1024),
    )


def neighbours(to_next, to_previous, axis):
    count = lax.axis_size(axis)
    before = lax.ppermute(to_next, axis, [(i, i + 1) for i in range(count - 1)])
    after = lax.ppermute(to_previous, axis, [(i + 1, i) for i in range(count - 1)])
    return before, after


SMOOTH_OUTS = [
    (3, 8, 8, 128),
    (4, 8, 8, 128),
    (COARSE_ROWS_X, 128),
    (COARSE_ROWS_X, 128),
    (4, 12, 128),
    (4, 12, 128),
    (8, 16, 16, 128),
    (6, 16, 16, 128),
]
SMOOTH_SCRATCH = [
    *[(3, 24, 40, 128)] * 4,
    *[(24, 40, 128)] * 4,
    (3, 24, 24, 128),
    (24, 40, 128),
    *[(24, 24, 128)] * 5,
    (24, 40, 128),
    *[(24, 24, 128)] * 4,
    (4, 8, 8, 128),
    (2, 8, 8, 128),
]
POST_OUTS = [(3, 8, 8, 128), (3, 4, 4, 64)]
POST_SCRATCH = [
    *[(3, 16, 32, 128)] * 4,
    (3, 16, 16, 128),
    (16, 32, 128),
    *[(16, 16, 128)] * 4,
    (3, 8, 8, 128),
    *[(3, 16, 32, 128)] * 4,
    *[(16, 32, 128)] * 4,
    (3, 8, 8, 128),
    (8, 8, 128),
    (3, 16, 16, 128),
    (16, 16, 128),
]


def on_device(levels, residual):
    own, ahead, behind = call(
        prepare,
        [(4, 8, 8, 128), (25, 8, 128), (25, 8, 128)],
        far=True,
        extra=[pltpu.VMEM((8, 8, 128), jnp.int32), pltpu.VMEM((3, 8, 8, 128), jnp.float32), pltpu.SemaphoreType.DMA((2,))],
    )(levels, residual)
    left, right = neighbours(ahead, behind, "gx")
    ahead, behind = call(pack_rows, [(FINE_ROWS, 128)] * 2)(own, left, right)
    down, up = neighbours(ahead, behind, "gy")
    main, first, last = call(pack_lanes, [(4, 24, 24, 128), (12, 24, 128), (12, 24, 128)])(own, left, right, down, up)
    before, after = neighbours(last, first, "gz")
    smooth, own, ahead, behind, layer_ahead, layer_behind, state, side_state = call(
        smooth_kernel, SMOOTH_OUTS, SMOOTH_SCRATCH
    )(main, before, after)
    left, right = neighbours(ahead, behind, "gx")
    ahead, behind = call(pack_coarse, [(COARSE_ROWS_Y, 128)] * 2)(own, left, right, layer_ahead, layer_behind)
    down, up = neighbours(ahead, behind, "gy")
    correction, coarse = call(post_kernel, POST_OUTS, POST_SCRATCH)(own, left, right, down, up, state, side_state, smooth)
    return correction, coarse


def solution(mesh):
    return jax.shard_map(
        on_device,
        mesh=mesh,
        in_specs=(P("gx", "gy", "gz"), P(None, "gx", "gy", "gz")),
        out_specs=(P(None, "gx", "gy", "gz"), P(None, "gx", "gy", "gz")),
        check_vma=False,
    )
```

```python
import jax
import jax.numpy as jnp
from jax import lax
from jax.experimental import pallas as pl
from jax.experimental.pallas import tpu as pltpu
from jax.sharding import PartitionSpec as P

SWEEPS = 4
THETA = 1.15
DELTA = 0.85

FACE, SIDE, EDGE, FLAT, TURN, TWIST = 9.6, 6.0, 2.7, 1.8, 0.9, 0.4
UNIT = 120.0
WHOLE = 1.92
HALO = 16
CHUNKS = (4, 3, 2, 1)


def sweep_scales():
    sigma = THETA / DELTA
    rho = 1.0 / sigma
    scales = []
    for _ in range(SWEEPS - 1):
        rho_next = 1.0 / (2.0 * sigma - rho)
        scales.append((rho_next * rho, 2.0 * rho_next / DELTA))
        rho = rho_next
    return scales


def lane_index():
    return lax.broadcasted_iota(jnp.int32, (8, 128), 1)


def by_group(values):
    group = lane_index() // 32
    out = jnp.full((8, 128), values[-1], jnp.float32)
    for g in range(len(values) - 1):
        out = jnp.where(group == g, values[g], out)
    return out


def neighbourhood(load, count):
    mid, summed, spread = [], [], []
    for p in range(-1, count + 1):
        u, yp, ym = load(p, 0), load(p, 1), load(p, -1)
        mid.append(u)
        summed.append(yp + ym)
        spread.append(yp - ym)
    return mid, summed, spread


def stencil(field, plane, count, row):
    def loader(c):
        return lambda p, dy: field[c, plane + p, pl.ds(row + dy, 8), :]

    flat, even, odd = ([[None] * 3 for _ in range(count)] for _ in range(3))
    cross, along, across = [None] * count, [None] * count, [None] * count
    mid, summed, spread = neighbourhood(loader(0), count)
    for p in range(count):
        u, sy = mid[p + 1], summed[p + 1]
        sx, sxy = mid[p + 2] + mid[p], summed[p + 2] + summed[p]
        flat[p][0] = FACE * sx + SIDE * sy + EDGE * sxy
        even[p][0] = SIDE * u + EDGE * sx + FLAT * sy + sxy
        cross[p] = spread[p + 2] - spread[p]
        along[p], across[p] = mid[p + 2] - mid[p], summed[p + 2] - summed[p]
    mid, summed, spread = neighbourhood(loader(1), count)
    for p in range(count):
        u, sy = mid[p + 1], summed[p + 1]
        sx, sxy = mid[p + 2] + mid[p], summed[p + 2] + summed[p]
        flat[p][1] = FACE * sy + SIDE * sx + EDGE * sxy + TURN * cross[p]
        even[p][1] = SIDE * u + EDGE * sy + FLAT * sx + sxy + TWIST * cross[p]
        back = spread[p + 2] - spread[p]
        flat[p][0] = flat[p][0] + TURN * back
        even[p][0] = even[p][0] + TWIST * back
        odd[p][2] = TURN * (along[p] + spread[p + 1]) + TWIST * (across[p] + (spread[p + 2] + spread[p]))
    mid, summed, spread = neighbourhood(loader(2), count)
    for p in range(count):
        both, sxy = mid[p + 2] + mid[p] + summed[p + 1], summed[p + 2] + summed[p]
        flat[p][2] = SIDE * both + FLAT * sxy
        even[p][2] = FACE * mid[p + 1] + EDGE * both + sxy
        odd[p][0] = TURN * (mid[p + 2] - mid[p]) + TWIST * (summed[p + 2] - summed[p])
        odd[p][1] = TURN * spread[p + 1] + TWIST * (spread[p + 2] + spread[p])
    return [[(flat[p][c], even[p][c] + odd[p][c], even[p][c] - odd[p][c]) for c in range(3)] for p in range(count)]


def side_stencil(field, plane, count, row):
    mid, summed, spread = neighbourhood(lambda p, dy: field[plane + p, pl.ds(row + dy, 8), :], count)
    group = lane_index() // 32
    flat_x, flat_y = by_group((FACE, SIDE, SIDE)), by_group((SIDE, FACE, SIDE))
    flat_xy, even_u = by_group((EDGE, EDGE, FLAT)), by_group((SIDE, SIDE, FACE))
    even_x, even_y = by_group((EDGE, FLAT, EDGE)), by_group((FLAT, EDGE, EDGE))
    found = []
    for p in range(count):
        u, sy, dy = mid[p + 1], summed[p + 1], spread[p + 1]
        sx, dx = mid[p + 2] + mid[p], mid[p + 2] - mid[p]
        sxy, dx_sy = summed[p + 2] + summed[p], summed[p + 2] - summed[p]
        dy_sx, dxy = spread[p + 2] + spread[p], spread[p + 2] - spread[p]
        along_x, along_y = TURN * dx + TWIST * dx_sy, TURN * dy + TWIST * dy_sx
        down = pltpu.roll(jnp.where(group == 1, dxy, along_y), 96, 1)
        up = pltpu.roll(jnp.where(group == 0, dxy, along_y), 32, 1)
        far = pltpu.roll(along_x, 64, 1)
        cross = jnp.where(group == 0, down, jnp.where(group == 1, up, 0.0))
        flat = flat_x * sx + flat_y * sy + flat_xy * sxy + TURN * cross
        even = even_u * u + even_x * sx + even_y * sy + sxy + TWIST * cross
        odd = jnp.where(group == 0, far, jnp.where(group == 1, down, far + up))
        found.append((flat, even + odd, even - odd))
    return found


def join_ring(part):
    centre, above, below = part
    return centre + (pltpu.roll(above, 127, 1) + pltpu.roll(below, 1, 1))


def side_lanes():
    lane = lane_index()
    return lane, lane % 32 == HALO


def join_sides(parts, side):
    lane, begins = side_lanes()
    ends = jnp.where(begins, side[1], side[2])
    side_above, side_below = side[1], side[2]
    joined = []
    for c, (centre, above, below) in enumerate(parts):
        inward = pltpu.roll(ends, 112 - 32 * c, 1)
        outward = pltpu.roll(jnp.where(lane == 0, above, below), 32 * c + HALO, 1)
        up = pltpu.roll(jnp.where(lane == 0, inward, above), 127, 1)
        down = pltpu.roll(jnp.where(lane == 127, inward, below), 1, 1)
        joined.append(centre + (up + down))
        side_above = jnp.where(lane == 32 * c + HALO, outward, side_above)
        side_below = jnp.where(lane == 32 * c + HALO - 1, outward, side_below)
    return joined, side[0] + (pltpu.roll(side_above, 127, 1) + pltpu.roll(side_below, 1, 1))


def shifted(main, side):
    lane, begins = side_lanes()
    inward = pltpu.roll(side, 112, 1)
    side_below, side_above = side, side
    for g in range(3):
        outward = pltpu.roll(main, 32 * g + HALO, 1)
        side_above = jnp.where(lane == 32 * g + HALO, outward, side_above)
        side_below = jnp.where(lane == 32 * g + HALO - 1, outward, side_below)
    return (
        (pltpu.roll(jnp.where(lane == 127, inward, main), 1, 1), pltpu.roll(jnp.where(lane == 0, inward, main), 127, 1)),
        (pltpu.roll(side_below, 1, 1), pltpu.roll(side_above, 127, 1)),
    )


def weighted(modulus, plain, heavy):
    here, before, after = modulus
    return (here * plain[0] + heavy[0], before * plain[1] + heavy[1], after * plain[2] + heavy[2])


def coupling(now, modulus, plane, count, row):
    plain, heavy = (stencil(now[k], plane, count, row) for k in range(2))
    parts = [[weighted(modulus[p][0], *both) for both in zip(plain[p], heavy[p])] for p in range(count)]
    if len(now) == 2:
        return [([join_ring(part) for part in parts[p]], None) for p in range(count)]
    plain, heavy = (side_stencil(now[2 + k], plane, count, row) for k in range(2))
    return [join_sides(parts[p], weighted(modulus[p][1], plain[p], heavy[p])) for p in range(count)]


def sweep(planes, rows, now, later, rest, modulus, diag, inverse, scale, emit=None):
    lo, hi = planes
    chunk = next(n for n in CHUNKS if (hi - lo) % n == 0)
    sides = len(rest) if not emit else 1

    def body(i, carry):
        first = lo + i * chunk
        for row in rows:
            mods = [[[read(first + j, row) for read in reads] for reads in modulus] for j in range(chunk)]
            out = coupling(now, mods, first, chunk, 8 + row)
            for j in range(chunk):
                plane = first + j
                for t in range(sides):
                    d = diag[t](plane, row)
                    if scale:
                        inv = inverse[t](plane, row) * scale[1]
                    for c in range(1 if t else 3):
                        at = (plane,) if t else (c, plane)
                        here, margin = (*at, pl.ds(row, 8), slice(None)), (*at, pl.ds(8 + row, 8), slice(None))
                        old = now[2 * t][margin]
                        r = rest[t][here] - d * old + (out[j][1] if t else out[j][0][c])
                        if not emit:
                            rest[t][here] = r
                        if scale:
                            step = inv * r
                            if scale[0]:
                                step = scale[0] * old + step
                            if emit:
                                emit(c, plane, step)
                            else:
                                later[2 * t][margin] = step
                                later[2 * t + 1][margin] = mods[j][t][0] * step
        return carry

    lax.fori_loop(0, (hi - lo) // chunk, body, 0)


def diagonal_parts(modulus, plane, row):
    def at(dx, dy):
        return modulus[plane + dx, pl.ds(row + dy, 8), :]

    u = at(0, 0)
    cross = (at(1, 0) + at(-1, 0)) + (at(0, 1) + at(0, -1))
    corner = (at(1, 1) + at(-1, -1)) + (at(1, -1) + at(-1, 1))
    even = 0.16 * u + 0.06 * cross + 0.03 * corner
    return u, (WHOLE * u + 0.16 * cross + 0.06 * corner, even, even)


def finish_diagonal(mid, total):
    diag = (1.05 * 0.5 * UNIT) * total
    inside = mid > 0.0
    return mid, diag, jnp.where(inside, 1.0 / jnp.where(inside, diag, 1.0), 0.0)


def ring_diagonal(modulus, plane, row):
    mid, part = diagonal_parts(modulus, plane, row)
    return finish_diagonal(mid, join_ring(part))


def side_diagonal(modulus, side_modulus, plane, row):
    mid, (centre, even, _) = diagonal_parts(modulus, plane, row)
    side_mid, (side_centre, side_even, _) = diagonal_parts(side_modulus, plane, row)
    (below, above), (side_below, side_above) = shifted(even, side_even)
    main = finish_diagonal(mid, centre + (below + above))
    side_mid, side_diag, side_inverse = finish_diagonal(side_mid, side_centre + (side_below + side_above))
    side_inverse = jnp.where(lane_index() < 96, side_inverse, 0.0)
    return main, (side_mid, side_diag, side_inverse), shifted(mid, side_mid)


def pair_matrix(group, fine_axis):
    fine = lax.broadcasted_iota(jnp.int32, (128, 128), fine_axis)
    coarse = lax.broadcasted_iota(jnp.int32, (128, 128), 1 - fine_axis)
    if group is None:
        return (lax.shift_right_logical(fine, 1) == coarse).astype(jnp.float32)
    inner = fine - 32 * group
    target = lax.shift_right_logical(fine, 1) - 16 * group + jnp.where(inner < HALO, 120, 56)
    return ((target == coarse) & (inner >= 0) & (inner < 32)).astype(jnp.float32)


def exact_dot(a, b):
    return jnp.dot(a, b, precision=lax.Precision.HIGHEST, preferred_element_type=jnp.float32)


def pack_planes(own, ahead, behind):
    for p in range(8):
        if p > 0:
            ahead[p - 1] = own[3, p]
        if p < 7:
            behind[p] = own[3, p]
        for c in range(3):
            if p > 1:
                ahead[7 + 6 * c + p - 2] = own[c, p]
            if p < 6:
                behind[7 + 6 * c + p] = own[c, p]


def fine_planes(own, left, right):
    found = []
    for plane in range(1, 23):
        if plane < 8:
            found.append((3, plane, left, (plane - 1,)))
        elif plane < 16:
            found.append((3, plane, own, (3, plane - 8)))
        else:
            found.append((3, plane, right, (plane - 16,)))
    for c in range(3):
        for plane in range(2, 22):
            if plane < 8:
                found.append((c, plane, left, (7 + 6 * c + plane - 2,)))
            elif plane < 16:
                found.append((c, plane, own, (c, plane - 8)))
            else:
                found.append((c, plane, right, (7 + 6 * c + plane - 16,)))
    return found


FINE_ROWS = 520


def fine_rows(c, plane):
    return (7 * (plane - 1), 7) if c == 3 else (154 + 6 * (20 * c + plane - 2), 6)


def pack_rows(own, right, left, ahead, behind):
    empty = jnp.zeros((8, 128), jnp.float32)
    ahead[pl.ds(FINE_ROWS - 8, 8), :] = empty
    behind[pl.ds(FINE_ROWS - 8, 8), :] = empty
    for c, plane, source, index in fine_planes(own, left, right):
        base, count = fine_rows(c, plane)
        ahead[pl.ds(base, count), :] = source[(*index, pl.ds(8 - count, count), slice(None))]
        behind[pl.ds(base, count), :] = source[(*index, pl.ds(0, count), slice(None))]


def pack_lanes(own, right, left, up, down, main, first, last):
    empty = jnp.zeros((24, 128), jnp.float32)
    for plane in (0, 1, 22, 23):
        for c in range(3):
            main[c, plane] = empty
    main[3, 0] = empty
    main[3, 23] = empty
    gap = jnp.zeros((2, 128), jnp.float32)
    for c, plane, source, index in fine_planes(own, left, right):
        base, count = fine_rows(c, plane)
        main[c, plane, pl.ds(0, 2), :] = gap
        main[c, plane, pl.ds(22, 2), :] = gap
        main[c, plane, pl.ds(8, 8), :] = source[index]
        main[c, plane, pl.ds(8 - count, count), :] = down[pl.ds(base, count), :]
        main[c, plane, pl.ds(16, count), :] = up[pl.ds(base, count), :]
    lane = lane_index()

    def pack(pair, carry):
        for t in range(3):
            head = jnp.zeros((8, 128), jnp.float32)
            tail = head
            for s in range(2):
                for c in range(4):
                    value, place = main[c, 2 * pair + s, pl.ds(8 * t, 8), :], 32 * c + HALO * s
                    mine = (lane >= place) & (lane < place + HALO)
                    head = jnp.where(mine, pltpu.roll(value, place, 1) if place else value, head)
                    turn = (place + HALO) % 128
                    tail = jnp.where(mine, pltpu.roll(value, turn, 1) if turn else value, tail)
            first[pair, pl.ds(8 * t, 8), :] = head
            last[pair, pl.ds(8 * t, 8), :] = tail
        return carry

    lax.fori_loop(0, 12, pack, 0, unroll=2)


LAYER_X = 6 * 8 + 3 * 5 * 6
LAYER_Y = 16 * 6 + 3 * 14 * 5
COARSE_ROWS_X = 192
COARSE_ROWS_Y = 368


def coarse_planes(own, left, right):
    found = []
    for i in range(16):
        if i < 6:
            found.append((3, i, left, (), 8 * i))
        elif i < 10:
            found.append((3, i, own, (3, i - 4), 0))
        else:
            found.append((3, i, right, (), 8 * (i - 10)))
    for c in range(3):
        for i in range(14):
            if i < 5:
                found.append((c, i + 1, left, (), 48 + 6 * (5 * c + i)))
            elif i < 9:
                found.append((c, i + 1, own, (c, i - 3), 1))
            else:
                found.append((c, i + 1, right, (), 48 + 6 * (5 * c + i - 9)))
    return found


def coarse_rows(c, plane):
    return (6 * plane, 6, 2) if c == 3 else (96 + 5 * (14 * c + plane - 1), 5, 1)


def pack_coarse(own, right, left, layer_ahead, layer_behind, ahead, behind):
    empty = jnp.zeros((8, 128), jnp.float32)
    for message, layer, offset in ((ahead, layer_ahead, 7), (behind, layer_behind, 4)):
        message[pl.ds(COARSE_ROWS_Y - 8, 8), :] = empty
        for f in range(4):
            base = LAYER_Y + 14 * f
            message[pl.ds(base, 1), :] = left[pl.ds(LAYER_X + 12 * f + offset, 1), :]
            message[pl.ds(base + 1, 12), :] = layer[f]
            message[pl.ds(base + 13, 1), :] = right[pl.ds(LAYER_X + 12 * f + offset, 1), :]
    for c, plane, source, index, row in coarse_planes(own, left, right):
        base, count, margin = coarse_rows(c, plane)
        ahead[pl.ds(base, count), :] = source[(*index, pl.ds(row, count), slice(None))]
        behind[pl.ds(base, count), :] = source[(*index, pl.ds(row + margin, count), slice(None))]


def smooth_kernel(
    main, after, before, smooth, message, ahead, behind, layer_ahead, layer_behind, state, side_state,
    ua, ub, va, vb, usa, usb, vsa, vsb, rest, modulus, diag, inverse, prev, next, rest_s, modulus_s, diag_s, inverse_s, prev_s, next_s, pairs, pairs_s,
):
    group = lane_index() // 32

    low = lane_index() % 32 < HALO

    def place(pair, carry):
        for s in range(2):
            plane = 2 * pair + s
            for t in range(3):
                here = pl.ds(8 * t, 8)
                for c in range(3):
                    rest[c, plane, here, :] = main[c, plane, here, :]
                modulus[plane, pl.ds(8 + 8 * t, 8), :] = main[3, plane, here, :]
                lower, upper = before[pair, here, :], after[pair, here, :]
                if s:
                    lower = pltpu.roll(lower, 128 - HALO, 1)
                else:
                    upper = pltpu.roll(upper, HALO, 1)
                value = jnp.where(low, lower, upper)
                rest_s[plane, here, :] = value
                spread = jnp.where(group == 1, pltpu.roll(value, 64, 1), pltpu.roll(value, 96, 1))
                spread = jnp.where(group == 0, pltpu.roll(value, 32, 1), spread)
                modulus_s[plane, pl.ds(8 + 8 * t, 8), :] = jnp.where(group == 3, value, spread)
        return carry

    lax.fori_loop(0, 12, place, 0, unroll=2)

    def begin(i, carry):
        for plane in (2 + 2 * i, 3 + 2 * i):
            for t in range(3):
                here, margin = pl.ds(8 * t, 8), pl.ds(8 + 8 * t, 8)
                (mid, d, inv), (mid_s, d_s, inv_s), beside = side_diagonal(modulus, modulus_s, plane, 8 + 8 * t)
                for refs, values in zip(((prev, next), (prev_s, next_s)), beside):
                    for ref, value in zip(refs, values):
                        ref[plane, here, :] = value
                diag[plane, here, :] = d
                inverse[plane, here, :] = inv
                diag_s[plane, here, :] = d_s
                inverse_s[plane, here, :] = inv_s
                inv = inv * (1.0 / THETA)
                for c in range(3):
                    step = rest[c, plane, here, :] * inv
                    ua[c, plane, margin, :] = step
                    va[c, plane, margin, :] = mid * step
                step = rest_s[plane, here, :] * (inv_s * (1.0 / THETA))
                usa[plane, margin, :] = step
                vsa[plane, margin, :] = mid_s * step
        return carry

    lax.fori_loop(0, 10, begin, 0)

    def gather(steps, start):
        def body(p, carry):
            for c in range(3):
                step = steps[c, 8 + p, pl.ds(16, 8), :]
                smooth[c, p] = step if start else smooth[c, p] + step
            return carry

        lax.fori_loop(0, 8, body, 0, unroll=4)

    gather(ua, True)
    scales = sweep_scales()

    def reader(ref, margin):
        return lambda plane, row: ref[plane, pl.ds(margin + row, 8), :]

    moduli = [
        [reader(modulus, 8), reader(prev, 0), reader(next, 0)],
        [reader(modulus_s, 8), reader(prev_s, 0), reader(next_s, 0)],
    ]
    readers = [moduli] + [[reader(ref, 0) for ref in refs] for refs in ((diag, diag_s), (inverse, inverse_s))]
    for k in range(1, SWEEPS + 1):
        now, later = (ua, va, usa, vsa), (ub, vb, usb, vsb)
        if k % 2 == 0:
            now, later = later, now
        rows = (0, 8, 16) if k == 1 else (4, 12)
        sweep((2 + k, 22 - k), rows, now, later, (rest, rest_s), *readers, scales[k - 1] if k < SWEEPS else None)
        if k < SWEEPS:
            gather(later[0], False)

    def restrict(p, carry):
        def four(ref, at, margin):
            a, b = (ref[(*at, 4 + 2 * p + dx, pl.ds(margin + 4, 8, stride=2), slice(None))] for dx in range(2))
            c, d = (ref[(*at, 4 + 2 * p + dx, pl.ds(margin + 5, 8, stride=2), slice(None))] for dx in range(2))
            return (a + b) + (c + d)

        for c in range(3):
            pairs[c, p] = four(rest, (c,), 0)
        pairs[3, p] = 0.25 * four(modulus, (), 8)
        pairs_s[0, p] = four(rest_s, (), 0)
        pairs_s[1, p] = 0.25 * four(modulus_s, (), 8)
        return carry

    lax.fori_loop(0, 8, restrict, 0, unroll=2)
    coarse = exact_dot(pairs[...].reshape(256, 128), pair_matrix(None, 0)).reshape(4, 8, 8, 128)
    for c in range(4):
        source = pairs_s[1 if c == 3 else 0].reshape(64, 128)
        message[c] = coarse[c] + exact_dot(source, pair_matrix(c % 3, 0)).reshape(8, 8, 128)
    for i in range(6):
        ahead[pl.ds(8 * i, 8), :] = message[3, i]
        behind[pl.ds(8 * i, 8), :] = message[3, 2 + i]
    for f, source in enumerate([rest.at[c] for c in range(3)] + [rest_s]):
        ahead[pl.ds(LAYER_X + 12 * f, 12), :] = source[13, pl.ds(6, 12), :]
        behind[pl.ds(LAYER_X + 12 * f, 12), :] = source[10, pl.ds(6, 12), :]
        for p in range(12):
            layer_ahead[f, pl.ds(p, 1), :] = source[6 + p, pl.ds(13, 1), :]
            layer_behind[f, pl.ds(p, 1), :] = source[6 + p, pl.ds(10, 1), :]
    empty = jnp.zeros((6, 128), jnp.float32)
    ahead[pl.ds(LAYER_X + 48, 6), :] = empty
    behind[pl.ds(LAYER_X + 48, 6), :] = empty
    for c in range(3):
        for i in range(5):
            ahead[pl.ds(48 + 6 * (5 * c + i), 6), :] = message[c, 1 + i, pl.ds(1, 6), :]
            behind[pl.ds(48 + 6 * (5 * c + i), 6), :] = message[c, 2 + i, pl.ds(1, 6), :]

    kept = (
        (modulus, modulus_s, 12), (diag, diag_s, 4), (inverse, inverse_s, 4), (prev, prev_s, 4), (next, next_s, 4)
    )

    def keep_state(p, carry):
        for c in range(3):
            state[c, p] = rest[c, 4 + p, pl.ds(4, 16), :]
        side_state[0, p] = rest_s[4 + p, pl.ds(4, 16), :]
        for f, (ref, ref_s, row) in enumerate(kept):
            state[3 + f, p] = ref[4 + p, pl.ds(row, 16), :]
            side_state[1 + f, p] = ref_s[4 + p, pl.ds(row, 16), :]
        return carry

    lax.fori_loop(0, 16, keep_state, 0, unroll=2)


def post_kernel(
    own, right, left, up, down, state_in, side_in, smooth, correction, coarse,
    ca, cb, cva, cvb, crest, cmod, cinv, cdiag, cprev, cnext, total, ua, ub, va, vb, usa, usb, vsa, vsb, wide, wide_s, rest, rest_s,
):
    scales = sweep_scales()

    empty = jnp.zeros((16, 128), jnp.float32)
    for c in range(3):
        crest[c, 0] = empty
        crest[c, 15] = empty
    edge = jnp.zeros((1, 128), jnp.float32)
    for c, plane, source, index, row in coarse_planes(own, left, right):
        base, count, margin = coarse_rows(c, plane)
        mid = source[(*index, pl.ds(row + margin, 4), slice(None))]
        below, above = down[pl.ds(base, count), :], up[pl.ds(base, count), :]
        if c < 3:
            crest[c, plane, pl.ds(0, 1), :] = edge
            crest[c, plane, pl.ds(1, 5), :] = below
            crest[c, plane, pl.ds(6, 4), :] = mid
            crest[c, plane, pl.ds(10, 5), :] = above
            crest[c, plane, pl.ds(15, 1), :] = edge
        else:
            cmod[plane, pl.ds(8, 6), :] = below
            cmod[plane, pl.ds(14, 4), :] = mid
            cmod[plane, pl.ds(18, 6), :] = above

    def begin(i, carry):
        for plane in (1 + 2 * i, 2 + 2 * i):
            for t in range(2):
                here, margin = pl.ds(8 * t, 8), pl.ds(8 + 8 * t, 8)
                mid, d, inv = ring_diagonal(cmod, plane, 8 + 8 * t)
                cdiag[plane, here, :] = d
                cprev[plane, here, :] = pltpu.roll(mid, 1, 1)
                cnext[plane, here, :] = pltpu.roll(mid, 127, 1)
                cinv[plane, here, :] = inv
                inv = inv * (1.0 / THETA)
                for c in range(3):
                    step = crest[c, plane, here, :] * inv
                    ca[c, plane, margin, :] = step
                    cva[c, plane, margin, :] = mid * step
        return carry

    lax.fori_loop(0, 7, begin, 0)

    def gather(steps, start):
        def body(p, carry):
            for c in range(3):
                step = steps[c, 4 + p, pl.ds(12, 8), :]
                total[c, p] = step if start else total[c, p] + step
            return carry

        lax.fori_loop(0, 8, body, 0, unroll=4)

    gather(ca, True)

    def reader(ref, margin):
        return lambda plane, row: ref[plane, pl.ds(margin + row, 8), :]

    coarse_moduli = [[reader(cmod, 8), reader(cprev, 0), reader(cnext, 0)]]
    for k in range(1, SWEEPS):
        now, later = ((ca, cva), (cb, cvb)) if k % 2 else ((cb, cvb), (ca, cva))
        sweep((1 + k, 15 - k), (0, 8) if k < 3 else (4,), now, later, (crest,), coarse_moduli, [reader(cdiag, 0)], [reader(cinv, 0)], scales[k - 1])
        gather(later[0], False)

    for c in range(3):
        for p in range(4):
            coarse[c, p] = total[c, 2 + p, pl.ds(2, 4), pl.ds(0, 64)]

    wide[...] = exact_dot(total[...].reshape(192, 128), pair_matrix(None, 1)).reshape(3, 8, 8, 128)
    spread = None
    for c in range(3):
        part = exact_dot(total[c].reshape(64, 128), pair_matrix(c, 1))
        spread = part if spread is None else spread + part
    wide_s[...] = spread.reshape(8, 8, 128)

    def lift(p, carry):
        for dx in range(2):
            for dy in range(2):
                for c in range(3):
                    ua[c, 2 * p + dx, pl.ds(8 + dy, 8, stride=2), :] = wide[c, p]
                usa[2 * p + dx, pl.ds(8 + dy, 8, stride=2), :] = wide_s[p]
        return carry

    lax.fori_loop(0, 8, lift, 0, unroll=2)

    def weigh(p, carry):
        for c in range(3):
            va[c, p, pl.ds(8, 16), :] = state_in[3, p] * ua[c, p, pl.ds(8, 16), :]
            rest[c, p] = state_in[c, p]
        vsa[p, pl.ds(8, 16), :] = side_in[1, p] * usa[p, pl.ds(8, 16), :]
        rest_s[p] = side_in[0, p]
        return carry

    lax.fori_loop(0, 16, weigh, 0, unroll=2)
    for f, target in enumerate([rest.at[c] for c in range(3)] + [rest_s]):
        target[1, pl.ds(2, 12), :] = left[pl.ds(LAYER_X + 12 * f, 12), :]
        target[14, pl.ds(2, 12), :] = right[pl.ds(LAYER_X + 12 * f, 12), :]
        for p in range(14):
            target[1 + p, pl.ds(1, 1), :] = down[pl.ds(LAYER_Y + 14 * f + p, 1), :]
            target[1 + p, pl.ds(14, 1), :] = up[pl.ds(LAYER_Y + 14 * f + p, 1), :]

    def add_own(steps, start):
        def body(p, carry):
            for c in range(3):
                step = steps[c, 4 + p, pl.ds(12, 8), :]
                correction[c, p] = (smooth[c, p] if start else correction[c, p]) + step
            return carry

        lax.fori_loop(0, 8, body, 0, unroll=4)

    add_own(ua, True)

    def held(f):
        return [
            lambda plane, row: state_in[3 + f, plane, pl.ds(row, 8), :],
            lambda plane, row: side_in[1 + f, plane, pl.ds(row, 8), :],
        ]

    moduli = list(zip(held(0), held(3), held(4)))

    def emit(c, plane, step):
        correction[c, plane - 4] = correction[c, plane - 4] + step

    for k in range(SWEEPS):
        now, later = (ua, va, usa, vsa), (ub, vb, usb, vsb)
        if k % 2:
            now, later = later, now
        scale = scales[k - 1] if k else (None, 1.0 / THETA)
        last = k == SWEEPS - 1
        sweep(
            (1 + k, 15 - k), (4,) if last else (0, 8), now, later, (rest, rest_s), moduli, held(1), held(2), scale,
            emit if last else None,
        )
        if not last:
            add_own(later[0], False)


def call(kernel, outs, scratch=()):
    return pl.pallas_call(
        kernel,
        out_shape=[jax.ShapeDtypeStruct(s, jnp.float32) for s in outs],
        scratch_shapes=[pltpu.VMEM(s, jnp.float32) for s in scratch],
        compiler_params=pltpu.CompilerParams(vmem_limit_bytes=48 * 1024 * 1024),
    )


def neighbours(to_next, to_previous, axis):
    count = lax.axis_size(axis)
    after = lax.ppermute(to_previous, axis, [(i + 1, i) for i in range(count - 1)])
    before = lax.ppermute(to_next, axis, [(i, i + 1) for i in range(count - 1)])
    return before, after


SMOOTH_OUTS = [
    (3, 8, 8, 128),
    (4, 8, 8, 128),
    (COARSE_ROWS_X, 128),
    (COARSE_ROWS_X, 128),
    (4, 12, 128),
    (4, 12, 128),
    (8, 16, 16, 128),
    (6, 16, 16, 128),
]
SMOOTH_SCRATCH = [
    *[(3, 24, 40, 128)] * 4,
    *[(24, 40, 128)] * 4,
    (3, 24, 24, 128),
    (24, 40, 128),
    *[(24, 24, 128)] * 5,
    (24, 40, 128),
    *[(24, 24, 128)] * 4,
    (4, 8, 8, 128),
    (2, 8, 8, 128),
]
POST_OUTS = [(3, 8, 8, 128), (3, 4, 4, 64)]
POST_SCRATCH = [
    *[(3, 16, 32, 128)] * 4,
    (3, 16, 16, 128),
    (16, 32, 128),
    *[(16, 16, 128)] * 4,
    (3, 8, 8, 128),
    *[(3, 16, 32, 128)] * 4,
    *[(16, 32, 128)] * 4,
    (3, 8, 8, 128),
    (8, 8, 128),
    (3, 16, 16, 128),
    (16, 16, 128),
]


def on_device(levels, residual):
    ratio = levels.astype(jnp.float32) / 255.0
    modulus = (0.05 + 0.95 * ratio * ratio * ratio) / UNIT
    own = jnp.concatenate([residual, modulus[None]])
    ahead, behind = call(pack_planes, [(25, 8, 128), (25, 8, 128)])(own)
    left, right = neighbours(ahead, behind, "gx")
    ahead, behind = call(pack_rows, [(FINE_ROWS, 128)] * 2)(own, right, left)
    down, up = neighbours(ahead, behind, "gy")
    main, first, last = call(pack_lanes, [(4, 24, 24, 128), (12, 24, 128), (12, 24, 128)])(own, right, left, up, down)
    before, after = neighbours(last, first, "gz")
    smooth, own, ahead, behind, layer_ahead, layer_behind, state, side_state = call(
        smooth_kernel, SMOOTH_OUTS, SMOOTH_SCRATCH
    )(main, after, before)
    left, right = neighbours(ahead, behind, "gx")
    ahead, behind = call(pack_coarse, [(COARSE_ROWS_Y, 128)] * 2)(own, right, left, layer_ahead, layer_behind)
    down, up = neighbours(ahead, behind, "gy")
    correction, coarse = call(post_kernel, POST_OUTS, POST_SCRATCH)(own, right, left, up, down, state, side_state, smooth)
    return correction, coarse


def solution(mesh):
    return jax.shard_map(
        on_device,
        mesh=mesh,
        in_specs=(P("gx", "gy", "gz"), P(None, "gx", "gy", "gz")),
        out_specs=(P(None, "gx", "gy", "gz"), P(None, "gx", "gy", "gz")),
        check_vma=False,
    )
```

```python
import jax
import jax.numpy as jnp
from jax import lax
from jax.experimental import pallas as pl
from jax.experimental.pallas import tpu as pltpu
from jax.sharding import PartitionSpec as P

SWEEPS = 4
THETA = 1.15
DELTA = 0.85

FACE, SIDE, EDGE, FLAT, TURN, TWIST = 9.6, 6.0, 2.7, 1.8, 0.9, 0.4
UNIT = 120.0
WHOLE = 1.92
HALO = 16
SMOOTH_CHUNKS = (4, 3, 2, 1)
POST_CHUNKS = (4, 3, 5, 7, 2, 1)


def sweep_scales():
    sigma = THETA / DELTA
    rho = 1.0 / sigma
    scales = []
    for _ in range(SWEEPS - 1):
        rho_next = 1.0 / (2.0 * sigma - rho)
        scales.append((rho_next * rho, 2.0 * rho_next / DELTA))
        rho = rho_next
    return scales


def lane_index():
    return lax.broadcasted_iota(jnp.int32, (8, 128), 1)


def by_group(values):
    group = lane_index() // 32
    out = jnp.full((8, 128), values[-1], jnp.float32)
    for g in range(len(values) - 1):
        out = jnp.where(group == g, values[g], out)
    return out


def neighbourhood(load, count):
    mid, summed, spread = [], [], []
    for p in range(-1, count + 1):
        u, yp, ym = load(p, 0), load(p, 1), load(p, -1)
        mid.append(u)
        summed.append(yp + ym)
        spread.append(yp - ym)
    return mid, summed, spread


def stencil(field, plane, count, row):
    def loader(c):
        return lambda p, dy: field[c, plane + p, pl.ds(row + dy, 8), :]

    flat, even, odd = ([[None] * 3 for _ in range(count)] for _ in range(3))
    cross, along, across = [None] * count, [None] * count, [None] * count
    mid, summed, spread = neighbourhood(loader(0), count)
    for p in range(count):
        u, sy = mid[p + 1], summed[p + 1]
        sx, sxy = mid[p + 2] + mid[p], summed[p + 2] + summed[p]
        flat[p][0] = FACE * sx + SIDE * sy + EDGE * sxy
        even[p][0] = SIDE * u + EDGE * sx + FLAT * sy + sxy
        cross[p] = spread[p + 2] - spread[p]
        along[p], across[p] = mid[p + 2] - mid[p], summed[p + 2] - summed[p]
    mid, summed, spread = neighbourhood(loader(1), count)
    for p in range(count):
        u, sy = mid[p + 1], summed[p + 1]
        sx, sxy = mid[p + 2] + mid[p], summed[p + 2] + summed[p]
        flat[p][1] = FACE * sy + SIDE * sx + EDGE * sxy + TURN * cross[p]
        even[p][1] = SIDE * u + EDGE * sy + FLAT * sx + sxy + TWIST * cross[p]
        back = spread[p + 2] - spread[p]
        flat[p][0] = flat[p][0] + TURN * back
        even[p][0] = even[p][0] + TWIST * back
        odd[p][2] = TURN * (along[p] + spread[p + 1]) + TWIST * (across[p] + (spread[p + 2] + spread[p]))
    mid, summed, spread = neighbourhood(loader(2), count)
    for p in range(count):
        both, sxy = mid[p + 2] + mid[p] + summed[p + 1], summed[p + 2] + summed[p]
        flat[p][2] = SIDE * both + FLAT * sxy
        even[p][2] = FACE * mid[p + 1] + EDGE * both + sxy
        odd[p][0] = TURN * (mid[p + 2] - mid[p]) + TWIST * (summed[p + 2] - summed[p])
        odd[p][1] = TURN * spread[p + 1] + TWIST * (spread[p + 2] + spread[p])
    return [[(flat[p][c], even[p][c] + odd[p][c], even[p][c] - odd[p][c]) for c in range(3)] for p in range(count)]


def side_stencil(field, plane, count, row):
    mid, summed, spread = neighbourhood(lambda p, dy: field[plane + p, pl.ds(row + dy, 8), :], count)
    group = lane_index() // 32
    flat_x, flat_y = by_group((FACE, SIDE, SIDE)), by_group((SIDE, FACE, SIDE))
    flat_xy, even_u = by_group((EDGE, EDGE, FLAT)), by_group((SIDE, SIDE, FACE))
    even_x, even_y = by_group((EDGE, FLAT, EDGE)), by_group((FLAT, EDGE, EDGE))
    found = []
    for p in range(count):
        u, sy, dy = mid[p + 1], summed[p + 1], spread[p + 1]
        sx, dx = mid[p + 2] + mid[p], mid[p + 2] - mid[p]
        sxy, dx_sy = summed[p + 2] + summed[p], summed[p + 2] - summed[p]
        dy_sx, dxy = spread[p + 2] + spread[p], spread[p + 2] - spread[p]
        along_x, along_y = TURN * dx + TWIST * dx_sy, TURN * dy + TWIST * dy_sx
        down = pltpu.roll(jnp.where(group == 1, dxy, along_y), 96, 1)
        up = pltpu.roll(jnp.where(group == 0, dxy, along_y), 32, 1)
        far = pltpu.roll(along_x, 64, 1)
        cross = jnp.where(group == 0, down, jnp.where(group == 1, up, 0.0))
        flat = flat_x * sx + flat_y * sy + flat_xy * sxy + TURN * cross
        even = even_u * u + even_x * sx + even_y * sy + sxy + TWIST * cross
        odd = jnp.where(group == 0, far, jnp.where(group == 1, down, far + up))
        found.append((flat, even + odd, even - odd))
    return found


def join_ring(part):
    centre, above, below = part
    return centre + (pltpu.roll(above, 127, 1) + pltpu.roll(below, 1, 1))


def side_lanes():
    lane = lane_index()
    return lane, lane % 32 == HALO


def join_sides(parts, side):
    lane, begins = side_lanes()
    ends = jnp.where(begins, side[1], side[2])
    side_above, side_below = side[1], side[2]
    joined = []
    for c, (centre, above, below) in enumerate(parts):
        inward = pltpu.roll(ends, 112 - 32 * c, 1)
        outward = pltpu.roll(jnp.where(lane == 0, above, below), 32 * c + HALO, 1)
        up = pltpu.roll(jnp.where(lane == 0, inward, above), 127, 1)
        down = pltpu.roll(jnp.where(lane == 127, inward, below), 1, 1)
        joined.append(centre + (up + down))
        side_above = jnp.where(lane == 32 * c + HALO, outward, side_above)
        side_below = jnp.where(lane == 32 * c + HALO - 1, outward, side_below)
    return joined, side[0] + (pltpu.roll(side_above, 127, 1) + pltpu.roll(side_below, 1, 1))


def shifted(main, side):
    lane, begins = side_lanes()
    inward = pltpu.roll(side, 112, 1)
    side_below, side_above = side, side
    for g in range(3):
        outward = pltpu.roll(main, 32 * g + HALO, 1)
        side_above = jnp.where(lane == 32 * g + HALO, outward, side_above)
        side_below = jnp.where(lane == 32 * g + HALO - 1, outward, side_below)
    return (
        (pltpu.roll(jnp.where(lane == 127, inward, main), 1, 1), pltpu.roll(jnp.where(lane == 0, inward, main), 127, 1)),
        (pltpu.roll(side_below, 1, 1), pltpu.roll(side_above, 127, 1)),
    )


def weighted(modulus, plain, heavy):
    here, before, after = modulus
    return (here * plain[0] + heavy[0], before * plain[1] + heavy[1], after * plain[2] + heavy[2])


def coupling(now, modulus, plane, count, row):
    plain, heavy = (stencil(now[k], plane, count, row) for k in range(2))
    parts = [[weighted(modulus[p][0], *both) for both in zip(plain[p], heavy[p])] for p in range(count)]
    if len(now) == 2:
        return [([join_ring(part) for part in parts[p]], None) for p in range(count)]
    plain, heavy = (side_stencil(now[2 + k], plane, count, row) for k in range(2))
    return [join_sides(parts[p], weighted(modulus[p][1], plain[p], heavy[p])) for p in range(count)]


def sweep(chunks, planes, rows, now, later, rest, modulus, diag, inverse, scale, emit=None):
    lo, hi = planes
    chunk = next(n for n in chunks if (hi - lo) % n == 0)
    sides = len(rest) if not emit else 1

    def body(i, carry):
        first = lo + i * chunk
        for row in rows:
            mods = [[[read(first + j, row) for read in reads] for reads in modulus] for j in range(chunk)]
            out = coupling(now, mods, first, chunk, 8 + row)
            for j in range(chunk):
                plane = first + j
                for t in range(sides):
                    d = diag[t](plane, row)
                    if scale:
                        inv = inverse[t](plane, row) * scale[1]
                    for c in range(1 if t else 3):
                        at = (plane,) if t else (c, plane)
                        here, margin = (*at, pl.ds(row, 8), slice(None)), (*at, pl.ds(8 + row, 8), slice(None))
                        old = now[2 * t][margin]
                        r = rest[t][here] - d * old + (out[j][1] if t else out[j][0][c])
                        if not emit:
                            rest[t][here] = r
                        if scale:
                            step = inv * r
                            if scale[0]:
                                step = scale[0] * old + step
                            if emit:
                                emit(c, plane, step)
                            else:
                                later[2 * t][margin] = step
                                later[2 * t + 1][margin] = mods[j][t][0] * step
        return carry

    lax.fori_loop(0, (hi - lo) // chunk, body, 0)


def diagonal_parts(modulus, plane, row):
    def at(dx, dy):
        return modulus[plane + dx, pl.ds(row + dy, 8), :]

    u = at(0, 0)
    cross = (at(1, 0) + at(-1, 0)) + (at(0, 1) + at(0, -1))
    corner = (at(1, 1) + at(-1, -1)) + (at(1, -1) + at(-1, 1))
    even = 0.16 * u + 0.06 * cross + 0.03 * corner
    return u, (WHOLE * u + 0.16 * cross + 0.06 * corner, even, even)


def finish_diagonal(mid, total):
    diag = (1.05 * 0.5 * UNIT) * total
    inside = mid > 0.0
    return mid, diag, jnp.where(inside, 1.0 / jnp.where(inside, diag, 1.0), 0.0)


def ring_diagonal(modulus, plane, row):
    mid, part = diagonal_parts(modulus, plane, row)
    return finish_diagonal(mid, join_ring(part))


def side_diagonal(modulus, side_modulus, plane, row):
    mid, (centre, even, _) = diagonal_parts(modulus, plane, row)
    side_mid, (side_centre, side_even, _) = diagonal_parts(side_modulus, plane, row)
    (below, above), (side_below, side_above) = shifted(even, side_even)
    main = finish_diagonal(mid, centre + (below + above))
    side_mid, side_diag, side_inverse = finish_diagonal(side_mid, side_centre + (side_below + side_above))
    side_inverse = jnp.where(lane_index() < 96, side_inverse, 0.0)
    return main, (side_mid, side_diag, side_inverse), shifted(mid, side_mid)


def pair_matrix(group, fine_axis):
    fine = lax.broadcasted_iota(jnp.int32, (128, 128), fine_axis)
    coarse = lax.broadcasted_iota(jnp.int32, (128, 128), 1 - fine_axis)
    if group is None:
        return (lax.shift_right_logical(fine, 1) == coarse).astype(jnp.float32)
    inner = fine - 32 * group
    target = lax.shift_right_logical(fine, 1) - 16 * group + jnp.where(inner < HALO, 120, 56)
    return ((target == coarse) & (inner >= 0) & (inner < 32)).astype(jnp.float32)


def exact_dot(a, b):
    return jnp.dot(a, b, precision=lax.Precision.HIGHEST, preferred_element_type=jnp.float32)


def pack_planes(own, ahead, behind):
    for p in range(8):
        if p > 0:
            ahead[p - 1] = own[3, p]
        if p < 7:
            behind[p] = own[3, p]
        for c in range(3):
            if p > 1:
                ahead[7 + 6 * c + p - 2] = own[c, p]
            if p < 6:
                behind[7 + 6 * c + p] = own[c, p]


def fine_planes(own, left, right):
    found = []
    for plane in range(1, 23):
        if plane < 8:
            found.append((3, plane, left, (plane - 1,)))
        elif plane < 16:
            found.append((3, plane, own, (3, plane - 8)))
        else:
            found.append((3, plane, right, (plane - 16,)))
    for c in range(3):
        for plane in range(2, 22):
            if plane < 8:
                found.append((c, plane, left, (7 + 6 * c + plane - 2,)))
            elif plane < 16:
                found.append((c, plane, own, (c, plane - 8)))
            else:
                found.append((c, plane, right, (7 + 6 * c + plane - 16,)))
    return found


FINE_ROWS = 520


def fine_rows(c, plane):
    return (7 * (plane - 1), 7) if c == 3 else (154 + 6 * (20 * c + plane - 2), 6)


def pack_rows(own, right, left, ahead, behind):
    empty = jnp.zeros((8, 128), jnp.float32)
    ahead[pl.ds(FINE_ROWS - 8, 8), :] = empty
    behind[pl.ds(FINE_ROWS - 8, 8), :] = empty
    for c, plane, source, index in fine_planes(own, left, right):
        base, count = fine_rows(c, plane)
        ahead[pl.ds(base, count), :] = source[(*index, pl.ds(8 - count, count), slice(None))]
        behind[pl.ds(base, count), :] = source[(*index, pl.ds(0, count), slice(None))]


def pack_lanes(own, right, left, up, down, main, first, last):
    empty = jnp.zeros((24, 128), jnp.float32)
    for plane in (0, 1, 22, 23):
        for c in range(3):
            main[c, plane] = empty
    main[3, 0] = empty
    main[3, 23] = empty
    gap = jnp.zeros((2, 128), jnp.float32)
    for c, plane, source, index in fine_planes(own, left, right):
        base, count = fine_rows(c, plane)
        main[c, plane, pl.ds(0, 2), :] = gap
        main[c, plane, pl.ds(22, 2), :] = gap
        main[c, plane, pl.ds(8, 8), :] = source[index]
        main[c, plane, pl.ds(8 - count, count), :] = down[pl.ds(base, count), :]
        main[c, plane, pl.ds(16, count), :] = up[pl.ds(base, count), :]
    lane = lane_index()

    def pack(pair, carry):
        for t in range(3):
            head = jnp.zeros((8, 128), jnp.float32)
            tail = head
            for s in range(2):
                for c in range(4):
                    value, place = main[c, 2 * pair + s, pl.ds(8 * t, 8), :], 32 * c + HALO * s
                    mine = (lane >= place) & (lane < place + HALO)
                    head = jnp.where(mine, pltpu.roll(value, place, 1) if place else value, head)
                    turn = (place + HALO) % 128
                    tail = jnp.where(mine, pltpu.roll(value, turn, 1) if turn else value, tail)
            first[pair, pl.ds(8 * t, 8), :] = head
            last[pair, pl.ds(8 * t, 8), :] = tail
        return carry

    lax.fori_loop(0, 12, pack, 0, unroll=2)


LAYER_X = 6 * 8 + 3 * 5 * 6
LAYER_Y = 16 * 6 + 3 * 14 * 5
COARSE_ROWS_X = 192
COARSE_ROWS_Y = 368


def coarse_planes(own, left, right):
    found = []
    for i in range(16):
        if i < 6:
            found.append((3, i, left, (), 8 * i))
        elif i < 10:
            found.append((3, i, own, (3, i - 4), 0))
        else:
            found.append((3, i, right, (), 8 * (i - 10)))
    for c in range(3):
        for i in range(14):
            if i < 5:
                found.append((c, i + 1, left, (), 48 + 6 * (5 * c + i)))
            elif i < 9:
                found.append((c, i + 1, own, (c, i - 3), 1))
            else:
                found.append((c, i + 1, right, (), 48 + 6 * (5 * c + i - 9)))
    return found


def coarse_rows(c, plane):
    return (6 * plane, 6, 2) if c == 3 else (96 + 5 * (14 * c + plane - 1), 5, 1)


def pack_coarse(own, right, left, layer_ahead, layer_behind, ahead, behind):
    empty = jnp.zeros((8, 128), jnp.float32)
    for message, layer, offset in ((ahead, layer_ahead, 7), (behind, layer_behind, 4)):
        message[pl.ds(COARSE_ROWS_Y - 8, 8), :] = empty
        for f in range(4):
            base = LAYER_Y + 14 * f
            message[pl.ds(base, 1), :] = left[pl.ds(LAYER_X + 12 * f + offset, 1), :]
            message[pl.ds(base + 1, 12), :] = layer[f]
            message[pl.ds(base + 13, 1), :] = right[pl.ds(LAYER_X + 12 * f + offset, 1), :]
    for c, plane, source, index, row in coarse_planes(own, left, right):
        base, count, margin = coarse_rows(c, plane)
        ahead[pl.ds(base, count), :] = source[(*index, pl.ds(row, count), slice(None))]
        behind[pl.ds(base, count), :] = source[(*index, pl.ds(row + margin, count), slice(None))]


def smooth_kernel(
    main, after, before, smooth, message, ahead, behind, layer_ahead, layer_behind, state, side_state,
    ua, ub, va, vb, usa, usb, vsa, vsb, rest, modulus, diag, inverse, prev, next, rest_s, modulus_s, diag_s, inverse_s, prev_s, next_s, pairs, pairs_s,
):
    group = lane_index() // 32

    low = lane_index() % 32 < HALO

    def place(pair, carry):
        for s in range(2):
            plane = 2 * pair + s
            for t in range(3):
                here = pl.ds(8 * t, 8)
                for c in range(3):
                    rest[c, plane, here, :] = main[c, plane, here, :]
                modulus[plane, pl.ds(8 + 8 * t, 8), :] = main[3, plane, here, :]
                lower, upper = before[pair, here, :], after[pair, here, :]
                if s:
                    lower = pltpu.roll(lower, 128 - HALO, 1)
                else:
                    upper = pltpu.roll(upper, HALO, 1)
                value = jnp.where(low, lower, upper)
                rest_s[plane, here, :] = value
                spread = jnp.where(group == 1, pltpu.roll(value, 64, 1), pltpu.roll(value, 96, 1))
                spread = jnp.where(group == 0, pltpu.roll(value, 32, 1), spread)
                modulus_s[plane, pl.ds(8 + 8 * t, 8), :] = jnp.where(group == 3, value, spread)
        return carry

    lax.fori_loop(0, 12, place, 0, unroll=2)

    def begin(i, carry):
        for plane in (2 + 2 * i, 3 + 2 * i):
            for t in range(3):
                here, margin = pl.ds(8 * t, 8), pl.ds(8 + 8 * t, 8)
                (mid, d, inv), (mid_s, d_s, inv_s), beside = side_diagonal(modulus, modulus_s, plane, 8 + 8 * t)
                for refs, values in zip(((prev, next), (prev_s, next_s)), beside):
                    for ref, value in zip(refs, values):
                        ref[plane, here, :] = value
                diag[plane, here, :] = d
                inverse[plane, here, :] = inv
                diag_s[plane, here, :] = d_s
                inverse_s[plane, here, :] = inv_s
                inv = inv * (1.0 / THETA)
                for c in range(3):
                    step = rest[c, plane, here, :] * inv
                    ua[c, plane, margin, :] = step
                    va[c, plane, margin, :] = mid * step
                step = rest_s[plane, here, :] * (inv_s * (1.0 / THETA))
                usa[plane, margin, :] = step
                vsa[plane, margin, :] = mid_s * step
        return carry

    lax.fori_loop(0, 10, begin, 0)

    def gather(steps, start):
        def body(p, carry):
            for c in range(3):
                step = steps[c, 8 + p, pl.ds(16, 8), :]
                smooth[c, p] = step if start else smooth[c, p] + step
            return carry

        lax.fori_loop(0, 8, body, 0, unroll=4)

    gather(ua, True)
    scales = sweep_scales()

    def reader(ref, margin):
        return lambda plane, row: ref[plane, pl.ds(margin + row, 8), :]

    moduli = [
        [reader(modulus, 8), reader(prev, 0), reader(next, 0)],
        [reader(modulus_s, 8), reader(prev_s, 0), reader(next_s, 0)],
    ]
    readers = [moduli] + [[reader(ref, 0) for ref in refs] for refs in ((diag, diag_s), (inverse, inverse_s))]
    for k in range(1, SWEEPS + 1):
        now, later = (ua, va, usa, vsa), (ub, vb, usb, vsb)
        if k % 2 == 0:
            now, later = later, now
        rows = (0, 8, 16) if k == 1 else (4, 12)
        sweep(SMOOTH_CHUNKS, (2 + k, 22 - k), rows, now, later, (rest, rest_s), *readers, scales[k - 1] if k < SWEEPS else None)
        if k < SWEEPS:
            gather(later[0], False)

    def restrict(p, carry):
        def four(ref, at, margin):
            a, b = (ref[(*at, 4 + 2 * p + dx, pl.ds(margin + 4, 8, stride=2), slice(None))] for dx in range(2))
            c, d = (ref[(*at, 4 + 2 * p + dx, pl.ds(margin + 5, 8, stride=2), slice(None))] for dx in range(2))
            return (a + b) + (c + d)

        for c in range(3):
            pairs[c, p] = four(rest, (c,), 0)
        pairs[3, p] = 0.25 * four(modulus, (), 8)
        pairs_s[0, p] = four(rest_s, (), 0)
        pairs_s[1, p] = 0.25 * four(modulus_s, (), 8)
        return carry

    lax.fori_loop(0, 8, restrict, 0, unroll=2)
    coarse = exact_dot(pairs[...].reshape(256, 128), pair_matrix(None, 0)).reshape(4, 8, 8, 128)
    for c in range(4):
        source = pairs_s[1 if c == 3 else 0].reshape(64, 128)
        message[c] = coarse[c] + exact_dot(source, pair_matrix(c % 3, 0)).reshape(8, 8, 128)
    for i in range(6):
        ahead[pl.ds(8 * i, 8), :] = message[3, i]
        behind[pl.ds(8 * i, 8), :] = message[3, 2 + i]
    for f, source in enumerate([rest.at[c] for c in range(3)] + [rest_s]):
        ahead[pl.ds(LAYER_X + 12 * f, 12), :] = source[13, pl.ds(6, 12), :]
        behind[pl.ds(LAYER_X + 12 * f, 12), :] = source[10, pl.ds(6, 12), :]
        for p in range(12):
            layer_ahead[f, pl.ds(p, 1), :] = source[6 + p, pl.ds(13, 1), :]
            layer_behind[f, pl.ds(p, 1), :] = source[6 + p, pl.ds(10, 1), :]
    empty = jnp.zeros((6, 128), jnp.float32)
    ahead[pl.ds(LAYER_X + 48, 6), :] = empty
    behind[pl.ds(LAYER_X + 48, 6), :] = empty
    for c in range(3):
        for i in range(5):
            ahead[pl.ds(48 + 6 * (5 * c + i), 6), :] = message[c, 1 + i, pl.ds(1, 6), :]
            behind[pl.ds(48 + 6 * (5 * c + i), 6), :] = message[c, 2 + i, pl.ds(1, 6), :]

    kept = (
        (modulus, modulus_s, 12), (diag, diag_s, 4), (inverse, inverse_s, 4), (prev, prev_s, 4), (next, next_s, 4)
    )

    def keep_state(p, carry):
        for c in range(3):
            state[c, p] = rest[c, 4 + p, pl.ds(4, 16), :]
        side_state[0, p] = rest_s[4 + p, pl.ds(4, 16), :]
        for f, (ref, ref_s, row) in enumerate(kept):
            state[3 + f, p] = ref[4 + p, pl.ds(row, 16), :]
            side_state[1 + f, p] = ref_s[4 + p, pl.ds(row, 16), :]
        return carry

    lax.fori_loop(0, 16, keep_state, 0, unroll=2)


def post_kernel(
    own, right, left, up, down, state_in, side_in, smooth, correction, coarse,
    ca, cb, cva, cvb, crest, cmod, cinv, cdiag, cprev, cnext, total, ua, ub, va, vb, usa, usb, vsa, vsb, wide, wide_s, rest, rest_s,
):
    scales = sweep_scales()

    empty = jnp.zeros((16, 128), jnp.float32)
    for c in range(3):
        crest[c, 0] = empty
        crest[c, 15] = empty
    edge = jnp.zeros((1, 128), jnp.float32)
    for c, plane, source, index, row in coarse_planes(own, left, right):
        base, count, margin = coarse_rows(c, plane)
        mid = source[(*index, pl.ds(row + margin, 4), slice(None))]
        below, above = down[pl.ds(base, count), :], up[pl.ds(base, count), :]
        if c < 3:
            crest[c, plane, pl.ds(0, 1), :] = edge
            crest[c, plane, pl.ds(1, 5), :] = below
            crest[c, plane, pl.ds(6, 4), :] = mid
            crest[c, plane, pl.ds(10, 5), :] = above
            crest[c, plane, pl.ds(15, 1), :] = edge
        else:
            cmod[plane, pl.ds(8, 6), :] = below
            cmod[plane, pl.ds(14, 4), :] = mid
            cmod[plane, pl.ds(18, 6), :] = above

    def begin(i, carry):
        for plane in [1 + 7 * i + j for j in range(7)]:
            for t in range(2):
                here, margin = pl.ds(8 * t, 8), pl.ds(8 + 8 * t, 8)
                mid, d, inv = ring_diagonal(cmod, plane, 8 + 8 * t)
                cdiag[plane, here, :] = d
                cprev[plane, here, :] = pltpu.roll(mid, 1, 1)
                cnext[plane, here, :] = pltpu.roll(mid, 127, 1)
                cinv[plane, here, :] = inv
                inv = inv * (1.0 / THETA)
                for c in range(3):
                    step = crest[c, plane, here, :] * inv
                    ca[c, plane, margin, :] = step
                    cva[c, plane, margin, :] = mid * step
        return carry

    lax.fori_loop(0, 2, begin, 0)

    def gather(steps, start):
        def body(p, carry):
            for c in range(3):
                step = steps[c, 4 + p, pl.ds(12, 8), :]
                total[c, p] = step if start else total[c, p] + step
            return carry

        lax.fori_loop(0, 8, body, 0, unroll=4)

    gather(ca, True)

    def reader(ref, margin):
        return lambda plane, row: ref[plane, pl.ds(margin + row, 8), :]

    coarse_moduli = [[reader(cmod, 8), reader(cprev, 0), reader(cnext, 0)]]
    for k in range(1, SWEEPS):
        now, later = ((ca, cva), (cb, cvb)) if k % 2 else ((cb, cvb), (ca, cva))
        sweep(POST_CHUNKS, (1 + k, 15 - k), (0, 8) if k < 3 else (4,), now, later, (crest,), coarse_moduli, [reader(cdiag, 0)], [reader(cinv, 0)], scales[k - 1])
        gather(later[0], False)

    for c in range(3):
        for p in range(4):
            coarse[c, p] = total[c, 2 + p, pl.ds(2, 4), pl.ds(0, 64)]

    wide[...] = exact_dot(total[...].reshape(192, 128), pair_matrix(None, 1)).reshape(3, 8, 8, 128)
    spread = None
    for c in range(3):
        part = exact_dot(total[c].reshape(64, 128), pair_matrix(c, 1))
        spread = part if spread is None else spread + part
    wide_s[...] = spread.reshape(8, 8, 128)

    def lift(p, carry):
        for dx in range(2):
            for dy in range(2):
                for c in range(3):
                    ua[c, 2 * p + dx, pl.ds(8 + dy, 8, stride=2), :] = wide[c, p]
                usa[2 * p + dx, pl.ds(8 + dy, 8, stride=2), :] = wide_s[p]
        return carry

    lax.fori_loop(0, 8, lift, 0, unroll=2)

    def weigh(p, carry):
        for c in range(3):
            va[c, p, pl.ds(8, 16), :] = state_in[3, p] * ua[c, p, pl.ds(8, 16), :]
            rest[c, p] = state_in[c, p]
        vsa[p, pl.ds(8, 16), :] = side_in[1, p] * usa[p, pl.ds(8, 16), :]
        rest_s[p] = side_in[0, p]
        return carry

    lax.fori_loop(0, 16, weigh, 0, unroll=2)
    for f, target in enumerate([rest.at[c] for c in range(3)] + [rest_s]):
        target[1, pl.ds(2, 12), :] = left[pl.ds(LAYER_X + 12 * f, 12), :]
        target[14, pl.ds(2, 12), :] = right[pl.ds(LAYER_X + 12 * f, 12), :]
        for p in range(14):
            target[1 + p, pl.ds(1, 1), :] = down[pl.ds(LAYER_Y + 14 * f + p, 1), :]
            target[1 + p, pl.ds(14, 1), :] = up[pl.ds(LAYER_Y + 14 * f + p, 1), :]

    def add_own(steps, start):
        def body(p, carry):
            for c in range(3):
                step = steps[c, 4 + p, pl.ds(12, 8), :]
                correction[c, p] = (smooth[c, p] if start else correction[c, p]) + step
            return carry

        lax.fori_loop(0, 8, body, 0, unroll=4)

    add_own(ua, True)

    def held(f):
        return [
            lambda plane, row: state_in[3 + f, plane, pl.ds(row, 8), :],
            lambda plane, row: side_in[1 + f, plane, pl.ds(row, 8), :],
        ]

    moduli = list(zip(held(0), held(3), held(4)))

    def emit(c, plane, step):
        correction[c, plane - 4] = correction[c, plane - 4] + step

    for k in range(SWEEPS):
        now, later = (ua, va, usa, vsa), (ub, vb, usb, vsb)
        if k % 2:
            now, later = later, now
        scale = scales[k - 1] if k else (None, 1.0 / THETA)
        last = k == SWEEPS - 1
        sweep(
            POST_CHUNKS, (1 + k, 15 - k), (4,) if last else (0, 8), now, later, (rest, rest_s), moduli, held(1), held(2), scale,
            emit if last else None,
        )
        if not last:
            add_own(later[0], False)


def call(kernel, outs, scratch=()):
    return pl.pallas_call(
        kernel,
        out_shape=[jax.ShapeDtypeStruct(s, jnp.float32) for s in outs],
        scratch_shapes=[pltpu.VMEM(s, jnp.float32) for s in scratch],
        compiler_params=pltpu.CompilerParams(vmem_limit_bytes=48 * 1024 * 1024),
    )


def neighbours(to_next, to_previous, axis):
    count = lax.axis_size(axis)
    after = lax.ppermute(to_previous, axis, [(i + 1, i) for i in range(count - 1)])
    before = lax.ppermute(to_next, axis, [(i, i + 1) for i in range(count - 1)])
    return before, after


SMOOTH_OUTS = [
    (3, 8, 8, 128),
    (4, 8, 8, 128),
    (COARSE_ROWS_X, 128),
    (COARSE_ROWS_X, 128),
    (4, 12, 128),
    (4, 12, 128),
    (8, 16, 16, 128),
    (6, 16, 16, 128),
]
SMOOTH_SCRATCH = [
    *[(3, 24, 40, 128)] * 4,
    *[(24, 40, 128)] * 4,
    (3, 24, 24, 128),
    (24, 40, 128),
    *[(24, 24, 128)] * 5,
    (24, 40, 128),
    *[(24, 24, 128)] * 4,
    (4, 8, 8, 128),
    (2, 8, 8, 128),
]
POST_OUTS = [(3, 8, 8, 128), (3, 4, 4, 64)]
POST_SCRATCH = [
    *[(3, 16, 32, 128)] * 4,
    (3, 16, 16, 128),
    (16, 32, 128),
    *[(16, 16, 128)] * 4,
    (3, 8, 8, 128),
    *[(3, 16, 32, 128)] * 4,
    *[(16, 32, 128)] * 4,
    (3, 8, 8, 128),
    (8, 8, 128),
    (3, 16, 16, 128),
    (16, 16, 128),
]


def on_device(levels, residual):
    ratio = levels.astype(jnp.float32) / 255.0
    modulus = (0.05 + 0.95 * ratio * ratio * ratio) / UNIT
    own = jnp.concatenate([residual, modulus[None]])
    ahead, behind = call(pack_planes, [(25, 8, 128), (25, 8, 128)])(own)
    left, right = neighbours(ahead, behind, "gx")
    ahead, behind = call(pack_rows, [(FINE_ROWS, 128)] * 2)(own, right, left)
    down, up = neighbours(ahead, behind, "gy")
    main, first, last = call(pack_lanes, [(4, 24, 24, 128), (12, 24, 128), (12, 24, 128)])(own, right, left, up, down)
    before, after = neighbours(last, first, "gz")
    smooth, own, ahead, behind, layer_ahead, layer_behind, state, side_state = call(
        smooth_kernel, SMOOTH_OUTS, SMOOTH_SCRATCH
    )(main, after, before)
    left, right = neighbours(ahead, behind, "gx")
    ahead, behind = call(pack_coarse, [(COARSE_ROWS_Y, 128)] * 2)(own, right, left, layer_ahead, layer_behind)
    down, up = neighbours(ahead, behind, "gy")
    correction, coarse = call(post_kernel, POST_OUTS, POST_SCRATCH)(own, right, left, up, down, state, side_state, smooth)
    return correction, coarse


def solution(mesh):
    return jax.shard_map(
        on_device,
        mesh=mesh,
        in_specs=(P("gx", "gy", "gz"), P(None, "gx", "gy", "gz")),
        out_specs=(P(None, "gx", "gy", "gz"), P(None, "gx", "gy", "gz")),
        check_vma=False,
    )
```

```python
import jax
import jax.numpy as jnp
from jax import lax
from jax.experimental import pallas as pl
from jax.experimental.pallas import tpu as pltpu
from jax.sharding import PartitionSpec as P

SWEEPS = 4
THETA = 1.15
DELTA = 0.85

FACE, SIDE, EDGE, FLAT, TURN, TWIST = 9.6, 6.0, 2.7, 1.8, 0.9, 0.4
UNIT = 120.0
WHOLE = 1.92
HALO = 16
SMOOTH_CHUNKS = (4, 3, 2, 1)
POST_CHUNKS = (4, 3, 5, 7, 2, 1)


def sweep_scales():
    sigma = THETA / DELTA
    rho = 1.0 / sigma
    scales = []
    for _ in range(SWEEPS - 1):
        rho_next = 1.0 / (2.0 * sigma - rho)
        scales.append((rho_next * rho, 2.0 * rho_next / DELTA))
        rho = rho_next
    return scales


def lane_index():
    return lax.broadcasted_iota(jnp.int32, (8, 128), 1)


def by_group(values):
    group = lane_index() // 32
    out = jnp.full((8, 128), values[-1], jnp.float32)
    for g in range(len(values) - 1):
        out = jnp.where(group == g, values[g], out)
    return out


def neighbourhood(load, count):
    mid, summed, spread = [], [], []
    for p in range(-1, count + 1):
        u, yp, ym = load(p, 0), load(p, 1), load(p, -1)
        mid.append(u)
        summed.append(yp + ym)
        spread.append(yp - ym)
    return mid, summed, spread


def stencil(field, plane, count, row):
    def loader(c):
        return lambda p, dy: field[c, plane + p, pl.ds(row + dy, 8), :]

    flat, even, odd = ([[None] * 3 for _ in range(count)] for _ in range(3))
    cross, along, across = [None] * count, [None] * count, [None] * count
    mid, summed, spread = neighbourhood(loader(0), count)
    for p in range(count):
        u, sy = mid[p + 1], summed[p + 1]
        sx, sxy = mid[p + 2] + mid[p], summed[p + 2] + summed[p]
        flat[p][0] = FACE * sx + SIDE * sy + EDGE * sxy
        even[p][0] = SIDE * u + EDGE * sx + FLAT * sy + sxy
        cross[p] = spread[p + 2] - spread[p]
        along[p], across[p] = mid[p + 2] - mid[p], summed[p + 2] - summed[p]
    mid, summed, spread = neighbourhood(loader(1), count)
    for p in range(count):
        u, sy = mid[p + 1], summed[p + 1]
        sx, sxy = mid[p + 2] + mid[p], summed[p + 2] + summed[p]
        flat[p][1] = FACE * sy + SIDE * sx + EDGE * sxy + TURN * cross[p]
        even[p][1] = SIDE * u + EDGE * sy + FLAT * sx + sxy + TWIST * cross[p]
        back = spread[p + 2] - spread[p]
        flat[p][0] = flat[p][0] + TURN * back
        even[p][0] = even[p][0] + TWIST * back
        odd[p][2] = TURN * (along[p] + spread[p + 1]) + TWIST * (across[p] + (spread[p + 2] + spread[p]))
    mid, summed, spread = neighbourhood(loader(2), count)
    for p in range(count):
        both, sxy = mid[p + 2] + mid[p] + summed[p + 1], summed[p + 2] + summed[p]
        flat[p][2] = SIDE * both + FLAT * sxy
        even[p][2] = FACE * mid[p + 1] + EDGE * both + sxy
        odd[p][0] = TURN * (mid[p + 2] - mid[p]) + TWIST * (summed[p + 2] - summed[p])
        odd[p][1] = TURN * spread[p + 1] + TWIST * (spread[p + 2] + spread[p])
    return [[(flat[p][c], even[p][c] + odd[p][c], even[p][c] - odd[p][c]) for c in range(3)] for p in range(count)]


def side_stencil(field, plane, count, row):
    mid, summed, spread = neighbourhood(lambda p, dy: field[plane + p, pl.ds(row + dy, 8), :], count)
    group = lane_index() // 32
    flat_x, flat_y = by_group((FACE, SIDE, SIDE)), by_group((SIDE, FACE, SIDE))
    flat_xy, even_u = by_group((EDGE, EDGE, FLAT)), by_group((SIDE, SIDE, FACE))
    even_x, even_y = by_group((EDGE, FLAT, EDGE)), by_group((FLAT, EDGE, EDGE))
    found = []
    for p in range(count):
        u, sy, dy = mid[p + 1], summed[p + 1], spread[p + 1]
        sx, dx = mid[p + 2] + mid[p], mid[p + 2] - mid[p]
        sxy, dx_sy = summed[p + 2] + summed[p], summed[p + 2] - summed[p]
        dy_sx, dxy = spread[p + 2] + spread[p], spread[p + 2] - spread[p]
        along_x, along_y = TURN * dx + TWIST * dx_sy, TURN * dy + TWIST * dy_sx
        down = pltpu.roll(jnp.where(group == 1, dxy, along_y), 96, 1)
        up = pltpu.roll(jnp.where(group == 0, dxy, along_y), 32, 1)
        far = pltpu.roll(along_x, 64, 1)
        cross = jnp.where(group == 0, down, jnp.where(group == 1, up, 0.0))
        flat = flat_x * sx + flat_y * sy + flat_xy * sxy + TURN * cross
        even = even_u * u + even_x * sx + even_y * sy + sxy + TWIST * cross
        odd = jnp.where(group == 0, far, jnp.where(group == 1, down, far + up))
        found.append((flat, even + odd, even - odd))
    return found


def join_ring(part):
    centre, above, below = part
    return centre + (pltpu.roll(above, 127, 1) + pltpu.roll(below, 1, 1))


def side_lanes():
    lane = lane_index()
    return lane, lane % 32 == HALO


def join_sides(parts, side):
    lane, begins = side_lanes()
    ends = jnp.where(begins, side[1], side[2])
    side_above, side_below = side[1], side[2]
    joined = []
    for c, (centre, above, below) in enumerate(parts):
        inward = pltpu.roll(ends, 112 - 32 * c, 1)
        outward = pltpu.roll(jnp.where(lane == 0, above, below), 32 * c + HALO, 1)
        up = pltpu.roll(jnp.where(lane == 0, inward, above), 127, 1)
        down = pltpu.roll(jnp.where(lane == 127, inward, below), 1, 1)
        joined.append(centre + (up + down))
        side_above = jnp.where(lane == 32 * c + HALO, outward, side_above)
        side_below = jnp.where(lane == 32 * c + HALO - 1, outward, side_below)
    return joined, side[0] + (pltpu.roll(side_above, 127, 1) + pltpu.roll(side_below, 1, 1))


def shifted(main, side):
    lane, begins = side_lanes()
    inward = pltpu.roll(side, 112, 1)
    side_below, side_above = side, side
    for g in range(3):
        outward = pltpu.roll(main, 32 * g + HALO, 1)
        side_above = jnp.where(lane == 32 * g + HALO, outward, side_above)
        side_below = jnp.where(lane == 32 * g + HALO - 1, outward, side_below)
    return (
        (pltpu.roll(jnp.where(lane == 127, inward, main), 1, 1), pltpu.roll(jnp.where(lane == 0, inward, main), 127, 1)),
        (pltpu.roll(side_below, 1, 1), pltpu.roll(side_above, 127, 1)),
    )


def weighted(modulus, plain, heavy):
    here, before, after = modulus
    return (here * plain[0] + heavy[0], before * plain[1] + heavy[1], after * plain[2] + heavy[2])


def coupling(now, modulus, plane, count, row):
    plain, heavy = (stencil(now[k], plane, count, row) for k in range(2))
    parts = [[weighted(modulus[p][0], *both) for both in zip(plain[p], heavy[p])] for p in range(count)]
    if len(now) == 2:
        return [([join_ring(part) for part in parts[p]], None) for p in range(count)]
    plain, heavy = (side_stencil(now[2 + k], plane, count, row) for k in range(2))
    return [join_sides(parts[p], weighted(modulus[p][1], plain[p], heavy[p])) for p in range(count)]


def sweep(chunks, planes, rows, now, later, rest, modulus, diag, inverse, scale, emit=None):
    lo, hi = planes
    chunk = next(n for n in chunks if (hi - lo) % n == 0)
    sides = len(rest) if not emit else 1

    def body(i, carry):
        first = lo + i * chunk
        for row in rows:
            mods = [[[read(first + j, row) for read in reads] for reads in modulus] for j in range(chunk)]
            out = coupling(now, mods, first, chunk, 8 + row)
            for j in range(chunk):
                plane = first + j
                for t in range(sides):
                    d = diag[t](plane, row)
                    if scale:
                        inv = inverse[t](plane, row) * scale[1]
                    for c in range(1 if t else 3):
                        at = (plane,) if t else (c, plane)
                        here, margin = (*at, pl.ds(row, 8), slice(None)), (*at, pl.ds(8 + row, 8), slice(None))
                        old = now[2 * t][margin]
                        r = rest[t][here] - d * old + (out[j][1] if t else out[j][0][c])
                        if not emit:
                            rest[t][here] = r
                        if scale:
                            step = inv * r
                            if scale[0]:
                                step = scale[0] * old + step
                            if emit:
                                emit(c, plane, step)
                            else:
                                later[2 * t][margin] = step
                                later[2 * t + 1][margin] = mods[j][t][0] * step
        return carry

    lax.fori_loop(0, (hi - lo) // chunk, body, 0)


def diagonal_parts(modulus, plane, row):
    def at(dx, dy):
        return modulus[plane + dx, pl.ds(row + dy, 8), :]

    u = at(0, 0)
    cross = (at(1, 0) + at(-1, 0)) + (at(0, 1) + at(0, -1))
    corner = (at(1, 1) + at(-1, -1)) + (at(1, -1) + at(-1, 1))
    even = 0.16 * u + 0.06 * cross + 0.03 * corner
    return u, (WHOLE * u + 0.16 * cross + 0.06 * corner, even, even)


def finish_diagonal(mid, total):
    diag = (1.05 * 0.5 * UNIT) * total
    inside = mid > 0.0
    return mid, diag, jnp.where(inside, 1.0 / jnp.where(inside, diag, 1.0), 0.0)


def ring_diagonal(modulus, plane, row):
    mid, part = diagonal_parts(modulus, plane, row)
    return finish_diagonal(mid, join_ring(part))


def side_diagonal(modulus, side_modulus, plane, row):
    mid, (centre, even, _) = diagonal_parts(modulus, plane, row)
    side_mid, (side_centre, side_even, _) = diagonal_parts(side_modulus, plane, row)
    (below, above), (side_below, side_above) = shifted(even, side_even)
    main = finish_diagonal(mid, centre + (below + above))
    side_mid, side_diag, side_inverse = finish_diagonal(side_mid, side_centre + (side_below + side_above))
    side_inverse = jnp.where(lane_index() < 96, side_inverse, 0.0)
    return main, (side_mid, side_diag, side_inverse), shifted(mid, side_mid)


def pair_matrix(group, fine_axis):
    fine = lax.broadcasted_iota(jnp.int32, (128, 128), fine_axis)
    coarse = lax.broadcasted_iota(jnp.int32, (128, 128), 1 - fine_axis)
    if group is None:
        return (lax.shift_right_logical(fine, 1) == coarse).astype(jnp.float32)
    inner = fine - 32 * group
    target = lax.shift_right_logical(fine, 1) - 16 * group + jnp.where(inner < HALO, 120, 56)
    return ((target == coarse) & (inner >= 0) & (inner < 32)).astype(jnp.float32)


def exact_dot(a, b):
    return jnp.dot(a, b, precision=lax.Precision.HIGHEST, preferred_element_type=jnp.float32)


def pack_planes(own, ahead, behind):
    for p in range(8):
        if p > 0:
            ahead[p - 1] = own[3, p]
        if p < 7:
            behind[p] = own[3, p]
        for c in range(3):
            if p > 1:
                ahead[7 + 6 * c + p - 2] = own[c, p]
            if p < 6:
                behind[7 + 6 * c + p] = own[c, p]


def fine_planes(own, left, right):
    found = []
    for plane in range(1, 23):
        if plane < 8:
            found.append((3, plane, left, (plane - 1,)))
        elif plane < 16:
            found.append((3, plane, own, (3, plane - 8)))
        else:
            found.append((3, plane, right, (plane - 16,)))
    for c in range(3):
        for plane in range(2, 22):
            if plane < 8:
                found.append((c, plane, left, (7 + 6 * c + plane - 2,)))
            elif plane < 16:
                found.append((c, plane, own, (c, plane - 8)))
            else:
                found.append((c, plane, right, (7 + 6 * c + plane - 16,)))
    return found


FINE_ROWS = 520


def fine_rows(c, plane):
    return (7 * (plane - 1), 7) if c == 3 else (154 + 6 * (20 * c + plane - 2), 6)


def pack_rows(own, right, left, ahead, behind):
    empty = jnp.zeros((8, 128), jnp.float32)
    ahead[pl.ds(FINE_ROWS - 8, 8), :] = empty
    behind[pl.ds(FINE_ROWS - 8, 8), :] = empty
    for c, plane, source, index in fine_planes(own, left, right):
        base, count = fine_rows(c, plane)
        ahead[pl.ds(base, count), :] = source[(*index, pl.ds(8 - count, count), slice(None))]
        behind[pl.ds(base, count), :] = source[(*index, pl.ds(0, count), slice(None))]


def pack_lanes(own, right, left, up, down, main, first, last):
    empty = jnp.zeros((24, 128), jnp.float32)
    for plane in (0, 1, 22, 23):
        for c in range(3):
            main[c, plane] = empty
    main[3, 0] = empty
    main[3, 23] = empty
    gap = jnp.zeros((2, 128), jnp.float32)
    for c, plane, source, index in fine_planes(own, left, right):
        base, count = fine_rows(c, plane)
        main[c, plane, pl.ds(0, 2), :] = gap
        main[c, plane, pl.ds(22, 2), :] = gap
        main[c, plane, pl.ds(8, 8), :] = source[index]
        main[c, plane, pl.ds(8 - count, count), :] = down[pl.ds(base, count), :]
        main[c, plane, pl.ds(16, count), :] = up[pl.ds(base, count), :]
    lane = lane_index()

    def pack(pair, carry):
        for t in range(3):
            head = jnp.zeros((8, 128), jnp.float32)
            tail = head
            for s in range(2):
                for c in range(4):
                    value, place = main[c, 2 * pair + s, pl.ds(8 * t, 8), :], 32 * c + HALO * s
                    mine = (lane >= place) & (lane < place + HALO)
                    head = jnp.where(mine, pltpu.roll(value, place, 1) if place else value, head)
                    turn = (place + HALO) % 128
                    tail = jnp.where(mine, pltpu.roll(value, turn, 1) if turn else value, tail)
            first[pair, pl.ds(8 * t, 8), :] = head
            last[pair, pl.ds(8 * t, 8), :] = tail
        return carry

    lax.fori_loop(0, 12, pack, 0, unroll=4)


LAYER_X = 6 * 8 + 3 * 5 * 6
LAYER_Y = 16 * 6 + 3 * 14 * 5
COARSE_ROWS_X = 192
COARSE_ROWS_Y = 368


def coarse_planes(own, left, right):
    found = []
    for i in range(16):
        if i < 6:
            found.append((3, i, left, (), 8 * i))
        elif i < 10:
            found.append((3, i, own, (3, i - 4), 0))
        else:
            found.append((3, i, right, (), 8 * (i - 10)))
    for c in range(3):
        for i in range(14):
            if i < 5:
                found.append((c, i + 1, left, (), 48 + 6 * (5 * c + i)))
            elif i < 9:
                found.append((c, i + 1, own, (c, i - 3), 1))
            else:
                found.append((c, i + 1, right, (), 48 + 6 * (5 * c + i - 9)))
    return found


def coarse_rows(c, plane):
    return (6 * plane, 6, 2) if c == 3 else (96 + 5 * (14 * c + plane - 1), 5, 1)


def pack_coarse(own, right, left, layer_ahead, layer_behind, ahead, behind):
    empty = jnp.zeros((8, 128), jnp.float32)
    for message, layer, offset in ((ahead, layer_ahead, 7), (behind, layer_behind, 4)):
        message[pl.ds(COARSE_ROWS_Y - 8, 8), :] = empty
        for f in range(4):
            base = LAYER_Y + 14 * f
            message[pl.ds(base, 1), :] = left[pl.ds(LAYER_X + 12 * f + offset, 1), :]
            message[pl.ds(base + 1, 12), :] = layer[f]
            message[pl.ds(base + 13, 1), :] = right[pl.ds(LAYER_X + 12 * f + offset, 1), :]
    for c, plane, source, index, row in coarse_planes(own, left, right):
        base, count, margin = coarse_rows(c, plane)
        ahead[pl.ds(base, count), :] = source[(*index, pl.ds(row, count), slice(None))]
        behind[pl.ds(base, count), :] = source[(*index, pl.ds(row + margin, count), slice(None))]


def smooth_kernel(
    main, after, before, smooth, message, ahead, behind, layer_ahead, layer_behind, state, side_state,
    ua, ub, va, vb, usa, usb, vsa, vsb, rest, modulus, diag, inverse, prev, next, rest_s, modulus_s, diag_s, inverse_s, prev_s, next_s, pairs, pairs_s,
):
    group = lane_index() // 32

    low = lane_index() % 32 < HALO

    def place(pair, carry):
        for s in range(2):
            plane = 2 * pair + s
            for t in range(3):
                here = pl.ds(8 * t, 8)
                for c in range(3):
                    rest[c, plane, here, :] = main[c, plane, here, :]
                modulus[plane, pl.ds(8 + 8 * t, 8), :] = main[3, plane, here, :]
                lower, upper = before[pair, here, :], after[pair, here, :]
                if s:
                    lower = pltpu.roll(lower, 128 - HALO, 1)
                else:
                    upper = pltpu.roll(upper, HALO, 1)
                value = jnp.where(low, lower, upper)
                rest_s[plane, here, :] = value
                spread = jnp.where(group == 1, pltpu.roll(value, 64, 1), pltpu.roll(value, 96, 1))
                spread = jnp.where(group == 0, pltpu.roll(value, 32, 1), spread)
                modulus_s[plane, pl.ds(8 + 8 * t, 8), :] = jnp.where(group == 3, value, spread)
        return carry

    lax.fori_loop(0, 12, place, 0, unroll=4)

    def begin(i, carry):
        for plane in (2 + 2 * i, 3 + 2 * i):
            for t in range(3):
                here, margin = pl.ds(8 * t, 8), pl.ds(8 + 8 * t, 8)
                (mid, d, inv), (mid_s, d_s, inv_s), beside = side_diagonal(modulus, modulus_s, plane, 8 + 8 * t)
                for refs, values in zip(((prev, next), (prev_s, next_s)), beside):
                    for ref, value in zip(refs, values):
                        ref[plane, here, :] = value
                diag[plane, here, :] = d
                inverse[plane, here, :] = inv
                diag_s[plane, here, :] = d_s
                inverse_s[plane, here, :] = inv_s
                inv = inv * (1.0 / THETA)
                for c in range(3):
                    step = rest[c, plane, here, :] * inv
                    ua[c, plane, margin, :] = step
                    va[c, plane, margin, :] = mid * step
                step = rest_s[plane, here, :] * (inv_s * (1.0 / THETA))
                usa[plane, margin, :] = step
                vsa[plane, margin, :] = mid_s * step
        return carry

    lax.fori_loop(0, 10, begin, 0)

    def gather(steps, start):
        def body(p, carry):
            for c in range(3):
                step = steps[c, 8 + p, pl.ds(16, 8), :]
                smooth[c, p] = step if start else smooth[c, p] + step
            return carry

        lax.fori_loop(0, 8, body, 0, unroll=4)

    gather(ua, True)
    scales = sweep_scales()

    def reader(ref, margin):
        return lambda plane, row: ref[plane, pl.ds(margin + row, 8), :]

    moduli = [
        [reader(modulus, 8), reader(prev, 0), reader(next, 0)],
        [reader(modulus_s, 8), reader(prev_s, 0), reader(next_s, 0)],
    ]
    readers = [moduli] + [[reader(ref, 0) for ref in refs] for refs in ((diag, diag_s), (inverse, inverse_s))]
    for k in range(1, SWEEPS + 1):
        now, later = (ua, va, usa, vsa), (ub, vb, usb, vsb)
        if k % 2 == 0:
            now, later = later, now
        rows = (0, 8, 16) if k == 1 else (4, 12)
        sweep(SMOOTH_CHUNKS, (2 + k, 22 - k), rows, now, later, (rest, rest_s), *readers, scales[k - 1] if k < SWEEPS else None)
        if k < SWEEPS:
            gather(later[0], False)

    def restrict(p, carry):
        def four(ref, at, margin):
            a, b = (ref[(*at, 4 + 2 * p + dx, pl.ds(margin + 4, 8, stride=2), slice(None))] for dx in range(2))
            c, d = (ref[(*at, 4 + 2 * p + dx, pl.ds(margin + 5, 8, stride=2), slice(None))] for dx in range(2))
            return (a + b) + (c + d)

        for c in range(3):
            pairs[c, p] = four(rest, (c,), 0)
        pairs[3, p] = 0.25 * four(modulus, (), 8)
        pairs_s[0, p] = four(rest_s, (), 0)
        pairs_s[1, p] = 0.25 * four(modulus_s, (), 8)
        return carry

    lax.fori_loop(0, 8, restrict, 0, unroll=4)
    coarse = exact_dot(pairs[...].reshape(256, 128), pair_matrix(None, 0)).reshape(4, 8, 8, 128)
    for c in range(4):
        source = pairs_s[1 if c == 3 else 0].reshape(64, 128)
        message[c] = coarse[c] + exact_dot(source, pair_matrix(c % 3, 0)).reshape(8, 8, 128)
    for i in range(6):
        ahead[pl.ds(8 * i, 8), :] = message[3, i]
        behind[pl.ds(8 * i, 8), :] = message[3, 2 + i]
    for f, source in enumerate([rest.at[c] for c in range(3)] + [rest_s]):
        ahead[pl.ds(LAYER_X + 12 * f, 12), :] = source[13, pl.ds(6, 12), :]
        behind[pl.ds(LAYER_X + 12 * f, 12), :] = source[10, pl.ds(6, 12), :]
        for p in range(12):
            layer_ahead[f, pl.ds(p, 1), :] = source[6 + p, pl.ds(13, 1), :]
            layer_behind[f, pl.ds(p, 1), :] = source[6 + p, pl.ds(10, 1), :]
    empty = jnp.zeros((6, 128), jnp.float32)
    ahead[pl.ds(LAYER_X + 48, 6), :] = empty
    behind[pl.ds(LAYER_X + 48, 6), :] = empty
    for c in range(3):
        for i in range(5):
            ahead[pl.ds(48 + 6 * (5 * c + i), 6), :] = message[c, 1 + i, pl.ds(1, 6), :]
            behind[pl.ds(48 + 6 * (5 * c + i), 6), :] = message[c, 2 + i, pl.ds(1, 6), :]

    kept = (
        (modulus, modulus_s, 12), (diag, diag_s, 4), (inverse, inverse_s, 4), (prev, prev_s, 4), (next, next_s, 4)
    )

    def keep_state(p, carry):
        for c in range(3):
            state[c, p] = rest[c, 4 + p, pl.ds(4, 16), :]
        side_state[0, p] = rest_s[4 + p, pl.ds(4, 16), :]
        for f, (ref, ref_s, row) in enumerate(kept):
            state[3 + f, p] = ref[4 + p, pl.ds(row, 16), :]
            side_state[1 + f, p] = ref_s[4 + p, pl.ds(row, 16), :]
        return carry

    lax.fori_loop(0, 16, keep_state, 0, unroll=4)


def post_kernel(
    own, right, left, up, down, state_in, side_in, smooth, correction, coarse,
    ca, cb, cva, cvb, crest, cmod, cinv, cdiag, cprev, cnext, total, ua, ub, va, vb, usa, usb, vsa, vsb, wide, wide_s, rest, rest_s,
):
    scales = sweep_scales()

    empty = jnp.zeros((16, 128), jnp.float32)
    for c in range(3):
        crest[c, 0] = empty
        crest[c, 15] = empty
    edge = jnp.zeros((1, 128), jnp.float32)
    for c, plane, source, index, row in coarse_planes(own, left, right):
        base, count, margin = coarse_rows(c, plane)
        mid = source[(*index, pl.ds(row + margin, 4), slice(None))]
        below, above = down[pl.ds(base, count), :], up[pl.ds(base, count), :]
        if c < 3:
            crest[c, plane, pl.ds(0, 1), :] = edge
            crest[c, plane, pl.ds(1, 5), :] = below
            crest[c, plane, pl.ds(6, 4), :] = mid
            crest[c, plane, pl.ds(10, 5), :] = above
            crest[c, plane, pl.ds(15, 1), :] = edge
        else:
            cmod[plane, pl.ds(8, 6), :] = below
            cmod[plane, pl.ds(14, 4), :] = mid
            cmod[plane, pl.ds(18, 6), :] = above

    def begin(i, carry):
        for plane in [1 + 7 * i + j for j in range(7)]:
            for t in range(2):
                here, margin = pl.ds(8 * t, 8), pl.ds(8 + 8 * t, 8)
                mid, d, inv = ring_diagonal(cmod, plane, 8 + 8 * t)
                cdiag[plane, here, :] = d
                cprev[plane, here, :] = pltpu.roll(mid, 1, 1)
                cnext[plane, here, :] = pltpu.roll(mid, 127, 1)
                cinv[plane, here, :] = inv
                inv = inv * (1.0 / THETA)
                for c in range(3):
                    step = crest[c, plane, here, :] * inv
                    ca[c, plane, margin, :] = step
                    cva[c, plane, margin, :] = mid * step
        return carry

    lax.fori_loop(0, 2, begin, 0)

    def gather(steps, start):
        def body(p, carry):
            for c in range(3):
                step = steps[c, 4 + p, pl.ds(12, 8), :]
                total[c, p] = step if start else total[c, p] + step
            return carry

        lax.fori_loop(0, 8, body, 0, unroll=4)

    gather(ca, True)

    def reader(ref, margin):
        return lambda plane, row: ref[plane, pl.ds(margin + row, 8), :]

    coarse_moduli = [[reader(cmod, 8), reader(cprev, 0), reader(cnext, 0)]]
    for k in range(1, SWEEPS):
        now, later = ((ca, cva), (cb, cvb)) if k % 2 else ((cb, cvb), (ca, cva))
        sweep(POST_CHUNKS, (1 + k, 15 - k), (0, 8) if k < 3 else (4,), now, later, (crest,), coarse_moduli, [reader(cdiag, 0)], [reader(cinv, 0)], scales[k - 1])
        gather(later[0], False)

    for c in range(3):
        for p in range(4):
            coarse[c, p] = total[c, 2 + p, pl.ds(2, 4), pl.ds(0, 64)]

    wide[...] = exact_dot(total[...].reshape(192, 128), pair_matrix(None, 1)).reshape(3, 8, 8, 128)
    spread = None
    for c in range(3):
        part = exact_dot(total[c].reshape(64, 128), pair_matrix(c, 1))
        spread = part if spread is None else spread + part
    wide_s[...] = spread.reshape(8, 8, 128)

    def lift(p, carry):
        for dx in range(2):
            for dy in range(2):
                for c in range(3):
                    ua[c, 2 * p + dx, pl.ds(8 + dy, 8, stride=2), :] = wide[c, p]
                usa[2 * p + dx, pl.ds(8 + dy, 8, stride=2), :] = wide_s[p]
        return carry

    lax.fori_loop(0, 8, lift, 0, unroll=2)

    def weigh(p, carry):
        for c in range(3):
            va[c, p, pl.ds(8, 16), :] = state_in[3, p] * ua[c, p, pl.ds(8, 16), :]
            rest[c, p] = state_in[c, p]
        vsa[p, pl.ds(8, 16), :] = side_in[1, p] * usa[p, pl.ds(8, 16), :]
        rest_s[p] = side_in[0, p]
        return carry

    lax.fori_loop(0, 16, weigh, 0, unroll=2)
    for f, target in enumerate([rest.at[c] for c in range(3)] + [rest_s]):
        target[1, pl.ds(2, 12), :] = left[pl.ds(LAYER_X + 12 * f, 12), :]
        target[14, pl.ds(2, 12), :] = right[pl.ds(LAYER_X + 12 * f, 12), :]
        for p in range(14):
            target[1 + p, pl.ds(1, 1), :] = down[pl.ds(LAYER_Y + 14 * f + p, 1), :]
            target[1 + p, pl.ds(14, 1), :] = up[pl.ds(LAYER_Y + 14 * f + p, 1), :]

    def add_own(steps, start):
        def body(p, carry):
            for c in range(3):
                step = steps[c, 4 + p, pl.ds(12, 8), :]
                correction[c, p] = (smooth[c, p] if start else correction[c, p]) + step
            return carry

        lax.fori_loop(0, 8, body, 0, unroll=4)

    add_own(ua, True)

    def held(f):
        return [
            lambda plane, row: state_in[3 + f, plane, pl.ds(row, 8), :],
            lambda plane, row: side_in[1 + f, plane, pl.ds(row, 8), :],
        ]

    moduli = list(zip(held(0), held(3), held(4)))

    def emit(c, plane, step):
        correction[c, plane - 4] = correction[c, plane - 4] + step

    for k in range(SWEEPS):
        now, later = (ua, va, usa, vsa), (ub, vb, usb, vsb)
        if k % 2:
            now, later = later, now
        scale = scales[k - 1] if k else (None, 1.0 / THETA)
        last = k == SWEEPS - 1
        sweep(
            POST_CHUNKS, (1 + k, 15 - k), (4,) if last else (0, 8), now, later, (rest, rest_s), moduli, held(1), held(2), scale,
            emit if last else None,
        )
        if not last:
            add_own(later[0], False)


def call(kernel, outs, scratch=()):
    return pl.pallas_call(
        kernel,
        out_shape=[jax.ShapeDtypeStruct(s, jnp.float32) for s in outs],
        scratch_shapes=[pltpu.VMEM(s, jnp.float32) for s in scratch],
        compiler_params=pltpu.CompilerParams(vmem_limit_bytes=48 * 1024 * 1024),
    )


def neighbours(to_next, to_previous, axis):
    count = lax.axis_size(axis)
    after = lax.ppermute(to_previous, axis, [(i + 1, i) for i in range(count - 1)])
    before = lax.ppermute(to_next, axis, [(i, i + 1) for i in range(count - 1)])
    return before, after


SMOOTH_OUTS = [
    (3, 8, 8, 128),
    (4, 8, 8, 128),
    (COARSE_ROWS_X, 128),
    (COARSE_ROWS_X, 128),
    (4, 12, 128),
    (4, 12, 128),
    (8, 16, 16, 128),
    (6, 16, 16, 128),
]
SMOOTH_SCRATCH = [
    *[(3, 24, 40, 128)] * 4,
    *[(24, 40, 128)] * 4,
    (3, 24, 24, 128),
    (24, 40, 128),
    *[(24, 24, 128)] * 5,
    (24, 40, 128),
    *[(24, 24, 128)] * 4,
    (4, 8, 8, 128),
    (2, 8, 8, 128),
]
POST_OUTS = [(3, 8, 8, 128), (3, 4, 4, 64)]
POST_SCRATCH = [
    *[(3, 16, 32, 128)] * 4,
    (3, 16, 16, 128),
    (16, 32, 128),
    *[(16, 16, 128)] * 4,
    (3, 8, 8, 128),
    *[(3, 16, 32, 128)] * 4,
    *[(16, 32, 128)] * 4,
    (3, 8, 8, 128),
    (8, 8, 128),
    (3, 16, 16, 128),
    (16, 16, 128),
]


def on_device(levels, residual):
    ratio = levels.astype(jnp.float32) / 255.0
    modulus = (0.05 + 0.95 * ratio * ratio * ratio) / UNIT
    own = jnp.concatenate([residual, modulus[None]])
    ahead, behind = call(pack_planes, [(25, 8, 128), (25, 8, 128)])(own)
    left, right = neighbours(ahead, behind, "gx")
    ahead, behind = call(pack_rows, [(FINE_ROWS, 128)] * 2)(own, right, left)
    down, up = neighbours(ahead, behind, "gy")
    main, first, last = call(pack_lanes, [(4, 24, 24, 128), (12, 24, 128), (12, 24, 128)])(own, right, left, up, down)
    before, after = neighbours(last, first, "gz")
    smooth, own, ahead, behind, layer_ahead, layer_behind, state, side_state = call(
        smooth_kernel, SMOOTH_OUTS, SMOOTH_SCRATCH
    )(main, after, before)
    left, right = neighbours(ahead, behind, "gx")
    ahead, behind = call(pack_coarse, [(COARSE_ROWS_Y, 128)] * 2)(own, right, left, layer_ahead, layer_behind)
    down, up = neighbours(ahead, behind, "gy")
    correction, coarse = call(post_kernel, POST_OUTS, POST_SCRATCH)(own, right, left, up, down, state, side_state, smooth)
    return correction, coarse


def solution(mesh):
    return jax.shard_map(
        on_device,
        mesh=mesh,
        in_specs=(P("gx", "gy", "gz"), P(None, "gx", "gy", "gz")),
        out_specs=(P(None, "gx", "gy", "gz"), P(None, "gx", "gy", "gz")),
        check_vma=False,
    )
```

```python
import jax
import jax.numpy as jnp
from jax import lax
from jax.experimental import pallas as pl
from jax.experimental.pallas import tpu as pltpu
from jax.sharding import PartitionSpec as P

SWEEPS = 4
THETA = 1.15
DELTA = 0.85

FACE, SIDE, EDGE, FLAT, TURN, TWIST = 9.6, 6.0, 2.7, 1.8, 0.9, 0.4
UNIT = 120.0
WHOLE = 1.92
HALO = 16
SMOOTH_CHUNKS = (4, 3, 2, 1)
POST_CHUNKS = (4, 3, 5, 7, 2, 1)


def sweep_scales():
    sigma = THETA / DELTA
    rho = 1.0 / sigma
    scales = []
    for _ in range(SWEEPS - 1):
        rho_next = 1.0 / (2.0 * sigma - rho)
        scales.append((rho_next * rho, 2.0 * rho_next / DELTA))
        rho = rho_next
    return scales


def lane_index():
    return lax.broadcasted_iota(jnp.int32, (8, 128), 1)


def by_group(values):
    group = lane_index() // 32
    out = jnp.full((8, 128), values[-1], jnp.float32)
    for g in range(len(values) - 1):
        out = jnp.where(group == g, values[g], out)
    return out


def neighbourhood(load, count):
    mid, summed, spread = [], [], []
    for p in range(-1, count + 1):
        u, yp, ym = load(p, 0), load(p, 1), load(p, -1)
        mid.append(u)
        summed.append(yp + ym)
        spread.append(yp - ym)
    return mid, summed, spread


def stencil(field, plane, count, row):
    def loader(c):
        return lambda p, dy: field[c, plane + p, pl.ds(row + dy, 8), :]

    flat, even, odd = ([[None] * 3 for _ in range(count)] for _ in range(3))
    cross, along, across = [None] * count, [None] * count, [None] * count
    mid, summed, spread = neighbourhood(loader(0), count)
    for p in range(count):
        u, sy = mid[p + 1], summed[p + 1]
        sx, sxy = mid[p + 2] + mid[p], summed[p + 2] + summed[p]
        flat[p][0] = FACE * sx + SIDE * sy + EDGE * sxy
        even[p][0] = SIDE * u + EDGE * sx + FLAT * sy + sxy
        cross[p] = spread[p + 2] - spread[p]
        along[p], across[p] = mid[p + 2] - mid[p], summed[p + 2] - summed[p]
    mid, summed, spread = neighbourhood(loader(1), count)
    for p in range(count):
        u, sy = mid[p + 1], summed[p + 1]
        sx, sxy = mid[p + 2] + mid[p], summed[p + 2] + summed[p]
        flat[p][1] = FACE * sy + SIDE * sx + EDGE * sxy + TURN * cross[p]
        even[p][1] = SIDE * u + EDGE * sy + FLAT * sx + sxy + TWIST * cross[p]
        back = spread[p + 2] - spread[p]
        flat[p][0] = flat[p][0] + TURN * back
        even[p][0] = even[p][0] + TWIST * back
        odd[p][2] = TURN * (along[p] + spread[p + 1]) + TWIST * (across[p] + (spread[p + 2] + spread[p]))
    mid, summed, spread = neighbourhood(loader(2), count)
    for p in range(count):
        both, sxy = mid[p + 2] + mid[p] + summed[p + 1], summed[p + 2] + summed[p]
        flat[p][2] = SIDE * both + FLAT * sxy
        even[p][2] = FACE * mid[p + 1] + EDGE * both + sxy
        odd[p][0] = TURN * (mid[p + 2] - mid[p]) + TWIST * (summed[p + 2] - summed[p])
        odd[p][1] = TURN * spread[p + 1] + TWIST * (spread[p + 2] + spread[p])
    return [[(flat[p][c], even[p][c] + odd[p][c], even[p][c] - odd[p][c]) for c in range(3)] for p in range(count)]


def side_stencil(field, plane, count, row):
    mid, summed, spread = neighbourhood(lambda p, dy: field[plane + p, pl.ds(row + dy, 8), :], count)
    group = lane_index() // 32
    flat_x, flat_y = by_group((FACE, SIDE, SIDE)), by_group((SIDE, FACE, SIDE))
    flat_xy, even_u = by_group((EDGE, EDGE, FLAT)), by_group((SIDE, SIDE, FACE))
    even_x, even_y = by_group((EDGE, FLAT, EDGE)), by_group((FLAT, EDGE, EDGE))
    found = []
    for p in range(count):
        u, sy, dy = mid[p + 1], summed[p + 1], spread[p + 1]
        sx, dx = mid[p + 2] + mid[p], mid[p + 2] - mid[p]
        sxy, dx_sy = summed[p + 2] + summed[p], summed[p + 2] - summed[p]
        dy_sx, dxy = spread[p + 2] + spread[p], spread[p + 2] - spread[p]
        along_x, along_y = TURN * dx + TWIST * dx_sy, TURN * dy + TWIST * dy_sx
        down = pltpu.roll(jnp.where(group == 1, dxy, along_y), 96, 1)
        up = pltpu.roll(jnp.where(group == 0, dxy, along_y), 32, 1)
        far = pltpu.roll(along_x, 64, 1)
        cross = jnp.where(group == 0, down, jnp.where(group == 1, up, 0.0))
        flat = flat_x * sx + flat_y * sy + flat_xy * sxy + TURN * cross
        even = even_u * u + even_x * sx + even_y * sy + sxy + TWIST * cross
        odd = jnp.where(group == 0, far, jnp.where(group == 1, down, far + up))
        found.append((flat, even + odd, even - odd))
    return found


def join_ring(part):
    centre, above, below = part
    return centre + (pltpu.roll(above, 127, 1) + pltpu.roll(below, 1, 1))


def side_lanes():
    lane = lane_index()
    return lane, lane % 32 == HALO


def join_sides(parts, side):
    lane, begins = side_lanes()
    ends = jnp.where(begins, side[1], side[2])
    side_above, side_below = side[1], side[2]
    joined = []
    for c, (centre, above, below) in enumerate(parts):
        inward = pltpu.roll(ends, 112 - 32 * c, 1)
        outward = pltpu.roll(jnp.where(lane == 0, above, below), 32 * c + HALO, 1)
        up = pltpu.roll(jnp.where(lane == 0, inward, above), 127, 1)
        down = pltpu.roll(jnp.where(lane == 127, inward, below), 1, 1)
        joined.append(centre + (up + down))
        side_above = jnp.where(lane == 32 * c + HALO, outward, side_above)
        side_below = jnp.where(lane == 32 * c + HALO - 1, outward, side_below)
    return joined, side[0] + (pltpu.roll(side_above, 127, 1) + pltpu.roll(side_below, 1, 1))


def shifted(main, side):
    lane, begins = side_lanes()
    inward = pltpu.roll(side, 112, 1)
    side_below, side_above = side, side
    for g in range(3):
        outward = pltpu.roll(main, 32 * g + HALO, 1)
        side_above = jnp.where(lane == 32 * g + HALO, outward, side_above)
        side_below = jnp.where(lane == 32 * g + HALO - 1, outward, side_below)
    return (
        (pltpu.roll(jnp.where(lane == 127, inward, main), 1, 1), pltpu.roll(jnp.where(lane == 0, inward, main), 127, 1)),
        (pltpu.roll(side_below, 1, 1), pltpu.roll(side_above, 127, 1)),
    )


def weighted(modulus, plain, heavy):
    here, before, after = modulus
    return (here * plain[0] + heavy[0], before * plain[1] + heavy[1], after * plain[2] + heavy[2])


def coupling(now, modulus, plane, count, row):
    plain, heavy = (stencil(now[k], plane, count, row) for k in range(2))
    parts = [[weighted(modulus[p][0], *both) for both in zip(plain[p], heavy[p])] for p in range(count)]
    if len(now) == 2:
        return [([join_ring(part) for part in parts[p]], None) for p in range(count)]
    plain, heavy = (side_stencil(now[2 + k], plane, count, row) for k in range(2))
    return [join_sides(parts[p], weighted(modulus[p][1], plain[p], heavy[p])) for p in range(count)]


def sweep(chunks, planes, rows, now, later, rest, modulus, diag, inverse, scale, emit=None):
    lo, hi = planes
    chunk = next(n for n in chunks if (hi - lo) % n == 0)
    sides = len(rest) if not emit else 1

    def body(i, carry):
        first = lo + i * chunk
        for row in rows:
            mods = [[[read(first + j, row) for read in reads] for reads in modulus] for j in range(chunk)]
            out = coupling(now, mods, first, chunk, 8 + row)
            for j in range(chunk):
                plane = first + j
                for t in range(sides):
                    d = diag[t](plane, row)
                    if scale:
                        inv = inverse[t](plane, row) * scale[1]
                    for c in range(1 if t else 3):
                        at = (plane,) if t else (c, plane)
                        here, margin = (*at, pl.ds(row, 8), slice(None)), (*at, pl.ds(8 + row, 8), slice(None))
                        old = now[2 * t][margin]
                        r = rest[t][here] - d * old + (out[j][1] if t else out[j][0][c])
                        if not emit:
                            rest[t][here] = r
                        if scale:
                            step = inv * r
                            if scale[0]:
                                step = scale[0] * old + step
                            if emit:
                                emit(c, plane, step)
                            else:
                                later[2 * t][margin] = step
                                later[2 * t + 1][margin] = mods[j][t][0] * step
        return carry

    lax.fori_loop(0, (hi - lo) // chunk, body, 0)


def diagonal_parts(modulus, plane, row):
    def at(dx, dy):
        return modulus[plane + dx, pl.ds(row + dy, 8), :]

    u = at(0, 0)
    cross = (at(1, 0) + at(-1, 0)) + (at(0, 1) + at(0, -1))
    corner = (at(1, 1) + at(-1, -1)) + (at(1, -1) + at(-1, 1))
    even = 0.16 * u + 0.06 * cross + 0.03 * corner
    return u, (WHOLE * u + 0.16 * cross + 0.06 * corner, even, even)


def finish_diagonal(mid, total):
    diag = (1.05 * 0.5 * UNIT) * total
    inside = mid > 0.0
    return mid, diag, jnp.where(inside, 1.0 / jnp.where(inside, diag, 1.0), 0.0)


def ring_diagonal(modulus, plane, row):
    mid, part = diagonal_parts(modulus, plane, row)
    return finish_diagonal(mid, join_ring(part))


def side_diagonal(modulus, side_modulus, plane, row):
    mid, (centre, even, _) = diagonal_parts(modulus, plane, row)
    side_mid, (side_centre, side_even, _) = diagonal_parts(side_modulus, plane, row)
    (below, above), (side_below, side_above) = shifted(even, side_even)
    main = finish_diagonal(mid, centre + (below + above))
    side_mid, side_diag, side_inverse = finish_diagonal(side_mid, side_centre + (side_below + side_above))
    side_inverse = jnp.where(lane_index() < 96, side_inverse, 0.0)
    return main, (side_mid, side_diag, side_inverse), shifted(mid, side_mid)


def pair_matrix(group, fine_axis):
    fine = lax.broadcasted_iota(jnp.int32, (128, 128), fine_axis)
    coarse = lax.broadcasted_iota(jnp.int32, (128, 128), 1 - fine_axis)
    if group is None:
        return (lax.shift_right_logical(fine, 1) == coarse).astype(jnp.float32)
    inner = fine - 32 * group
    target = lax.shift_right_logical(fine, 1) - 16 * group + jnp.where(inner < HALO, 120, 56)
    return ((target == coarse) & (inner >= 0) & (inner < 32)).astype(jnp.float32)


def exact_dot(a, b):
    return jnp.dot(a, b, precision=lax.Precision.HIGHEST, preferred_element_type=jnp.float32)


def pack_planes(own, ahead, behind):
    for p in range(8):
        if p > 0:
            ahead[p - 1] = own[3, p]
        if p < 7:
            behind[p] = own[3, p]
        for c in range(3):
            if p > 1:
                ahead[7 + 6 * c + p - 2] = own[c, p]
            if p < 6:
                behind[7 + 6 * c + p] = own[c, p]


def fine_planes(own, left, right):
    found = []
    for plane in range(1, 23):
        if plane < 8:
            found.append((3, plane, left, (plane - 1,)))
        elif plane < 16:
            found.append((3, plane, own, (3, plane - 8)))
        else:
            found.append((3, plane, right, (plane - 16,)))
    for c in range(3):
        for plane in range(2, 22):
            if plane < 8:
                found.append((c, plane, left, (7 + 6 * c + plane - 2,)))
            elif plane < 16:
                found.append((c, plane, own, (c, plane - 8)))
            else:
                found.append((c, plane, right, (7 + 6 * c + plane - 16,)))
    return found


FINE_ROWS = 520


def fine_rows(c, plane):
    return (7 * (plane - 1), 7) if c == 3 else (154 + 6 * (20 * c + plane - 2), 6)


def pack_rows(own, right, left, ahead, behind):
    empty = jnp.zeros((8, 128), jnp.float32)
    ahead[pl.ds(FINE_ROWS - 8, 8), :] = empty
    behind[pl.ds(FINE_ROWS - 8, 8), :] = empty
    for c, plane, source, index in fine_planes(own, left, right):
        base, count = fine_rows(c, plane)
        ahead[pl.ds(base, count), :] = source[(*index, pl.ds(8 - count, count), slice(None))]
        behind[pl.ds(base, count), :] = source[(*index, pl.ds(0, count), slice(None))]


def pack_lanes(own, right, left, up, down, main, first, last):
    empty = jnp.zeros((24, 128), jnp.float32)
    for plane in (0, 1, 22, 23):
        for c in range(3):
            main[c, plane] = empty
    main[3, 0] = empty
    main[3, 23] = empty
    gap = jnp.zeros((2, 128), jnp.float32)
    for c, plane, source, index in fine_planes(own, left, right):
        base, count = fine_rows(c, plane)
        main[c, plane, pl.ds(0, 2), :] = gap
        main[c, plane, pl.ds(22, 2), :] = gap
        main[c, plane, pl.ds(8, 8), :] = source[index]
        main[c, plane, pl.ds(8 - count, count), :] = down[pl.ds(base, count), :]
        main[c, plane, pl.ds(16, count), :] = up[pl.ds(base, count), :]
    group, lower = lane_index() // 32, lane_index() % 32 < HALO

    def pack(pair, carry):
        for t in range(3):
            ends = []
            for s in range(2):
                value = pltpu.roll(main[3, 2 * pair + s, pl.ds(8 * t, 8), :], 96 + HALO, 1)
                for c in range(3):
                    turned = pltpu.roll(main[c, 2 * pair + s, pl.ds(8 * t, 8), :], 32 * c + HALO, 1)
                    value = jnp.where(group == c, turned, value)
                ends.append(value)
            first[pair, pl.ds(8 * t, 8), :] = jnp.where(lower, pltpu.roll(ends[0], 128 - HALO, 1), ends[1])
            last[pair, pl.ds(8 * t, 8), :] = jnp.where(lower, ends[0], pltpu.roll(ends[1], HALO, 1))
        return carry

    lax.fori_loop(0, 12, pack, 0, unroll=6)


LAYER_X = 6 * 8 + 3 * 5 * 6
LAYER_Y = 16 * 6 + 3 * 14 * 5
COARSE_ROWS_X = 192
COARSE_ROWS_Y = 368


def coarse_planes(own, left, right):
    found = []
    for i in range(16):
        if i < 6:
            found.append((3, i, left, (), 8 * i))
        elif i < 10:
            found.append((3, i, own, (3, i - 4), 0))
        else:
            found.append((3, i, right, (), 8 * (i - 10)))
    for c in range(3):
        for i in range(14):
            if i < 5:
                found.append((c, i + 1, left, (), 48 + 6 * (5 * c + i)))
            elif i < 9:
                found.append((c, i + 1, own, (c, i - 3), 1))
            else:
                found.append((c, i + 1, right, (), 48 + 6 * (5 * c + i - 9)))
    return found


def coarse_rows(c, plane):
    return (6 * plane, 6, 2) if c == 3 else (96 + 5 * (14 * c + plane - 1), 5, 1)


def pack_coarse(own, right, left, layer_ahead, layer_behind, ahead, behind):
    empty = jnp.zeros((8, 128), jnp.float32)
    for message, layer, offset in ((ahead, layer_ahead, 7), (behind, layer_behind, 4)):
        message[pl.ds(COARSE_ROWS_Y - 8, 8), :] = empty
        for f in range(4):
            base = LAYER_Y + 14 * f
            message[pl.ds(base, 1), :] = left[pl.ds(LAYER_X + 12 * f + offset, 1), :]
            message[pl.ds(base + 1, 12), :] = layer[f]
            message[pl.ds(base + 13, 1), :] = right[pl.ds(LAYER_X + 12 * f + offset, 1), :]
    for c, plane, source, index, row in coarse_planes(own, left, right):
        base, count, margin = coarse_rows(c, plane)
        ahead[pl.ds(base, count), :] = source[(*index, pl.ds(row, count), slice(None))]
        behind[pl.ds(base, count), :] = source[(*index, pl.ds(row + margin, count), slice(None))]


def smooth_kernel(
    main, after, before, smooth, message, ahead, behind, layer_ahead, layer_behind, state, side_state,
    ua, ub, va, vb, usa, usb, vsa, vsb, rest, modulus, diag, inverse, prev, next, rest_s, modulus_s, diag_s, inverse_s, prev_s, next_s, pairs, pairs_s,
):
    group = lane_index() // 32

    low = lane_index() % 32 < HALO

    def place(pair, carry):
        for s in range(2):
            plane = 2 * pair + s
            for t in range(3):
                here = pl.ds(8 * t, 8)
                for c in range(3):
                    rest[c, plane, here, :] = main[c, plane, here, :]
                modulus[plane, pl.ds(8 + 8 * t, 8), :] = main[3, plane, here, :]
                lower, upper = before[pair, here, :], after[pair, here, :]
                if s:
                    lower = pltpu.roll(lower, 128 - HALO, 1)
                else:
                    upper = pltpu.roll(upper, HALO, 1)
                value = jnp.where(low, lower, upper)
                rest_s[plane, here, :] = value
                spread = jnp.where(group == 1, pltpu.roll(value, 64, 1), pltpu.roll(value, 96, 1))
                spread = jnp.where(group == 0, pltpu.roll(value, 32, 1), spread)
                modulus_s[plane, pl.ds(8 + 8 * t, 8), :] = jnp.where(group == 3, value, spread)
        return carry

    lax.fori_loop(0, 12, place, 0, unroll=4)

    def begin(i, carry):
        for plane in (2 + 2 * i, 3 + 2 * i):
            for t in range(3):
                here, margin = pl.ds(8 * t, 8), pl.ds(8 + 8 * t, 8)
                (mid, d, inv), (mid_s, d_s, inv_s), beside = side_diagonal(modulus, modulus_s, plane, 8 + 8 * t)
                for refs, values in zip(((prev, next), (prev_s, next_s)), beside):
                    for ref, value in zip(refs, values):
                        ref[plane, here, :] = value
                diag[plane, here, :] = d
                inverse[plane, here, :] = inv
                diag_s[plane, here, :] = d_s
                inverse_s[plane, here, :] = inv_s
                inv = inv * (1.0 / THETA)
                for c in range(3):
                    step = rest[c, plane, here, :] * inv
                    ua[c, plane, margin, :] = step
                    va[c, plane, margin, :] = mid * step
                step = rest_s[plane, here, :] * (inv_s * (1.0 / THETA))
                usa[plane, margin, :] = step
                vsa[plane, margin, :] = mid_s * step
        return carry

    lax.fori_loop(0, 10, begin, 0)

    def gather(steps, start):
        def body(p, carry):
            for c in range(3):
                step = steps[c, 8 + p, pl.ds(16, 8), :]
                smooth[c, p] = step if start else smooth[c, p] + step
            return carry

        lax.fori_loop(0, 8, body, 0, unroll=4)

    gather(ua, True)
    scales = sweep_scales()

    def reader(ref, margin):
        return lambda plane, row: ref[plane, pl.ds(margin + row, 8), :]

    moduli = [
        [reader(modulus, 8), reader(prev, 0), reader(next, 0)],
        [reader(modulus_s, 8), reader(prev_s, 0), reader(next_s, 0)],
    ]
    readers = [moduli] + [[reader(ref, 0) for ref in refs] for refs in ((diag, diag_s), (inverse, inverse_s))]
    for k in range(1, SWEEPS + 1):
        now, later = (ua, va, usa, vsa), (ub, vb, usb, vsb)
        if k % 2 == 0:
            now, later = later, now
        rows = (0, 8, 16) if k == 1 else (4, 12)
        sweep(SMOOTH_CHUNKS, (2 + k, 22 - k), rows, now, later, (rest, rest_s), *readers, scales[k - 1] if k < SWEEPS else None)
        if k < SWEEPS:
            gather(later[0], False)

    def restrict(p, carry):
        def four(ref, at, margin):
            a, b = (ref[(*at, 4 + 2 * p + dx, pl.ds(margin + 4, 8, stride=2), slice(None))] for dx in range(2))
            c, d = (ref[(*at, 4 + 2 * p + dx, pl.ds(margin + 5, 8, stride=2), slice(None))] for dx in range(2))
            return (a + b) + (c + d)

        for c in range(3):
            pairs[c, p] = four(rest, (c,), 0)
        pairs[3, p] = 0.25 * four(modulus, (), 8)
        pairs_s[0, p] = four(rest_s, (), 0)
        pairs_s[1, p] = 0.25 * four(modulus_s, (), 8)
        return carry

    lax.fori_loop(0, 8, restrict, 0, unroll=8)
    coarse = exact_dot(pairs[...].reshape(256, 128), pair_matrix(None, 0)).reshape(4, 8, 8, 128)
    for c in range(4):
        source = pairs_s[1 if c == 3 else 0].reshape(64, 128)
        message[c] = coarse[c] + exact_dot(source, pair_matrix(c % 3, 0)).reshape(8, 8, 128)
    for i in range(6):
        ahead[pl.ds(8 * i, 8), :] = message[3, i]
        behind[pl.ds(8 * i, 8), :] = message[3, 2 + i]
    for f, source in enumerate([rest.at[c] for c in range(3)] + [rest_s]):
        ahead[pl.ds(LAYER_X + 12 * f, 12), :] = source[13, pl.ds(6, 12), :]
        behind[pl.ds(LAYER_X + 12 * f, 12), :] = source[10, pl.ds(6, 12), :]
        for p in range(12):
            layer_ahead[f, pl.ds(p, 1), :] = source[6 + p, pl.ds(13, 1), :]
            layer_behind[f, pl.ds(p, 1), :] = source[6 + p, pl.ds(10, 1), :]
    empty = jnp.zeros((6, 128), jnp.float32)
    ahead[pl.ds(LAYER_X + 48, 6), :] = empty
    behind[pl.ds(LAYER_X + 48, 6), :] = empty
    for c in range(3):
        for i in range(5):
            ahead[pl.ds(48 + 6 * (5 * c + i), 6), :] = message[c, 1 + i, pl.ds(1, 6), :]
            behind[pl.ds(48 + 6 * (5 * c + i), 6), :] = message[c, 2 + i, pl.ds(1, 6), :]

    kept = (
        (modulus, modulus_s, 12), (diag, diag_s, 4), (inverse, inverse_s, 4), (prev, prev_s, 4), (next, next_s, 4)
    )

    def keep_state(p, carry):
        for c in range(3):
            state[c, p] = rest[c, 4 + p, pl.ds(4, 16), :]
        side_state[0, p] = rest_s[4 + p, pl.ds(4, 16), :]
        for f, (ref, ref_s, row) in enumerate(kept):
            state[3 + f, p] = ref[4 + p, pl.ds(row, 16), :]
            side_state[1 + f, p] = ref_s[4 + p, pl.ds(row, 16), :]
        return carry

    lax.fori_loop(0, 16, keep_state, 0, unroll=8)


def post_kernel(
    own, right, left, up, down, state_in, side_in, smooth, correction, coarse,
    ca, cb, cva, cvb, crest, cmod, cinv, cdiag, cprev, cnext, total, ua, ub, va, vb, usa, usb, vsa, vsb, wide, wide_s, rest, rest_s,
):
    scales = sweep_scales()

    empty = jnp.zeros((16, 128), jnp.float32)
    for c in range(3):
        crest[c, 0] = empty
        crest[c, 15] = empty
    edge = jnp.zeros((1, 128), jnp.float32)
    for c, plane, source, index, row in coarse_planes(own, left, right):
        base, count, margin = coarse_rows(c, plane)
        mid = source[(*index, pl.ds(row + margin, 4), slice(None))]
        below, above = down[pl.ds(base, count), :], up[pl.ds(base, count), :]
        if c < 3:
            crest[c, plane, pl.ds(0, 1), :] = edge
            crest[c, plane, pl.ds(1, 5), :] = below
            crest[c, plane, pl.ds(6, 4), :] = mid
            crest[c, plane, pl.ds(10, 5), :] = above
            crest[c, plane, pl.ds(15, 1), :] = edge
        else:
            cmod[plane, pl.ds(8, 6), :] = below
            cmod[plane, pl.ds(14, 4), :] = mid
            cmod[plane, pl.ds(18, 6), :] = above

    def begin(i, carry):
        for plane in [1 + 7 * i + j for j in range(7)]:
            for t in range(2):
                here, margin = pl.ds(8 * t, 8), pl.ds(8 + 8 * t, 8)
                mid, d, inv = ring_diagonal(cmod, plane, 8 + 8 * t)
                cdiag[plane, here, :] = d
                cprev[plane, here, :] = pltpu.roll(mid, 1, 1)
                cnext[plane, here, :] = pltpu.roll(mid, 127, 1)
                cinv[plane, here, :] = inv
                inv = inv * (1.0 / THETA)
                for c in range(3):
                    step = crest[c, plane, here, :] * inv
                    ca[c, plane, margin, :] = step
                    cva[c, plane, margin, :] = mid * step
        return carry

    lax.fori_loop(0, 2, begin, 0)

    def gather(steps, start):
        def body(p, carry):
            for c in range(3):
                step = steps[c, 4 + p, pl.ds(12, 8), :]
                total[c, p] = step if start else total[c, p] + step
            return carry

        lax.fori_loop(0, 8, body, 0, unroll=4)

    gather(ca, True)

    def reader(ref, margin):
        return lambda plane, row: ref[plane, pl.ds(margin + row, 8), :]

    coarse_moduli = [[reader(cmod, 8), reader(cprev, 0), reader(cnext, 0)]]
    for k in range(1, SWEEPS):
        now, later = ((ca, cva), (cb, cvb)) if k % 2 else ((cb, cvb), (ca, cva))
        sweep(POST_CHUNKS, (1 + k, 15 - k), (0, 8) if k < 3 else (4,), now, later, (crest,), coarse_moduli, [reader(cdiag, 0)], [reader(cinv, 0)], scales[k - 1])
        gather(later[0], False)

    for c in range(3):
        for p in range(4):
            coarse[c, p] = total[c, 2 + p, pl.ds(2, 4), pl.ds(0, 64)]

    wide[...] = exact_dot(total[...].reshape(192, 128), pair_matrix(None, 1)).reshape(3, 8, 8, 128)
    spread = None
    for c in range(3):
        part = exact_dot(total[c].reshape(64, 128), pair_matrix(c, 1))
        spread = part if spread is None else spread + part
    wide_s[...] = spread.reshape(8, 8, 128)

    def lift(p, carry):
        for dx in range(2):
            for dy in range(2):
                for c in range(3):
                    ua[c, 2 * p + dx, pl.ds(8 + dy, 8, stride=2), :] = wide[c, p]
                usa[2 * p + dx, pl.ds(8 + dy, 8, stride=2), :] = wide_s[p]
        return carry

    lax.fori_loop(0, 8, lift, 0, unroll=4)

    def weigh(p, carry):
        for c in range(3):
            va[c, p, pl.ds(8, 16), :] = state_in[3, p] * ua[c, p, pl.ds(8, 16), :]
            rest[c, p] = state_in[c, p]
        vsa[p, pl.ds(8, 16), :] = side_in[1, p] * usa[p, pl.ds(8, 16), :]
        rest_s[p] = side_in[0, p]
        return carry

    lax.fori_loop(0, 16, weigh, 0, unroll=4)
    for f, target in enumerate([rest.at[c] for c in range(3)] + [rest_s]):
        target[1, pl.ds(2, 12), :] = left[pl.ds(LAYER_X + 12 * f, 12), :]
        target[14, pl.ds(2, 12), :] = right[pl.ds(LAYER_X + 12 * f, 12), :]
        for p in range(14):
            target[1 + p, pl.ds(1, 1), :] = down[pl.ds(LAYER_Y + 14 * f + p, 1), :]
            target[1 + p, pl.ds(14, 1), :] = up[pl.ds(LAYER_Y + 14 * f + p, 1), :]

    def add_own(steps, start):
        def body(p, carry):
            for c in range(3):
                step = steps[c, 4 + p, pl.ds(12, 8), :]
                correction[c, p] = (smooth[c, p] if start else correction[c, p]) + step
            return carry

        lax.fori_loop(0, 8, body, 0, unroll=4)

    add_own(ua, True)

    def held(f):
        return [
            lambda plane, row: state_in[3 + f, plane, pl.ds(row, 8), :],
            lambda plane, row: side_in[1 + f, plane, pl.ds(row, 8), :],
        ]

    moduli = list(zip(held(0), held(3), held(4)))

    def emit(c, plane, step):
        correction[c, plane - 4] = correction[c, plane - 4] + step

    for k in range(SWEEPS):
        now, later = (ua, va, usa, vsa), (ub, vb, usb, vsb)
        if k % 2:
            now, later = later, now
        scale = scales[k - 1] if k else (None, 1.0 / THETA)
        last = k == SWEEPS - 1
        sweep(
            POST_CHUNKS, (1 + k, 15 - k), (4,) if last else (0, 8), now, later, (rest, rest_s), moduli, held(1), held(2), scale,
            emit if last else None,
        )
        if not last:
            add_own(later[0], False)


def call(kernel, outs, scratch=()):
    return pl.pallas_call(
        kernel,
        out_shape=[jax.ShapeDtypeStruct(s, jnp.float32) for s in outs],
        scratch_shapes=[pltpu.VMEM(s, jnp.float32) for s in scratch],
        compiler_params=pltpu.CompilerParams(vmem_limit_bytes=48 * 1024 * 1024),
    )


def neighbours(to_next, to_previous, axis):
    count = lax.axis_size(axis)
    after = lax.ppermute(to_previous, axis, [(i + 1, i) for i in range(count - 1)])
    before = lax.ppermute(to_next, axis, [(i, i + 1) for i in range(count - 1)])
    return before, after


SMOOTH_OUTS = [
    (3, 8, 8, 128),
    (4, 8, 8, 128),
    (COARSE_ROWS_X, 128),
    (COARSE_ROWS_X, 128),
    (4, 12, 128),
    (4, 12, 128),
    (8, 16, 16, 128),
    (6, 16, 16, 128),
]
SMOOTH_SCRATCH = [
    *[(3, 24, 40, 128)] * 4,
    *[(24, 40, 128)] * 4,
    (3, 24, 24, 128),
    (24, 40, 128),
    *[(24, 24, 128)] * 5,
    (24, 40, 128),
    *[(24, 24, 128)] * 4,
    (4, 8, 8, 128),
    (2, 8, 8, 128),
]
POST_OUTS = [(3, 8, 8, 128), (3, 4, 4, 64)]
POST_SCRATCH = [
    *[(3, 16, 32, 128)] * 4,
    (3, 16, 16, 128),
    (16, 32, 128),
    *[(16, 16, 128)] * 4,
    (3, 8, 8, 128),
    *[(3, 16, 32, 128)] * 4,
    *[(16, 32, 128)] * 4,
    (3, 8, 8, 128),
    (8, 8, 128),
    (3, 16, 16, 128),
    (16, 16, 128),
]


def on_device(levels, residual):
    ratio = levels.astype(jnp.float32) / 255.0
    modulus = (0.05 + 0.95 * ratio * ratio * ratio) / UNIT
    own = jnp.concatenate([residual, modulus[None]])
    ahead, behind = call(pack_planes, [(25, 8, 128), (25, 8, 128)])(own)
    left, right = neighbours(ahead, behind, "gx")
    ahead, behind = call(pack_rows, [(FINE_ROWS, 128)] * 2)(own, right, left)
    down, up = neighbours(ahead, behind, "gy")
    main, first, last = call(pack_lanes, [(4, 24, 24, 128), (12, 24, 128), (12, 24, 128)])(own, right, left, up, down)
    before, after = neighbours(last, first, "gz")
    smooth, own, ahead, behind, layer_ahead, layer_behind, state, side_state = call(
        smooth_kernel, SMOOTH_OUTS, SMOOTH_SCRATCH
    )(main, after, before)
    left, right = neighbours(ahead, behind, "gx")
    ahead, behind = call(pack_coarse, [(COARSE_ROWS_Y, 128)] * 2)(own, right, left, layer_ahead, layer_behind)
    down, up = neighbours(ahead, behind, "gy")
    correction, coarse = call(post_kernel, POST_OUTS, POST_SCRATCH)(own, right, left, up, down, state, side_state, smooth)
    return correction, coarse


def solution(mesh):
    return jax.shard_map(
        on_device,
        mesh=mesh,
        in_specs=(P("gx", "gy", "gz"), P(None, "gx", "gy", "gz")),
        out_specs=(P(None, "gx", "gy", "gz"), P(None, "gx", "gy", "gz")),
        check_vma=False,
    )
```

```python
import jax
import jax.numpy as jnp
from jax import lax
from jax.experimental import pallas as pl
from jax.experimental.pallas import tpu as pltpu
from jax.sharding import PartitionSpec as P

SWEEPS = 4
THETA = 1.15
DELTA = 0.85

FACE, SIDE, EDGE, FLAT, TURN, TWIST = 9.6, 6.0, 2.7, 1.8, 0.9, 0.4
UNIT = 120.0
WHOLE = 1.92
HALO = 16
SMOOTH_CHUNKS = (4, 3, 2, 1)
POST_CHUNKS = (4, 3, 5, 7, 2, 1)


def sweep_scales():
    sigma = THETA / DELTA
    rho = 1.0 / sigma
    scales = []
    for _ in range(SWEEPS - 1):
        rho_next = 1.0 / (2.0 * sigma - rho)
        scales.append((rho_next * rho, 2.0 * rho_next / DELTA))
        rho = rho_next
    return scales


def lane_index():
    return lax.broadcasted_iota(jnp.int32, (8, 128), 1)


def by_group(values):
    group = lane_index() // 32
    out = jnp.full((8, 128), values[-1], jnp.float32)
    for g in range(len(values) - 1):
        out = jnp.where(group == g, values[g], out)
    return out


def neighbourhood(load, count):
    mid, summed, spread = [], [], []
    for p in range(-1, count + 1):
        u, yp, ym = load(p, 0), load(p, 1), load(p, -1)
        mid.append(u)
        summed.append(yp + ym)
        spread.append(yp - ym)
    return mid, summed, spread


def stencil(field, plane, count, row):
    def loader(c):
        return lambda p, dy: field[c, plane + p, pl.ds(row + dy, 8), :]

    flat, even, odd = ([[None] * 3 for _ in range(count)] for _ in range(3))
    cross, along, across = [None] * count, [None] * count, [None] * count
    mid, summed, spread = neighbourhood(loader(0), count)
    for p in range(count):
        u, sy = mid[p + 1], summed[p + 1]
        sx, sxy = mid[p + 2] + mid[p], summed[p + 2] + summed[p]
        flat[p][0] = FACE * sx + SIDE * sy + EDGE * sxy
        even[p][0] = SIDE * u + EDGE * sx + FLAT * sy + sxy
        cross[p] = spread[p + 2] - spread[p]
        along[p], across[p] = mid[p + 2] - mid[p], summed[p + 2] - summed[p]
    mid, summed, spread = neighbourhood(loader(1), count)
    for p in range(count):
        u, sy = mid[p + 1], summed[p + 1]
        sx, sxy = mid[p + 2] + mid[p], summed[p + 2] + summed[p]
        flat[p][1] = FACE * sy + SIDE * sx + EDGE * sxy + TURN * cross[p]
        even[p][1] = SIDE * u + EDGE * sy + FLAT * sx + sxy + TWIST * cross[p]
        back = spread[p + 2] - spread[p]
        flat[p][0] = flat[p][0] + TURN * back
        even[p][0] = even[p][0] + TWIST * back
        odd[p][2] = TURN * (along[p] + spread[p + 1]) + TWIST * (across[p] + (spread[p + 2] + spread[p]))
    mid, summed, spread = neighbourhood(loader(2), count)
    for p in range(count):
        both, sxy = mid[p + 2] + mid[p] + summed[p + 1], summed[p + 2] + summed[p]
        flat[p][2] = SIDE * both + FLAT * sxy
        even[p][2] = FACE * mid[p + 1] + EDGE * both + sxy
        odd[p][0] = TURN * (mid[p + 2] - mid[p]) + TWIST * (summed[p + 2] - summed[p])
        odd[p][1] = TURN * spread[p + 1] + TWIST * (spread[p + 2] + spread[p])
    return [[(flat[p][c], even[p][c] + odd[p][c], even[p][c] - odd[p][c]) for c in range(3)] for p in range(count)]


def side_stencil(field, plane, count, row):
    mid, summed, spread = neighbourhood(lambda p, dy: field[plane + p, pl.ds(row + dy, 8), :], count)
    group = lane_index() // 32
    flat_x, flat_y = by_group((FACE, SIDE, SIDE)), by_group((SIDE, FACE, SIDE))
    flat_xy, even_u = by_group((EDGE, EDGE, FLAT)), by_group((SIDE, SIDE, FACE))
    even_x, even_y = by_group((EDGE, FLAT, EDGE)), by_group((FLAT, EDGE, EDGE))
    found = []
    for p in range(count):
        u, sy, dy = mid[p + 1], summed[p + 1], spread[p + 1]
        sx, dx = mid[p + 2] + mid[p], mid[p + 2] - mid[p]
        sxy, dx_sy = summed[p + 2] + summed[p], summed[p + 2] - summed[p]
        dy_sx, dxy = spread[p + 2] + spread[p], spread[p + 2] - spread[p]
        along_x, along_y = TURN * dx + TWIST * dx_sy, TURN * dy + TWIST * dy_sx
        down = pltpu.roll(jnp.where(group == 1, dxy, along_y), 96, 1)
        up = pltpu.roll(jnp.where(group == 0, dxy, along_y), 32, 1)
        far = pltpu.roll(along_x, 64, 1)
        cross = jnp.where(group == 0, down, jnp.where(group == 1, up, 0.0))
        flat = flat_x * sx + flat_y * sy + flat_xy * sxy + TURN * cross
        even = even_u * u + even_x * sx + even_y * sy + sxy + TWIST * cross
        odd = jnp.where(group == 0, far, jnp.where(group == 1, down, far + up))
        found.append((flat, even + odd, even - odd))
    return found


def join_ring(part):
    centre, above, below = part
    return centre + (pltpu.roll(above, 127, 1) + pltpu.roll(below, 1, 1))


def side_lanes():
    lane = lane_index()
    return lane, lane % 32 == HALO


def join_sides(parts, side):
    lane, begins = side_lanes()
    ends = jnp.where(begins, side[1], side[2])
    side_above, side_below = side[1], side[2]
    joined = []
    for c, (centre, above, below) in enumerate(parts):
        inward = pltpu.roll(ends, 112 - 32 * c, 1)
        outward = pltpu.roll(jnp.where(lane == 0, above, below), 32 * c + HALO, 1)
        up = pltpu.roll(jnp.where(lane == 0, inward, above), 127, 1)
        down = pltpu.roll(jnp.where(lane == 127, inward, below), 1, 1)
        joined.append(centre + (up + down))
        side_above = jnp.where(lane == 32 * c + HALO, outward, side_above)
        side_below = jnp.where(lane == 32 * c + HALO - 1, outward, side_below)
    return joined, side[0] + (pltpu.roll(side_above, 127, 1) + pltpu.roll(side_below, 1, 1))


def shifted(main, side):
    lane, begins = side_lanes()
    inward = pltpu.roll(side, 112, 1)
    side_below, side_above = side, side
    for g in range(3):
        outward = pltpu.roll(main, 32 * g + HALO, 1)
        side_above = jnp.where(lane == 32 * g + HALO, outward, side_above)
        side_below = jnp.where(lane == 32 * g + HALO - 1, outward, side_below)
    return (
        (pltpu.roll(jnp.where(lane == 127, inward, main), 1, 1), pltpu.roll(jnp.where(lane == 0, inward, main), 127, 1)),
        (pltpu.roll(side_below, 1, 1), pltpu.roll(side_above, 127, 1)),
    )


def weighted(modulus, plain, heavy):
    here, before, after = modulus
    return (here * plain[0] + heavy[0], before * plain[1] + heavy[1], after * plain[2] + heavy[2])


def coupling(now, modulus, plane, count, row):
    plain, heavy = (stencil(now[k], plane, count, row) for k in range(2))
    parts = [[weighted(modulus[p][0], *both) for both in zip(plain[p], heavy[p])] for p in range(count)]
    if len(now) == 2:
        return [([join_ring(part) for part in parts[p]], None) for p in range(count)]
    plain, heavy = (side_stencil(now[2 + k], plane, count, row) for k in range(2))
    return [join_sides(parts[p], weighted(modulus[p][1], plain[p], heavy[p])) for p in range(count)]


def sweep(chunks, planes, rows, now, later, rest, modulus, diag, inverse, scale, emit=None):
    lo, hi = planes
    chunk = next(n for n in chunks if (hi - lo) % n == 0)
    sides = len(rest) if not emit else 1

    def body(i, carry):
        first = lo + i * chunk
        for row in rows:
            mods = [[[read(first + j, row) for read in reads] for reads in modulus] for j in range(chunk)]
            out = coupling(now, mods, first, chunk, 8 + row)
            for j in range(chunk):
                plane = first + j
                for t in range(sides):
                    d = diag[t](plane, row)
                    if scale:
                        inv = inverse[t](plane, row) * scale[1]
                    for c in range(1 if t else 3):
                        at = (plane,) if t else (c, plane)
                        here, margin = (*at, pl.ds(row, 8), slice(None)), (*at, pl.ds(8 + row, 8), slice(None))
                        old = now[2 * t][margin]
                        r = rest[t][here] - d * old + (out[j][1] if t else out[j][0][c])
                        if not emit:
                            rest[t][here] = r
                        if scale:
                            step = inv * r
                            if scale[0]:
                                step = scale[0] * old + step
                            if emit:
                                emit(c, plane, step)
                            else:
                                later[2 * t][margin] = step
                                later[2 * t + 1][margin] = mods[j][t][0] * step
        return carry

    lax.fori_loop(0, (hi - lo) // chunk, body, 0)


def diagonal_parts(modulus, plane, row):
    def at(dx, dy):
        return modulus[plane + dx, pl.ds(row + dy, 8), :]

    u = at(0, 0)
    cross = (at(1, 0) + at(-1, 0)) + (at(0, 1) + at(0, -1))
    corner = (at(1, 1) + at(-1, -1)) + (at(1, -1) + at(-1, 1))
    even = 0.16 * u + 0.06 * cross + 0.03 * corner
    return u, (WHOLE * u + 0.16 * cross + 0.06 * corner, even, even)


def finish_diagonal(mid, total):
    diag = (1.05 * 0.5 * UNIT) * total
    inside = mid > 0.0
    return mid, diag, jnp.where(inside, 1.0 / jnp.where(inside, diag, 1.0), 0.0)


def ring_diagonal(modulus, plane, row):
    mid, part = diagonal_parts(modulus, plane, row)
    return finish_diagonal(mid, join_ring(part))


def side_diagonal(modulus, side_modulus, plane, row):
    mid, (centre, even, _) = diagonal_parts(modulus, plane, row)
    side_mid, (side_centre, side_even, _) = diagonal_parts(side_modulus, plane, row)
    (below, above), (side_below, side_above) = shifted(even, side_even)
    main = finish_diagonal(mid, centre + (below + above))
    side_mid, side_diag, side_inverse = finish_diagonal(side_mid, side_centre + (side_below + side_above))
    side_inverse = jnp.where(lane_index() < 96, side_inverse, 0.0)
    return main, (side_mid, side_diag, side_inverse), shifted(mid, side_mid)


def pair_matrix(group, fine_axis):
    fine = lax.broadcasted_iota(jnp.int32, (128, 128), fine_axis)
    coarse = lax.broadcasted_iota(jnp.int32, (128, 128), 1 - fine_axis)
    if group is None:
        return (lax.shift_right_logical(fine, 1) == coarse).astype(jnp.float32)
    inner = fine - 32 * group
    target = lax.shift_right_logical(fine, 1) - 16 * group + jnp.where(inner < HALO, 120, 56)
    return ((target == coarse) & (inner >= 0) & (inner < 32)).astype(jnp.float32)


def exact_dot(a, b):
    return jnp.dot(a, b, precision=lax.Precision.HIGHEST, preferred_element_type=jnp.float32)


def pack_planes(own, ahead, behind):
    for p in range(8):
        if p > 0:
            ahead[p - 1] = own[3, p]
        if p < 7:
            behind[p] = own[3, p]
        for c in range(3):
            if p > 1:
                ahead[7 + 6 * c + p - 2] = own[c, p]
            if p < 6:
                behind[7 + 6 * c + p] = own[c, p]


def fine_planes(own, left, right):
    found = []
    for plane in range(1, 23):
        if plane < 8:
            found.append((3, plane, left, (plane - 1,)))
        elif plane < 16:
            found.append((3, plane, own, (3, plane - 8)))
        else:
            found.append((3, plane, right, (plane - 16,)))
    for c in range(3):
        for plane in range(2, 22):
            if plane < 8:
                found.append((c, plane, left, (7 + 6 * c + plane - 2,)))
            elif plane < 16:
                found.append((c, plane, own, (c, plane - 8)))
            else:
                found.append((c, plane, right, (7 + 6 * c + plane - 16,)))
    return found


FINE_ROWS = 520


def fine_rows(c, plane):
    return (7 * (plane - 1), 7) if c == 3 else (154 + 6 * (20 * c + plane - 2), 6)


def pack_rows(own, right, left, ahead, behind):
    empty = jnp.zeros((8, 128), jnp.float32)
    ahead[pl.ds(FINE_ROWS - 8, 8), :] = empty
    behind[pl.ds(FINE_ROWS - 8, 8), :] = empty
    for c, plane, source, index in fine_planes(own, left, right):
        base, count = fine_rows(c, plane)
        ahead[pl.ds(base, count), :] = source[(*index, pl.ds(8 - count, count), slice(None))]
        behind[pl.ds(base, count), :] = source[(*index, pl.ds(0, count), slice(None))]


def pack_lanes(own, right, left, up, down, main, first, last):
    empty = jnp.zeros((24, 128), jnp.float32)
    for plane in (0, 1, 22, 23):
        for c in range(3):
            main[c, plane] = empty
    main[3, 0] = empty
    main[3, 23] = empty
    gap = jnp.zeros((2, 128), jnp.float32)
    for c, plane, source, index in fine_planes(own, left, right):
        base, count = fine_rows(c, plane)
        main[c, plane, pl.ds(0, 2), :] = gap
        main[c, plane, pl.ds(22, 2), :] = gap
        main[c, plane, pl.ds(8, 8), :] = source[index]
        main[c, plane, pl.ds(8 - count, count), :] = down[pl.ds(base, count), :]
        main[c, plane, pl.ds(16, count), :] = up[pl.ds(base, count), :]
    lane = lane_index()

    def pack(pair, carry):
        for t in range(3):
            head = jnp.zeros((8, 128), jnp.float32)
            tail = head
            for s in range(2):
                for c in range(4):
                    value, place = main[c, 2 * pair + s, pl.ds(8 * t, 8), :], 32 * c + HALO * s
                    mine = (lane >= place) & (lane < place + HALO)
                    head = jnp.where(mine, pltpu.roll(value, place, 1) if place else value, head)
                    turn = (place + HALO) % 128
                    tail = jnp.where(mine, pltpu.roll(value, turn, 1) if turn else value, tail)
            first[pair, pl.ds(8 * t, 8), :] = head
            last[pair, pl.ds(8 * t, 8), :] = tail
        return carry

    lax.fori_loop(0, 12, pack, 0, unroll=6)


LAYER_X = 6 * 8 + 3 * 5 * 6
LAYER_Y = 16 * 6 + 3 * 14 * 5
COARSE_ROWS_X = 192
COARSE_ROWS_Y = 368


def coarse_planes(own, left, right):
    found = []
    for i in range(16):
        if i < 6:
            found.append((3, i, left, (), 8 * i))
        elif i < 10:
            found.append((3, i, own, (3, i - 4), 0))
        else:
            found.append((3, i, right, (), 8 * (i - 10)))
    for c in range(3):
        for i in range(14):
            if i < 5:
                found.append((c, i + 1, left, (), 48 + 6 * (5 * c + i)))
            elif i < 9:
                found.append((c, i + 1, own, (c, i - 3), 1))
            else:
                found.append((c, i + 1, right, (), 48 + 6 * (5 * c + i - 9)))
    return found


def coarse_rows(c, plane):
    return (6 * plane, 6, 2) if c == 3 else (96 + 5 * (14 * c + plane - 1), 5, 1)


def pack_coarse(own, right, left, layer_ahead, layer_behind, ahead, behind):
    empty = jnp.zeros((8, 128), jnp.float32)
    for message, layer, offset in ((ahead, layer_ahead, 7), (behind, layer_behind, 4)):
        message[pl.ds(COARSE_ROWS_Y - 8, 8), :] = empty
        for f in range(4):
            base = LAYER_Y + 14 * f
            message[pl.ds(base, 1), :] = left[pl.ds(LAYER_X + 12 * f + offset, 1), :]
            message[pl.ds(base + 1, 12), :] = layer[f]
            message[pl.ds(base + 13, 1), :] = right[pl.ds(LAYER_X + 12 * f + offset, 1), :]
    for c, plane, source, index, row in coarse_planes(own, left, right):
        base, count, margin = coarse_rows(c, plane)
        ahead[pl.ds(base, count), :] = source[(*index, pl.ds(row, count), slice(None))]
        behind[pl.ds(base, count), :] = source[(*index, pl.ds(row + margin, count), slice(None))]


def smooth_kernel(
    main, after, before, smooth, message, ahead, behind, layer_ahead, layer_behind, state, side_state,
    ua, ub, va, vb, usa, usb, vsa, vsb, rest, modulus, diag, inverse, prev, next, rest_s, modulus_s, diag_s, inverse_s, prev_s, next_s, pairs, pairs_s,
):
    group = lane_index() // 32

    low = lane_index() % 32 < HALO

    def place(pair, carry):
        for s in range(2):
            plane = 2 * pair + s
            for t in range(3):
                here = pl.ds(8 * t, 8)
                for c in range(3):
                    rest[c, plane, here, :] = main[c, plane, here, :]
                modulus[plane, pl.ds(8 + 8 * t, 8), :] = main[3, plane, here, :]
                lower, upper = before[pair, here, :], after[pair, here, :]
                if s:
                    lower = pltpu.roll(lower, 128 - HALO, 1)
                else:
                    upper = pltpu.roll(upper, HALO, 1)
                value = jnp.where(low, lower, upper)
                rest_s[plane, here, :] = value
                spread = jnp.where(group == 1, pltpu.roll(value, 64, 1), pltpu.roll(value, 96, 1))
                spread = jnp.where(group == 0, pltpu.roll(value, 32, 1), spread)
                modulus_s[plane, pl.ds(8 + 8 * t, 8), :] = jnp.where(group == 3, value, spread)
        return carry

    lax.fori_loop(0, 12, place, 0, unroll=4)

    def begin(i, carry):
        for plane in (2 + 2 * i, 3 + 2 * i):
            for t in range(3):
                here, margin = pl.ds(8 * t, 8), pl.ds(8 + 8 * t, 8)
                (mid, d, inv), (mid_s, d_s, inv_s), beside = side_diagonal(modulus, modulus_s, plane, 8 + 8 * t)
                for refs, values in zip(((prev, next), (prev_s, next_s)), beside):
                    for ref, value in zip(refs, values):
                        ref[plane, here, :] = value
                diag[plane, here, :] = d
                inverse[plane, here, :] = inv
                diag_s[plane, here, :] = d_s
                inverse_s[plane, here, :] = inv_s
                inv = inv * (1.0 / THETA)
                for c in range(3):
                    step = rest[c, plane, here, :] * inv
                    ua[c, plane, margin, :] = step
                    va[c, plane, margin, :] = mid * step
                step = rest_s[plane, here, :] * (inv_s * (1.0 / THETA))
                usa[plane, margin, :] = step
                vsa[plane, margin, :] = mid_s * step
        return carry

    lax.fori_loop(0, 10, begin, 0)

    def gather(steps, start):
        def body(p, carry):
            for c in range(3):
                step = steps[c, 8 + p, pl.ds(16, 8), :]
                smooth[c, p] = step if start else smooth[c, p] + step
            return carry

        lax.fori_loop(0, 8, body, 0, unroll=4)

    gather(ua, True)
    scales = sweep_scales()

    def reader(ref, margin):
        return lambda plane, row: ref[plane, pl.ds(margin + row, 8), :]

    moduli = [
        [reader(modulus, 8), reader(prev, 0), reader(next, 0)],
        [reader(modulus_s, 8), reader(prev_s, 0), reader(next_s, 0)],
    ]
    readers = [moduli] + [[reader(ref, 0) for ref in refs] for refs in ((diag, diag_s), (inverse, inverse_s))]
    for k in range(1, SWEEPS + 1):
        now, later = (ua, va, usa, vsa), (ub, vb, usb, vsb)
        if k % 2 == 0:
            now, later = later, now
        rows = (0, 8, 16) if k == 1 else (4, 12)
        sweep(SMOOTH_CHUNKS, (2 + k, 22 - k), rows, now, later, (rest, rest_s), *readers, scales[k - 1] if k < SWEEPS else None)
        if k < SWEEPS:
            gather(later[0], False)

    def restrict(p, carry):
        def four(ref, at, margin):
            a, b = (ref[(*at, 4 + 2 * p + dx, pl.ds(margin + 4, 8, stride=2), slice(None))] for dx in range(2))
            c, d = (ref[(*at, 4 + 2 * p + dx, pl.ds(margin + 5, 8, stride=2), slice(None))] for dx in range(2))
            return (a + b) + (c + d)

        for c in range(3):
            pairs[c, p] = four(rest, (c,), 0)
        pairs[3, p] = 0.25 * four(modulus, (), 8)
        pairs_s[0, p] = four(rest_s, (), 0)
        pairs_s[1, p] = 0.25 * four(modulus_s, (), 8)
        return carry

    lax.fori_loop(0, 8, restrict, 0, unroll=8)
    coarse = exact_dot(pairs[...].reshape(256, 128), pair_matrix(None, 0)).reshape(4, 8, 8, 128)
    for c in range(4):
        source = pairs_s[1 if c == 3 else 0].reshape(64, 128)
        message[c] = coarse[c] + exact_dot(source, pair_matrix(c % 3, 0)).reshape(8, 8, 128)
    for i in range(6):
        ahead[pl.ds(8 * i, 8), :] = message[3, i]
        behind[pl.ds(8 * i, 8), :] = message[3, 2 + i]
    for f, source in enumerate([rest.at[c] for c in range(3)] + [rest_s]):
        ahead[pl.ds(LAYER_X + 12 * f, 12), :] = source[13, pl.ds(6, 12), :]
        behind[pl.ds(LAYER_X + 12 * f, 12), :] = source[10, pl.ds(6, 12), :]
        for p in range(12):
            layer_ahead[f, pl.ds(p, 1), :] = source[6 + p, pl.ds(13, 1), :]
            layer_behind[f, pl.ds(p, 1), :] = source[6 + p, pl.ds(10, 1), :]
    empty = jnp.zeros((6, 128), jnp.float32)
    ahead[pl.ds(LAYER_X + 48, 6), :] = empty
    behind[pl.ds(LAYER_X + 48, 6), :] = empty
    for c in range(3):
        for i in range(5):
            ahead[pl.ds(48 + 6 * (5 * c + i), 6), :] = message[c, 1 + i, pl.ds(1, 6), :]
            behind[pl.ds(48 + 6 * (5 * c + i), 6), :] = message[c, 2 + i, pl.ds(1, 6), :]

    kept = (
        (modulus, modulus_s, 12), (diag, diag_s, 4), (inverse, inverse_s, 4), (prev, prev_s, 4), (next, next_s, 4)
    )

    def keep_state(p, carry):
        for c in range(3):
            state[c, p] = rest[c, 4 + p, pl.ds(4, 16), :]
        side_state[0, p] = rest_s[4 + p, pl.ds(4, 16), :]
        for f, (ref, ref_s, row) in enumerate(kept):
            state[3 + f, p] = ref[4 + p, pl.ds(row, 16), :]
            side_state[1 + f, p] = ref_s[4 + p, pl.ds(row, 16), :]
        return carry

    lax.fori_loop(0, 16, keep_state, 0, unroll=8)


def post_kernel(
    own, right, left, up, down, state_in, side_in, smooth, correction, coarse,
    ca, cb, cva, cvb, crest, cmod, cinv, cdiag, cprev, cnext, total, ua, ub, va, vb, usa, usb, vsa, vsb, wide, wide_s, rest, rest_s,
):
    scales = sweep_scales()

    empty = jnp.zeros((16, 128), jnp.float32)
    for c in range(3):
        crest[c, 0] = empty
        crest[c, 15] = empty
    edge = jnp.zeros((1, 128), jnp.float32)
    for c, plane, source, index, row in coarse_planes(own, left, right):
        base, count, margin = coarse_rows(c, plane)
        mid = source[(*index, pl.ds(row + margin, 4), slice(None))]
        below, above = down[pl.ds(base, count), :], up[pl.ds(base, count), :]
        if c < 3:
            crest[c, plane, pl.ds(0, 1), :] = edge
            crest[c, plane, pl.ds(1, 5), :] = below
            crest[c, plane, pl.ds(6, 4), :] = mid
            crest[c, plane, pl.ds(10, 5), :] = above
            crest[c, plane, pl.ds(15, 1), :] = edge
        else:
            cmod[plane, pl.ds(8, 6), :] = below
            cmod[plane, pl.ds(14, 4), :] = mid
            cmod[plane, pl.ds(18, 6), :] = above

    def begin(i, carry):
        for plane in [1 + 7 * i + j for j in range(7)]:
            for t in range(2):
                here, margin = pl.ds(8 * t, 8), pl.ds(8 + 8 * t, 8)
                mid, d, inv = ring_diagonal(cmod, plane, 8 + 8 * t)
                cdiag[plane, here, :] = d
                cprev[plane, here, :] = pltpu.roll(mid, 1, 1)
                cnext[plane, here, :] = pltpu.roll(mid, 127, 1)
                cinv[plane, here, :] = inv
                inv = inv * (1.0 / THETA)
                for c in range(3):
                    step = crest[c, plane, here, :] * inv
                    ca[c, plane, margin, :] = step
                    cva[c, plane, margin, :] = mid * step
        return carry

    lax.fori_loop(0, 2, begin, 0)

    def gather(steps, start):
        def body(p, carry):
            for c in range(3):
                step = steps[c, 4 + p, pl.ds(12, 8), :]
                total[c, p] = step if start else total[c, p] + step
            return carry

        lax.fori_loop(0, 8, body, 0, unroll=4)

    gather(ca, True)

    def reader(ref, margin):
        return lambda plane, row: ref[plane, pl.ds(margin + row, 8), :]

    coarse_moduli = [[reader(cmod, 8), reader(cprev, 0), reader(cnext, 0)]]
    for k in range(1, SWEEPS):
        now, later = ((ca, cva), (cb, cvb)) if k % 2 else ((cb, cvb), (ca, cva))
        sweep(POST_CHUNKS, (1 + k, 15 - k), (0, 8) if k < 3 else (4,), now, later, (crest,), coarse_moduli, [reader(cdiag, 0)], [reader(cinv, 0)], scales[k - 1])
        gather(later[0], False)

    for c in range(3):
        for p in range(4):
            coarse[c, p] = total[c, 2 + p, pl.ds(2, 4), pl.ds(0, 64)]

    wide[...] = exact_dot(total[...].reshape(192, 128), pair_matrix(None, 1)).reshape(3, 8, 8, 128)
    spread = None
    for c in range(3):
        part = exact_dot(total[c].reshape(64, 128), pair_matrix(c, 1))
        spread = part if spread is None else spread + part
    wide_s[...] = spread.reshape(8, 8, 128)

    def lift(p, carry):
        for dx in range(2):
            for dy in range(2):
                for c in range(3):
                    ua[c, 2 * p + dx, pl.ds(8 + dy, 8, stride=2), :] = wide[c, p]
                usa[2 * p + dx, pl.ds(8 + dy, 8, stride=2), :] = wide_s[p]
        return carry

    lax.fori_loop(0, 8, lift, 0, unroll=2)

    def weigh(p, carry):
        for c in range(3):
            va[c, p, pl.ds(8, 16), :] = state_in[3, p] * ua[c, p, pl.ds(8, 16), :]
            rest[c, p] = state_in[c, p]
        vsa[p, pl.ds(8, 16), :] = side_in[1, p] * usa[p, pl.ds(8, 16), :]
        rest_s[p] = side_in[0, p]
        return carry

    lax.fori_loop(0, 16, weigh, 0, unroll=2)
    for f, target in enumerate([rest.at[c] for c in range(3)] + [rest_s]):
        target[1, pl.ds(2, 12), :] = left[pl.ds(LAYER_X + 12 * f, 12), :]
        target[14, pl.ds(2, 12), :] = right[pl.ds(LAYER_X + 12 * f, 12), :]
        for p in range(14):
            target[1 + p, pl.ds(1, 1), :] = down[pl.ds(LAYER_Y + 14 * f + p, 1), :]
            target[1 + p, pl.ds(14, 1), :] = up[pl.ds(LAYER_Y + 14 * f + p, 1), :]

    def add_own(steps, start):
        def body(p, carry):
            for c in range(3):
                step = steps[c, 4 + p, pl.ds(12, 8), :]
                correction[c, p] = (smooth[c, p] if start else correction[c, p]) + step
            return carry

        lax.fori_loop(0, 8, body, 0, unroll=4)

    add_own(ua, True)

    def held(f):
        return [
            lambda plane, row: state_in[3 + f, plane, pl.ds(row, 8), :],
            lambda plane, row: side_in[1 + f, plane, pl.ds(row, 8), :],
        ]

    moduli = list(zip(held(0), held(3), held(4)))

    def emit(c, plane, step):
        correction[c, plane - 4] = correction[c, plane - 4] + step

    for k in range(SWEEPS):
        now, later = (ua, va, usa, vsa), (ub, vb, usb, vsb)
        if k % 2:
            now, later = later, now
        scale = scales[k - 1] if k else (None, 1.0 / THETA)
        last = k == SWEEPS - 1
        sweep(
            POST_CHUNKS, (1 + k, 15 - k), (4,) if last else (0, 8), now, later, (rest, rest_s), moduli, held(1), held(2), scale,
            emit if last else None,
        )
        if not last:
            add_own(later[0], False)


def call(kernel, outs, scratch=()):
    return pl.pallas_call(
        kernel,
        out_shape=[jax.ShapeDtypeStruct(s, jnp.float32) for s in outs],
        scratch_shapes=[pltpu.VMEM(s, jnp.float32) for s in scratch],
        compiler_params=pltpu.CompilerParams(vmem_limit_bytes=48 * 1024 * 1024),
    )


def neighbours(to_next, to_previous, axis):
    count = lax.axis_size(axis)
    after = lax.ppermute(to_previous, axis, [(i + 1, i) for i in range(count - 1)])
    before = lax.ppermute(to_next, axis, [(i, i + 1) for i in range(count - 1)])
    return before, after


SMOOTH_OUTS = [
    (3, 8, 8, 128),
    (4, 8, 8, 128),
    (COARSE_ROWS_X, 128),
    (COARSE_ROWS_X, 128),
    (4, 12, 128),
    (4, 12, 128),
    (8, 16, 16, 128),
    (6, 16, 16, 128),
]
SMOOTH_SCRATCH = [
    *[(3, 24, 40, 128)] * 4,
    *[(24, 40, 128)] * 4,
    (3, 24, 24, 128),
    (24, 40, 128),
    *[(24, 24, 128)] * 5,
    (24, 40, 128),
    *[(24, 24, 128)] * 4,
    (4, 8, 8, 128),
    (2, 8, 8, 128),
]
POST_OUTS = [(3, 8, 8, 128), (3, 4, 4, 64)]
POST_SCRATCH = [
    *[(3, 16, 32, 128)] * 4,
    (3, 16, 16, 128),
    (16, 32, 128),
    *[(16, 16, 128)] * 4,
    (3, 8, 8, 128),
    *[(3, 16, 32, 128)] * 4,
    *[(16, 32, 128)] * 4,
    (3, 8, 8, 128),
    (8, 8, 128),
    (3, 16, 16, 128),
    (16, 16, 128),
]


def on_device(levels, residual):
    ratio = levels.astype(jnp.float32) / 255.0
    modulus = (0.05 + 0.95 * ratio * ratio * ratio) / UNIT
    own = jnp.concatenate([residual, modulus[None]])
    ahead, behind = call(pack_planes, [(25, 8, 128), (25, 8, 128)])(own)
    left, right = neighbours(ahead, behind, "gx")
    ahead, behind = call(pack_rows, [(FINE_ROWS, 128)] * 2)(own, right, left)
    down, up = neighbours(ahead, behind, "gy")
    main, first, last = call(pack_lanes, [(4, 24, 24, 128), (12, 24, 128), (12, 24, 128)])(own, right, left, up, down)
    before, after = neighbours(last, first, "gz")
    smooth, own, ahead, behind, layer_ahead, layer_behind, state, side_state = call(
        smooth_kernel, SMOOTH_OUTS, SMOOTH_SCRATCH
    )(main, after, before)
    left, right = neighbours(ahead, behind, "gx")
    ahead, behind = call(pack_coarse, [(COARSE_ROWS_Y, 128)] * 2)(own, right, left, layer_ahead, layer_behind)
    down, up = neighbours(ahead, behind, "gy")
    correction, coarse = call(post_kernel, POST_OUTS, POST_SCRATCH)(own, right, left, up, down, state, side_state, smooth)
    return correction, coarse


def solution(mesh):
    return jax.shard_map(
        on_device,
        mesh=mesh,
        in_specs=(P("gx", "gy", "gz"), P(None, "gx", "gy", "gz")),
        out_specs=(P(None, "gx", "gy", "gz"), P(None, "gx", "gy", "gz")),
        check_vma=False,
    )
```
